128 devices in a mesh: chain: 16 (over z, x), tp: 8 (over y, core).
Axes of the slice: x: 4, y: 4, z: 4, core: 2. Of those that a mesh axis runs over, the one named last changes fastest.
Arguments:
- tokens: bfloat16 [4096, 7168], P('chain', 'tp'), may hold values from -6 to 6
- w_down_q: bfloat16 [7168, 1536], P('tp'), may hold values from -0.0625 to 0.0625
- w_down_kv: bfloat16 [7168, 576], P('tp'), may hold values from -0.0625 to 0.0625
- q_gain: float32 [1536], replicated, may hold values from 0.1 to 1.9
- kv_gain: float32 [512], replicated, may hold values from 0.1 to 1.9
- w_up_q: bfloat16 [1536, 12288], P(None, 'tp'), may hold values from -0.15625 to 0.15625
- w_absorb: bfloat16 [64, 128, 512], P('tp')
- w_value: bfloat16 [64, 512, 128], P('tp'), may hold values from -0.25 to 0.25
- slot_block: int32 [32], P('chain'), may hold values from 0 to 31, each once
Outputs:
- attended: bfloat16 [4096, 8192], P('chain', 'tp')
- latent_cache: bfloat16 [32, 128, 576], P('chain', 'tp')
The draws below stay inside these ranges and needn't reach their ends.
Inputs may be any that keep to these rules, and one draw needn't show every extreme that they name: `slot_block`: every prompt block is named by exactly one slot.
All inputs are finite; a program needn't handle non-finite values.
Results may differ from the reference program's by a relative error of at most 0.04.
Values may be sent and summed in bfloat16 or wider, within the bound.
A program may use at most 128 MiB of HBM per device.

```python
import jax
import jax.numpy as jnp
from jax import lax

D = 7168
H = 64
QL = 1536
KVL = 512
ROPE = 64
NOPE = 128
VH = 128
TOK_DEV = 256
BLOCK = 128
TOKENS = 4096
CACHE_SLOTS = 32
N_CHAIN = 16


def draw_w_absorb(key, part):
    key = jax.random.fold_in(key, 11)
    entry_key, order_key = jax.random.split(key)
    ranking = jax.random.permutation(order_key, H)
    strong_count = max(3, H // 8)
    entries = jax.random.normal(entry_key, (H, NOPE, KVL), jnp.float32)
    levels = jnp.array([12.0, 24.0, 48.0], jnp.float32)
    picked = jnp.sum(jnp.where((ranking % 3)[:, None] == jnp.arange(3, dtype=jnp.int32)[None, :], levels[None, :], 0.0), 1)
    head_scale = jnp.where(ranking < strong_count, picked, 1.0)
    return (entries * head_scale[:, None, None] * NOPE ** (-0.5)).astype(jnp.bfloat16)


def shard_levels(key, dims, pieces, low, largest):
    def one(axis_at, shards_of):
        steps = jax.random.uniform(jax.random.fold_in(jax.random.fold_in(key, 6), axis_at), (shards_of,), jnp.float32, low / len(pieces), largest / len(pieces))
        return jnp.repeat(jnp.exp(steps), dims[axis_at] // shards_of).reshape((-1,) + (1,) * (len(dims) - axis_at - 1))

    loudness = one(*pieces[0])
    for cut in pieces[1:]:
        loudness = loudness * one(*cut)
    return loudness


def normal_values(stream_key, dims, width, bound, cuts=(), held_as=jnp.bfloat16):
    values = jax.random.normal(stream_key, dims, jnp.float32) * width
    if len(cuts) > 0:
        values = shard_levels(stream_key, dims, cuts, -0.22, 0.18) * values
    return jnp.clip(values, min=-bound, max=bound).astype(held_as)


def setup_inputs(seed: int = 0) -> dict:
    key_list = jax.random.split(jax.random.key(seed), 10)
    tokens = normal_values(key_list[0], (TOKENS, D), 1.0, 6.0, ((0, 16), (1, 8)))
    w_down_q = normal_values(key_list[1], (D, QL), D ** -0.5, 0.0625, ((0, 8),))
    w_down_kv = normal_values(key_list[2], (D, KVL + ROPE), D ** -0.5, 0.0625, ((0, 8),))
    q_gain = jnp.clip(1.0 + 0.18 * jax.random.normal(key_list[3], (QL,), jnp.float32), 0.1, 1.9)
    kv_gain = jnp.clip(1.0 + 0.18 * jax.random.normal(key_list[4], (KVL,), jnp.float32), 0.1, 1.9)
    w_up_q = normal_values(key_list[5], (QL, H * (NOPE + ROPE)), QL ** -0.5, 0.15625, ((1, 8),))
    w_absorb = draw_w_absorb(jax.random.fold_in(key_list[9], 71), 0)
    w_value = normal_values(key_list[7], (H, KVL, VH), KVL ** -0.5, 0.25, ((0, 8),))
    slot_block = jax.random.permutation(key_list[8], CACHE_SLOTS).astype(jnp.int32)
    return {"tokens": tokens, "w_down_q": w_down_q, "w_down_kv": w_down_kv, "q_gain": q_gain, "kv_gain": kv_gain, "w_up_q": w_up_q, "w_absorb": w_absorb, "w_value": w_value, "slot_block": slot_block}


ROPE_BASE = 50000.0

def rotate_pairs(values, positions):
    half = values.shape[-1] // 2
    inverse = ROPE_BASE ** (-2.0 * jnp.arange(half, dtype=jnp.float32) / values.shape[-1])
    angles = positions * inverse
    cosine = jnp.cos(angles)
    sine = jnp.sin(angles)
    first = values[..., :half]
    second = values[..., half:]
    return jnp.concatenate([first * cosine - second * sine, second * cosine + first * sine], -1)

def normalize_rows(values, gain):
    return values * lax.rsqrt(lax.optimization_barrier(jnp.mean(values * values, -1, keepdims=True)) + 1e-06) * gain

def reference(tokens, w_down_q, w_down_kv, q_gain, kv_gain, w_up_q, w_absorb, w_value, slot_block):
    positions = jnp.arange(TOKENS, dtype=jnp.int32).astype(jnp.float32)
    down_q = jnp.dot(tokens, w_down_q, preferred_element_type=jnp.float32)
    down_kv = jnp.dot(tokens, w_down_kv, preferred_element_type=jnp.float32)
    compressed = normalize_rows(down_q, q_gain).astype(jnp.bfloat16)
    latent = normalize_rows(down_kv[:, :KVL], kv_gain).astype(jnp.bfloat16)
    rotated = rotate_pairs(down_kv[:, KVL:], positions[:, None]).astype(jnp.bfloat16)
    keys = jnp.concatenate([latent, rotated], 1)
    projected = jnp.dot(compressed, w_up_q, preferred_element_type=jnp.float32).reshape(TOKENS, H, NOPE + ROPE)
    nope = projected[..., :NOPE].astype(jnp.bfloat16)
    rotated_q = rotate_pairs(projected[..., NOPE:], positions[:, None, None]).astype(jnp.bfloat16)
    absorbed = jnp.einsum('thn,hnc->thc', nope.astype(jnp.float32), w_absorb.astype(jnp.float32)).astype(jnp.bfloat16)
    queries = jnp.transpose(jnp.concatenate([absorbed, rotated_q], -1), (1, 0, 2))
    scale = (NOPE + ROPE) ** (-0.5)

    def one_head(operands):
        head_queries, value_map = operands
        outputs = []
        for block_index in range(N_CHAIN):
            lower = block_index * TOK_DEV
            query_rows = head_queries[lower:lower + TOK_DEV]
            key_rows = keys[:lower + TOK_DEV]
            scores = jnp.dot(query_rows, key_rows.T, preferred_element_type=jnp.float32) * scale
            query_index = lower + jnp.arange(TOK_DEV, dtype=jnp.int32)
            key_index = jnp.arange(lower + TOK_DEV, dtype=jnp.int32)
            visible = key_index[None, :] <= query_index[:, None]
            scores = jnp.where(visible, scores, -jnp.inf)
            peak = lax.optimization_barrier(jnp.max(scores, -1, keepdims=True))
            exponent = jnp.exp(scores - peak)
            totals = lax.optimization_barrier(jnp.sum(exponent, -1, keepdims=True))
            mixed = (jnp.dot(exponent.astype(jnp.bfloat16), key_rows[:, :KVL], preferred_element_type=jnp.float32) / totals).astype(jnp.bfloat16)
            outputs.append(jnp.dot(mixed, value_map, preferred_element_type=jnp.float32).astype(jnp.bfloat16))
        return jnp.concatenate(outputs, 0)
    stacked = lax.map(one_head, (queries, w_value))
    attended = jnp.transpose(stacked, (1, 0, 2)).reshape(TOKENS, H * VH)
    blocks = keys.reshape(CACHE_SLOTS, BLOCK, KVL + ROPE)
    latent_cache = jnp.take(blocks, slot_block.astype(jnp.int32), axis=0)
    return (attended, latent_cache)
```

```python
import functools
import math

import jax
import jax.numpy as jnp
import numpy as np
from jax import lax
from jax.experimental import pallas as pl
from jax.experimental.pallas import tpu as pltpu
from jax.sharding import PartitionSpec as P

MESH = pl.DeviceIdType.MESH
ROPE_BASE = 50000.0
FLOOR_SCORE = -1e30
QL, LAT, ROPE, NOPE, VH, HEADS = 1536, 512, 64, 128, 128, 8
KEYW = 640
KV = LAT + ROPE
SCALE2 = (NOPE + ROPE) ** -0.5 * math.log2(math.e)
NT = (((1,), (1,)), ((), ()))
N_SEND = 80
RINGS = (
    (0, 0), (3, 0), (1, 0), (0, 3), (0, 1), (3, 3), (3, 1), (1, 3), (1, 1), (2, 0), (0, 2),
    (2, 3), (2, 1), (3, 2), (1, 2), (2, 2),
)


def rotary_tables():
    inverse = ROPE_BASE ** (-2.0 * np.arange(ROPE // 2) / ROPE)
    angles = np.arange(4096)[:, None] * inverse[None, :]
    cosine = np.concatenate([np.cos(angles), np.cos(angles)], 1)
    sine = np.concatenate([-np.sin(angles), np.sin(angles)], 1)
    both = np.concatenate([cosine, sine], 1).astype(np.float32)
    return both.reshape(16, 8, 2, 16, 2 * ROPE)


def rotate(values, table):
    half = ROPE // 2
    swapped = jnp.concatenate([values[:, half:], values[:, :half]], 1)
    return values * table[:, :ROPE] + swapped * table[:, ROPE:]


def normalize(values, gain):
    return values * lax.rsqrt(jnp.mean(values * values, -1, keepdims=True) + 1e-06) * gain


def kernel(
    tok_h, wq_h, wkv_h, qg_h, kvg_h, wu_h, wa_h, wv_h, slot_ref, tab_h,
    out_h, cache_ref,
    tok, wq, wkv, qg, kvg, wu, wa, wv, tabk, tabq,
    psk, pok, prk, psq, poq, prq, rks, rkr, rqs, rqr, cs, cq, kb, qt, wat, wvt, acc, mx, tot, ob,
    load_sem, send_sem, sib_sem, rk_sem, rq_sem, cq_sem, ky_sem, kp_sem, ks_sem, out_sem, own_sem,
):
    chain = lax.axis_index("chain")
    tp = lax.axis_index("tp")
    z, x = chain // 4, chain % 4
    y, core = tp // 2, tp % 2
    other = 1 - core
    mirror = 15 - chain
    half = chain // 8
    piece = core * 4 + y
    yp, ym, yf = (y + 1) % 4, (y + 3) % 4, (y + 2) % 4
    sibling = {"chain": chain, "tp": 2 * y + other}
    up = {"chain": chain, "tp": 2 * yp + core}
    down = {"chain": chain, "tp": 2 * ym + core}
    pair = {"chain": mirror, "tp": tp}
    a = x + core * (z - x)
    b = z + core * (x - z)
    stride_a, stride_b = 1 + 3 * core, 4 - 3 * core

    def at(da, db):
        return ((a + da) % 4) * stride_a + ((b + db) % 4) * stride_b

    ap = {"chain": at(1, 0), "tp": tp}
    am = {"chain": at(3, 0), "tp": tp}
    bp = {"chain": at(0, 1), "tp": tp}
    bm = {"chain": at(0, 3), "tp": tp}

    loads = {}
    for k, (name, src, dst) in enumerate(
        [
            ("tok", tok_h, tok), ("wkv", wkv_h, wkv), ("wq", wq_h, wq), ("kvg", kvg_h, kvg),
            ("qg", qg_h, qg), ("tabk", tab_h.at[chain, piece], tabk), ("wa", wa_h, wa),
            ("wu", wu_h, wu), ("wv", wv_h, wv), ("tab0", tab_h.at[chain, :, half], tabq.at[0]),
            ("tab1", tab_h.at[mirror, :, half], tabq.at[1]),
        ]
    ):
        loads[name] = pltpu.make_async_copy(src, dst, load_sem.at[k])
        loads[name].start()

    def loaded(*names):
        for name in names:
            loads[name].wait()

    barrier = pltpu.get_barrier_semaphore()
    partners = (sibling, up, down, pair, ap, am, bp, bm)
    for device in partners:
        pl.semaphore_signal(barrier, inc=1, device_id=device, device_id_type=MESH)
    pl.semaphore_wait(barrier, len(partners))

    sent = []

    def send(src, dst, recv, device):
        copy = pltpu.make_async_remote_copy(
            src_ref=src, dst_ref=dst, send_sem=send_sem.at[len(sent)], recv_sem=recv,
            device_id=device, device_id_type=MESH,
        )
        copy.start()
        sent.append(copy)

    def arrived(dst, recv):
        pltpu.make_async_remote_copy(
            src_ref=dst, dst_ref=dst, send_sem=send_sem.at[0], recv_sem=recv,
            device_id=sibling, device_id_type=MESH,
        ).wait_recv()

    def rows_of(c):
        return tok[pl.ds(pl.multiple_of(c * 128, 128), 128), :]

    def project_keys(c, dst):
        dst[...] = lax.dot_general(rows_of(c), wkv[...], NT, preferred_element_type=jnp.float32)

    def project_queries(c, dst):
        left = rows_of(c)

        def tile(i, _):
            cols = pl.ds(pl.multiple_of(i * 512, 512), 512)
            dst[:, cols] = jnp.dot(left, wq[:, cols], preferred_element_type=jnp.float32)
            return 0

        lax.fori_loop(0, 3, tile, 0)

    def ring_of(own, got, out, came, sems):
        def part(yy, h):
            rows = pl.ds(pl.multiple_of(yy * 32 + h * 16, 16), 16)
            return own[rows, :] + got[rows, :]

        def push(k, value, device):
            out[k] = value.astype(out.dtype)
            send(out.at[k], came.at[k], sems.at[k], device)

        def start():
            push(0, part(yf, 0), up)
            push(1, part(yf, 1), down)
            push(2, part(yp, 1), up)
            push(3, part(ym, 0), down)

        def middle():
            arrived(came.at[0], sems.at[0])
            push(4, part(yp, 0) + came[0].astype(jnp.float32), up)
            arrived(came.at[1], sems.at[1])
            push(5, part(ym, 1) + came[1].astype(jnp.float32), down)

        def end():
            for k in (2, 3, 4, 5):
                arrived(came.at[k], sems.at[k])
            totals = []
            for h, first, second in ((0, 4, 3), (1, 2, 5)):
                total = part(y, h) + came[first].astype(jnp.float32)
                totals.append(total + came[second].astype(jnp.float32))
            return totals

        return start, middle, end

    keys_start, keys_middle, keys_end = ring_of(pok, prk, rks, rkr, rk_sem)
    queries_start, queries_middle, queries_end = ring_of(poq, prq, rqs, rqr, rq_sem)

    loaded("tok", "wkv")
    project_keys(other, psk)
    send(psk, prk, sib_sem.at[0], sibling)
    project_keys(core, pok)
    loaded("wq")
    project_queries(other, psq)
    send(psq, prq, sib_sem.at[1], sibling)
    arrived(prk, sib_sem.at[0])
    keys_start()
    project_queries(core, poq)
    keys_middle()
    arrived(prq, sib_sem.at[1])
    queries_start()

    loaded("wa")

    def turn_absorb(h, _):
        wat[h] = wa[h].T
        return 0

    lax.fori_loop(0, HEADS, turn_absorb, 0)

    slot_own = 2 * chain + core

    def keys_y(yy, h, n):
        return kb.at[slot_own, pl.ds(pl.multiple_of(yy * 32 + h * 16, 16), n)]

    loaded("kvg", "tabk")
    gain_kv = jnp.concatenate([kvg[k : k + 1, :] for k in range(LAT // 128)], 1)
    for h, total in enumerate(keys_end()):
        latent = normalize(total[:, :LAT], gain_kv)
        turned = rotate(total[:, LAT:], tabk[h])
        rows = pl.ds(pl.multiple_of(y * 32 + h * 16, 16), 16)
        kb[slot_own, rows, :LAT] = latent.astype(jnp.bfloat16)
        kb[slot_own, rows, LAT:] = jnp.concatenate(
            [turned, jnp.zeros_like(turned)], 1
        ).astype(jnp.bfloat16)
    for k, device in enumerate((up, down)):
        send(keys_y(y, 0, 32), keys_y(y, 0, 32), ky_sem.at[k], device)
    queries_middle()
    arrived(keys_y(ym, 0, 32), ky_sem.at[0])
    send(keys_y(ym, 0, 16), keys_y(ym, 0, 16), ky_sem.at[2], up)
    arrived(keys_y(yp, 0, 32), ky_sem.at[1])
    send(keys_y(yp, 1, 16), keys_y(yp, 1, 16), ky_sem.at[3], down)

    def block(n, p=None):
        if p is None:
            return kb.at[2 * n + core]
        return kb.at[2 * n + core, pl.ds(64 * p, 64)]

    def pass_on(n, *devices):
        for device in devices:
            send(block(n), block(n), kp_sem.at[n, 0], device)
        send(block(n), block(n), ks_sem.at[n], sibling)

    def pass_part(n, p, device):
        send(block(n, p), block(n, p), kp_sem.at[n, p], device)

    def whole(n):
        arrived(block(n), kp_sem.at[n, 0])

    def halves(n):
        for p in range(2):
            arrived(block(n, p), kp_sem.at[n, p])

    def relay(u, v):
        n = at(u, v)
        if v == 2 or (u, v) == (2, 0):
            halves(n)
        else:
            whole(n)
        if v == 0:
            if u != 2:
                pass_part(n, 0 if u == 3 else 1, ap if u == 3 else am)
            pass_on(n, bp, bm)
        else:
            if v != 2:
                pass_part(n, 0 if v == 3 else 1, bp if v == 3 else bm)
            pass_on(n)

    arrived(keys_y(yf, 0, 16), ky_sem.at[2])
    arrived(keys_y(yf, 1, 16), ky_sem.at[3])
    pass_on(at(0, 0), ap, am, bp, bm)

    loaded("qg")
    gain_q = jnp.concatenate([qg[k : k + 1, :] for k in range(QL // 128)], 1)
    for h, total in enumerate(queries_end()):
        cs[h] = normalize(total, gain_q).astype(jnp.bfloat16)

    def give(s, p, *devices):
        for device in devices:
            send(cq.at[s, p], cq.at[s, p], cq_sem.at[s, p], device)

    def take(s, p):
        arrived(cq.at[s, p], cq_sem.at[s, p])

    send(cs.at[1 - half], cq.at[1, piece], cq_sem.at[1, piece], pair)
    cq[0, piece] = cs[half]
    give(0, piece, up, down, sibling)
    pm, pp, pf = core * 4 + ym, core * 4 + yp, core * 4 + yf
    for u, v in RINGS[1:5]:
        relay(u, v)
    take(1, piece)
    give(1, piece, up, down, sibling)
    take(0, pm)
    give(0, pm, up, sibling)
    take(0, pp)
    give(0, pp, sibling)
    take(1, pp)
    give(1, pp, down, sibling)
    take(1, pm)
    give(1, pm, sibling)
    for u, v in ((2, 0), (3, 3), (3, 1), (1, 3), (1, 1), (0, 2)):
        relay(u, v)
    loaded("wv")

    def turn_value(h, _):
        wvt[h] = wv[h].T
        return 0

    lax.fori_loop(0, HEADS, turn_value, 0)
    take(0, pf)
    give(0, pf, sibling)
    take(1, pf)
    give(1, pf, sibling)
    for s in range(2):
        for yy in range(4):
            take(s, other * 4 + yy)

    loaded("wu", "tab0", "tab1")

    def expand(i, _):
        cols = pl.ds(pl.multiple_of(i * 384, 384), 384)
        rows = cq[...].reshape(256, QL)
        projected = jnp.dot(rows, wu[:, cols], preferred_element_type=jnp.float32)
        table = tabq[...].reshape(256, 2 * ROPE)
        for j in range(2):
            head = 2 * i + j
            base = j * (NOPE + ROPE)
            nope = projected[:, base : base + NOPE].astype(jnp.bfloat16)
            turned = rotate(projected[:, base + NOPE : base + NOPE + ROPE], table)
            turned = jnp.concatenate([turned, jnp.zeros_like(turned)], 1).astype(jnp.bfloat16).T
            absorbed = jnp.dot(wat[head], nope.T, preferred_element_type=jnp.float32)
            absorbed = absorbed.astype(jnp.bfloat16)
            places = pl.ds(pl.multiple_of(head * 128, 128), 128)
            for s in range(2):
                qt[s, :LAT, places] = absorbed[:, s * 128 : s * 128 + 128]
                qt[s, LAT:, places] = turned[:, s * 128 : s * 128 + 128]
        return 0

    lax.fori_loop(0, HEADS // 4, expand, 0)
    for u, v in ((2, 3), (2, 1), (3, 2), (1, 2)):
        relay(u, v)
    lax.fori_loop(HEADS // 4, HEADS // 2, expand, 0)
    acc[...] = jnp.zeros_like(acc)
    tot[...] = jnp.zeros_like(tot)
    mx[...] = jnp.full_like(mx, FLOOR_SCORE)

    def whole(n):
        arrived(block(n), kp_sem.at[n, 0])

    def halves(n):
        for p in range(2):
            arrived(block(n, p), kp_sem.at[n, p])

    relay(2, 2)
    for n in range(16):
        arrived(kb.at[2 * n + other], ks_sem.at[n])
    for j in range(2):
        rows = pl.ds(pl.multiple_of(tp * 16, 16), 16)
        cache_ref[j] = kb[slot_ref[j], rows, :][:, :KV]

    token = lax.broadcasted_iota(jnp.int32, (1, 256), 1) & 127
    place = ((token >> 4) << 5) + (token & 15) + half * 16
    key_iota = lax.broadcasted_iota(jnp.int32, (512, 1), 0)

    def chunk(s, c, blk, masked):
        keys = kb[pl.ds(4 * c, 4)].reshape(512, KEYW)
        latent_t = keys[:, :LAT].T

        def score(r):
            queries = qt[s, :, 256 * r : 256 * r + 256]
            return jnp.dot(keys, queries, preferred_element_type=jnp.float32)

        ahead = score(0)
        for r in range(4):
            cols = slice(256 * r, 256 * r + 256)
            scores = ahead * SCALE2
            if r < 3:
                ahead = score(r + 1)
            if masked:
                visible = key_iota + 512 * c <= place + 256 * blk
                scores = jnp.where(visible, scores, FLOOR_SCORE)
            before = mx[s, :, cols]
            peak = jnp.maximum(before, jnp.max(scores, 0, keepdims=True))
            shrink = jnp.exp2(before - peak)
            weights = jnp.exp2(scores - peak)
            mx[s, :, cols] = peak
            tot[s, :, cols] = tot[s, :, cols] * shrink + jnp.sum(weights, 0, keepdims=True)
            mixed = jnp.dot(latent_t, weights.astype(jnp.bfloat16), preferred_element_type=jnp.float32)
            acc[s, :, cols] = acc[s, :, cols] * shrink + mixed

    def attend(s, blk):
        def step(c, _):
            chunk(s, c, blk, False)
            return 0

        lax.fori_loop(0, blk // 2, step, 0)
        chunk(s, blk // 2, blk, True)

    def finish(s):
        def value_of(h, _):
            cols = pl.ds(pl.multiple_of(h * VH, VH), VH)
            mixed = (acc[s, :, cols] / tot[s, :, cols]).astype(jnp.bfloat16)
            value = jnp.dot(wvt[h], mixed, preferred_element_type=jnp.float32).T
            ob[s, :, :, cols] = value.astype(jnp.bfloat16).reshape(8, 16, VH)
            return 0

        lax.fori_loop(0, HEADS, value_of, 0)

    attend(1, mirror)
    finish(1)
    send(ob.at[1], out_h.at[:, half], out_sem.at[0], pair)
    attend(0, chain)
    finish(0)
    keep = pltpu.make_async_copy(ob.at[0], out_h.at[:, half], own_sem.at[0])
    keep.start()
    keep.wait()
    arrived(out_h.at[:, 1 - half], out_sem.at[0])
    for copy in sent:
        copy.wait_send()


def hand_over(att_h, cache_h, att_out, cache_out, att, cache, sem):
    pieces = [(cache_h, cache, cache_out)]
    for k in range(4):
        rows = pl.ds(64 * k, 64)
        pieces.append((att_h.at[rows], att.at[rows], att_out.at[rows]))
    into = [pltpu.make_async_copy(p[0], p[1], sem.at[0, k]) for k, p in enumerate(pieces)]
    out = [pltpu.make_async_copy(p[1], p[2], sem.at[1, k]) for k, p in enumerate(pieces)]
    for copy in into:
        copy.start()
    for first, second in zip(into, out):
        first.wait()
        second.start()
    for copy in out:
        copy.wait()


def per_device(tokens, w_down_q, w_down_kv, q_gain, kv_gain, w_up_q, w_absorb, w_value, slot_block):
    bf16, f32 = jnp.bfloat16, jnp.float32
    table = jnp.asarray(rotary_tables())
    hbm = pl.BlockSpec(memory_space=pl.ANY)
    dma = pltpu.SemaphoreType.DMA
    attended, cache = pl.pallas_call(
        kernel,
        out_shape=(
            jax.ShapeDtypeStruct((8, 2, 16, HEADS * VH), bf16),
            jax.ShapeDtypeStruct((2, 16, KV), bf16),
        ),
        in_specs=[hbm] * 8 + [pl.BlockSpec(memory_space=pltpu.SMEM), hbm],
        out_specs=(hbm, pl.BlockSpec(memory_space=pltpu.VMEM)),
        scratch_shapes=[
            pltpu.VMEM((256, 896), bf16),
            pltpu.VMEM((896, QL), bf16),
            pltpu.VMEM((KV, 896), bf16),
            pltpu.VMEM((QL // 128, 128), f32),
            pltpu.VMEM((LAT // 128, 128), f32),
            pltpu.VMEM((QL, HEADS * (NOPE + ROPE)), bf16),
            pltpu.VMEM((HEADS, NOPE, LAT), bf16),
            pltpu.VMEM((HEADS, LAT, VH), bf16),
            pltpu.VMEM((2, 16, 2 * ROPE), f32),
            pltpu.VMEM((2, 8, 16, 2 * ROPE), f32),
            pltpu.VMEM((128, KV), f32),
            pltpu.VMEM((128, KV), f32),
            pltpu.VMEM((128, KV), f32),
            pltpu.VMEM((128, QL), f32),
            pltpu.VMEM((128, QL), f32),
            pltpu.VMEM((128, QL), f32),
            pltpu.VMEM((6, 16, KV), bf16),
            pltpu.VMEM((6, 16, KV), bf16),
            pltpu.VMEM((6, 16, QL), f32),
            pltpu.VMEM((6, 16, QL), f32),
            pltpu.VMEM((2, 16, QL), bf16),
            pltpu.VMEM((2, 8, 16, QL), bf16),
            pltpu.VMEM((32, 128, KEYW), bf16),
            pltpu.VMEM((2, KEYW, HEADS * 128), bf16),
            pltpu.VMEM((HEADS, LAT, NOPE), bf16),
            pltpu.VMEM((HEADS, VH, LAT), bf16),
            pltpu.VMEM((2, LAT, HEADS * 128), f32),
            pltpu.VMEM((2, 1, HEADS * 128), f32),
            pltpu.VMEM((2, 1, HEADS * 128), f32),
            pltpu.VMEM((2, 8, 16, HEADS * VH), bf16),
            dma((11,)),
            dma((N_SEND,)),
            dma((2,)),
            dma((6,)),
            dma((6,)),
            dma((2, 8)),
            dma((4,)),
            dma((16, 2)),
            dma((16,)),
            dma((1,)),
            dma((1,)),
        ],
        compiler_params=pltpu.CompilerParams(
            collective_id=0, has_side_effects=True, vmem_limit_bytes=56 * 2**20
        ),
    )(
        tokens, w_down_q, w_down_kv.T, q_gain.reshape(-1, 128), kv_gain.reshape(-1, 128),
        w_up_q, w_absorb, w_value, slot_block, table,
    )
    attended = attended.reshape(256, HEADS * VH)
    return pl.pallas_call(
        hand_over,
        out_shape=(
            jax.ShapeDtypeStruct(attended.shape, bf16),
            jax.ShapeDtypeStruct(cache.shape, bf16),
        ),
        in_specs=[hbm, hbm],
        out_specs=(hbm, hbm),
        scratch_shapes=[
            pltpu.VMEM(attended.shape, bf16),
            pltpu.VMEM(cache.shape, bf16),
            dma((2, 5)),
        ],
        compiler_params=pltpu.CompilerParams(vmem_limit_bytes=60 * 2**20),
    )(attended, cache)


def solution(mesh):
    placed = (
        P("chain", "tp"),
        P("tp", None),
        P("tp", None),
        P(),
        P(),
        P(None, "tp"),
        P("tp", None, None),
        P("tp", None, None),
        P("chain"),
    )
    return jax.shard_map(
        per_device,
        mesh=mesh,
        in_specs=placed,
        out_specs=(P("chain", "tp"), P("chain", "tp", None)),
        check_vma=False,
    )
```

```python
import functools
import math

import jax
import jax.numpy as jnp
import numpy as np
from jax import lax
from jax.experimental import pallas as pl
from jax.experimental.pallas import tpu as pltpu
from jax.sharding import PartitionSpec as P

MESH = pl.DeviceIdType.MESH
ROPE_BASE = 50000.0
FLOOR_SCORE = -1e30
QL, LAT, ROPE, NOPE, VH, HEADS = 1536, 512, 64, 128, 128, 8
KEYW = 640
KV = LAT + ROPE
SCALE2 = (NOPE + ROPE) ** -0.5 * math.log2(math.e)
NT = (((1,), (1,)), ((), ()))
N_SEND = 80
RINGS = (
    (0, 0), (3, 0), (1, 0), (0, 3), (0, 1), (2, 0), (3, 3), (3, 1), (1, 3), (1, 1), (0, 2),
    (2, 3), (2, 1), (3, 2), (1, 2), (2, 2),
)


def rotary_tables():
    inverse = ROPE_BASE ** (-2.0 * np.arange(ROPE // 2) / ROPE)
    angles = np.arange(4096)[:, None] * inverse[None, :]
    cosine = np.concatenate([np.cos(angles), np.cos(angles)], 1)
    sine = np.concatenate([-np.sin(angles), np.sin(angles)], 1)
    both = np.concatenate([cosine, sine], 1).astype(np.float32)
    return both.reshape(16, 8, 2, 16, 2 * ROPE)


def rotate(values, table):
    half = ROPE // 2
    swapped = jnp.concatenate([values[:, half:], values[:, :half]], 1)
    return values * table[:, :ROPE] + swapped * table[:, ROPE:]


def normalize(values, gain):
    return values * lax.rsqrt(jnp.mean(values * values, -1, keepdims=True) + 1e-06) * gain


def kernel(
    tok_h, wq_h, wkv_h, qg_h, kvg_h, wu_h, wa_h, wv_h, slot_ref, tab_h,
    out_h, cache_ref,
    tok, wq, wkv, qg, kvg, wu, wa, wv, tabk, tabq,
    psk, pok, prk, psq, poq, prq, rks, rkr, rqs, rqr, cs, cq, kb, kt, qt, wat, wvt, first, acc, mx, tot, ob,
    load_sem, send_sem, sib_sem, rk_sem, rq_sem, cq_sem, ky_sem, kp_sem, ks_sem, out_sem, own_sem,
):
    chain = lax.axis_index("chain")
    tp = lax.axis_index("tp")
    z, x = chain // 4, chain % 4
    y, core = tp // 2, tp % 2
    other = 1 - core
    mirror = 15 - chain
    half = chain // 8
    piece = core * 4 + y
    yp, ym, yf = (y + 1) % 4, (y + 3) % 4, (y + 2) % 4
    sibling = {"chain": chain, "tp": 2 * y + other}
    up = {"chain": chain, "tp": 2 * yp + core}
    down = {"chain": chain, "tp": 2 * ym + core}
    pair = {"chain": mirror, "tp": tp}
    a = x + core * (z - x)
    b = z + core * (x - z)
    stride_a, stride_b = 1 + 3 * core, 4 - 3 * core

    def at(da, db):
        return ((a + da) % 4) * stride_a + ((b + db) % 4) * stride_b

    ap = {"chain": at(1, 0), "tp": tp}
    am = {"chain": at(3, 0), "tp": tp}
    bp = {"chain": at(0, 1), "tp": tp}
    bm = {"chain": at(0, 3), "tp": tp}

    loads = {}
    for k, (name, src, dst) in enumerate(
        [
            ("tok", tok_h, tok), ("wkv", wkv_h, wkv), ("wq", wq_h, wq), ("kvg", kvg_h, kvg),
            ("qg", qg_h, qg), ("tabk", tab_h.at[chain, piece], tabk), ("wa", wa_h, wa),
            ("wu", wu_h, wu), ("wv", wv_h, wv), ("tab0", tab_h.at[chain, :, half], tabq.at[0]),
            ("tab1", tab_h.at[mirror, :, half], tabq.at[1]),
        ]
    ):
        loads[name] = pltpu.make_async_copy(src, dst, load_sem.at[k])
        loads[name].start()

    def loaded(*names):
        for name in names:
            loads[name].wait()

    barrier = pltpu.get_barrier_semaphore()
    partners = (sibling, up, down, pair, ap, am, bp, bm)
    for device in partners:
        pl.semaphore_signal(barrier, inc=1, device_id=device, device_id_type=MESH)
    pl.semaphore_wait(barrier, len(partners))

    sent = []

    def send(src, dst, recv, device):
        copy = pltpu.make_async_remote_copy(
            src_ref=src, dst_ref=dst, send_sem=send_sem.at[len(sent)], recv_sem=recv,
            device_id=device, device_id_type=MESH,
        )
        copy.start()
        sent.append(copy)

    def arrived(dst, recv):
        pltpu.make_async_remote_copy(
            src_ref=dst, dst_ref=dst, send_sem=send_sem.at[0], recv_sem=recv,
            device_id=sibling, device_id_type=MESH,
        ).wait_recv()

    def rows_of(c):
        return tok[pl.ds(pl.multiple_of(c * 128, 128), 128), :]

    def project_keys(c, dst):
        dst[...] = lax.dot_general(rows_of(c), wkv[...], NT, preferred_element_type=jnp.float32)

    def project_queries(c, dst):
        left = rows_of(c)

        def tile(i, _):
            cols = pl.ds(pl.multiple_of(i * 512, 512), 512)
            dst[:, cols] = jnp.dot(left, wq[:, cols], preferred_element_type=jnp.float32)
            return 0

        lax.fori_loop(0, 3, tile, 0)

    def ring_of(own, got, out, came, sems):
        def part(yy, h):
            rows = pl.ds(pl.multiple_of(yy * 32 + h * 16, 16), 16)
            return own[rows, :] + got[rows, :]

        def push(k, value, device):
            out[k] = value.astype(out.dtype)
            send(out.at[k], came.at[k], sems.at[k], device)

        def start():
            push(0, part(yf, 0), up)
            push(1, part(yf, 1), down)
            push(2, part(yp, 1), up)
            push(3, part(ym, 0), down)

        def middle():
            arrived(came.at[0], sems.at[0])
            push(4, part(yp, 0) + came[0].astype(jnp.float32), up)
            arrived(came.at[1], sems.at[1])
            push(5, part(ym, 1) + came[1].astype(jnp.float32), down)

        def end():
            for k in (2, 3, 4, 5):
                arrived(came.at[k], sems.at[k])
            totals = []
            for h, first, second in ((0, 4, 3), (1, 2, 5)):
                total = part(y, h) + came[first].astype(jnp.float32)
                totals.append(total + came[second].astype(jnp.float32))
            return totals

        return start, middle, end

    keys_start, keys_middle, keys_end = ring_of(pok, prk, rks, rkr, rk_sem)
    queries_start, queries_middle, queries_end = ring_of(poq, prq, rqs, rqr, rq_sem)

    loaded("tok", "wkv")
    project_keys(other, psk)
    send(psk, prk, sib_sem.at[0], sibling)
    project_keys(core, pok)
    loaded("wq")
    project_queries(other, psq)
    send(psq, prq, sib_sem.at[1], sibling)
    arrived(prk, sib_sem.at[0])
    keys_start()
    project_queries(core, poq)
    keys_middle()
    arrived(prq, sib_sem.at[1])
    queries_start()

    loaded("wa")

    def turn_absorb(h, _):
        wat[h] = wa[h].T
        return 0

    lax.fori_loop(0, HEADS, turn_absorb, 0)

    slot_own = 2 * chain + core

    def keys_y(yy, h, n):
        return kb.at[slot_own, pl.ds(pl.multiple_of(yy * 32 + h * 16, 16), n)]

    loaded("kvg", "tabk")
    gain_kv = jnp.concatenate([kvg[k : k + 1, :] for k in range(LAT // 128)], 1)
    for h, total in enumerate(keys_end()):
        latent = normalize(total[:, :LAT], gain_kv)
        turned = rotate(total[:, LAT:], tabk[h])
        rows = pl.ds(pl.multiple_of(y * 32 + h * 16, 16), 16)
        kb[slot_own, rows, :LAT] = latent.astype(jnp.bfloat16)
        kb[slot_own, rows, LAT:] = jnp.concatenate(
            [turned, jnp.zeros_like(turned)], 1
        ).astype(jnp.bfloat16)
    for k, device in enumerate((up, down)):
        send(keys_y(y, 0, 32), keys_y(y, 0, 32), ky_sem.at[k], device)
    queries_middle()
    arrived(keys_y(ym, 0, 32), ky_sem.at[0])
    send(keys_y(ym, 0, 16), keys_y(ym, 0, 16), ky_sem.at[2], up)
    arrived(keys_y(yp, 0, 32), ky_sem.at[1])
    send(keys_y(yp, 1, 16), keys_y(yp, 1, 16), ky_sem.at[3], down)

    def block(n, p=None):
        if p is None:
            return kb.at[2 * n + core]
        return kb.at[2 * n + core, pl.ds(64 * p, 64)]

    def pass_on(n, *devices):
        for device in devices:
            send(block(n), block(n), kp_sem.at[n, 0], device)
        send(block(n), block(n), ks_sem.at[n], sibling)

    def pass_part(n, p, device):
        send(block(n, p), block(n, p), kp_sem.at[n, p], device)

    def turn(n, side):
        cols = pl.ds(pl.multiple_of((n % 2) * 256 + side * 128, 128), 128)
        kt[n // 2, :, cols] = kb[2 * n + side, :, :LAT].T

    def turn_own(steps):
        for u, v in steps:
            turn(at(u, v), core)

    def turn_other(steps):
        for u, v in steps:
            n = at(u, v)
            arrived(kb.at[2 * n + other], ks_sem.at[n])
            turn(n, other)

    def whole(n):
        arrived(block(n), kp_sem.at[n, 0])

    def halves(n):
        for p in range(2):
            arrived(block(n, p), kp_sem.at[n, p])

    def relay(u, v):
        n = at(u, v)
        if v == 2 or (u, v) == (2, 0):
            halves(n)
        else:
            whole(n)
        if v == 0:
            if u != 2:
                pass_part(n, 0 if u == 3 else 1, ap if u == 3 else am)
            pass_on(n, bp, bm)
        else:
            if v != 2:
                pass_part(n, 0 if v == 3 else 1, bp if v == 3 else bm)
            pass_on(n)

    arrived(keys_y(yf, 0, 16), ky_sem.at[2])
    arrived(keys_y(yf, 1, 16), ky_sem.at[3])
    pass_on(at(0, 0), ap, am, bp, bm)
    turn_own(RINGS[:1])

    loaded("qg")
    gain_q = jnp.concatenate([qg[k : k + 1, :] for k in range(QL // 128)], 1)
    for h, total in enumerate(queries_end()):
        cs[h] = normalize(total, gain_q).astype(jnp.bfloat16)

    def give(s, p, *devices):
        for device in devices:
            send(cq.at[s, p], cq.at[s, p], cq_sem.at[s, p], device)

    def take(s, p):
        arrived(cq.at[s, p], cq_sem.at[s, p])

    send(cs.at[1 - half], cq.at[1, piece], cq_sem.at[1, piece], pair)
    cq[0, piece] = cs[half]
    give(0, piece, up, down, sibling)
    pm, pp, pf = core * 4 + ym, core * 4 + yp, core * 4 + yf
    for u, v in RINGS[1:5]:
        relay(u, v)
    take(1, piece)
    give(1, piece, up, down, sibling)
    turn_own(RINGS[1:5])
    turn_other(RINGS[:1])
    take(0, pm)
    give(0, pm, up, sibling)
    take(0, pp)
    give(0, pp, sibling)
    take(1, pp)
    give(1, pp, down, sibling)
    take(1, pm)
    give(1, pm, sibling)
    for u, v in RINGS[5:11]:
        relay(u, v)
    turn_other(RINGS[1:5])
    loaded("wv")

    def turn_value(h, _):
        wvt[h] = wv[h].T
        return 0

    lax.fori_loop(0, HEADS, turn_value, 0)
    take(0, pf)
    give(0, pf, sibling)
    take(1, pf)
    give(1, pf, sibling)
    for s in range(2):
        for yy in range(4):
            take(s, other * 4 + yy)

    loaded("wu", "tab0", "tab1")

    def expand(i, _):
        cols = pl.ds(pl.multiple_of(i * 384, 384), 384)
        rows = cq[...].reshape(256, QL)
        projected = jnp.dot(rows, wu[:, cols], preferred_element_type=jnp.float32)
        table = tabq[...].reshape(256, 2 * ROPE)
        for j in range(2):
            head = 2 * i + j
            base = j * (NOPE + ROPE)
            nope = projected[:, base : base + NOPE].astype(jnp.bfloat16)
            turned = rotate(projected[:, base + NOPE : base + NOPE + ROPE], table)
            turned = jnp.concatenate([turned, jnp.zeros_like(turned)], 1).astype(jnp.bfloat16).T
            absorbed = jnp.dot(wat[head], nope.T, preferred_element_type=jnp.float32)
            absorbed = absorbed.astype(jnp.bfloat16)
            places = pl.ds(pl.multiple_of(head * 128, 128), 128)
            for s in range(2):
                qt[s, :LAT, places] = absorbed[:, s * 128 : s * 128 + 128]
                qt[s, LAT:, places] = turned[:, s * 128 : s * 128 + 128]
        return 0

    expand(0, 0)
    turn_own(RINGS[5:11])
    expand(1, 0)
    for u, v in RINGS[11:15]:
        relay(u, v)
    expand(2, 0)
    turn_own(RINGS[11:15])
    for u, v in RINGS[5:11]:
        arrived(kb.at[2 * at(u, v) + other], ks_sem.at[at(u, v)])
    expand(3, 0)
    for u, v in RINGS[5:11]:
        turn(at(u, v), other)
    acc[...] = jnp.zeros_like(acc)
    tot[...] = jnp.zeros_like(tot)
    mx[...] = jnp.full_like(mx, FLOOR_SCORE)

    def turn(n, side):
        cols = pl.ds(pl.multiple_of((n % 2) * 256 + side * 128, 128), 128)
        kt[n // 2, :, cols] = kb[2 * n + side, :, :LAT].T

    def turn_own(steps):
        for u, v in steps:
            turn(at(u, v), core)

    def turn_other(steps):
        for u, v in steps:
            n = at(u, v)
            arrived(kb.at[2 * n + other], ks_sem.at[n])
            turn(n, other)

    def whole(n):
        arrived(block(n), kp_sem.at[n, 0])

    def halves(n):
        for p in range(2):
            arrived(block(n, p), kp_sem.at[n, p])

    relay(2, 2)
    turn_own(RINGS[15:])
    turn_other(RINGS[11:])
    for j in range(2):
        rows = pl.ds(pl.multiple_of(tp * 16, 16), 16)
        cache_ref[j] = kb[slot_ref[j], rows, :][:, :KV]

    token = lax.broadcasted_iota(jnp.int32, (1, 256), 1) & 127
    place = ((token >> 4) << 5) + (token & 15) + half * 16
    key_iota = lax.broadcasted_iota(jnp.int32, (512, 1), 0)

    def score(s, c, r):
        keys = kb[pl.ds(4 * c, 4)].reshape(512, KEYW)
        queries = qt[s, :, 256 * r : 256 * r + 256]
        return jnp.dot(keys, queries, preferred_element_type=jnp.float32)

    def chunk(s, c, blk, last):
        ahead = first[...]
        for r in range(4):
            cols = slice(256 * r, 256 * r + 256)
            scores = ahead * SCALE2
            if r < 3:
                ahead = score(s, c, r + 1)
            elif not last:
                first[...] = score(s, c + 1, 0)
            if last:
                visible = key_iota + 512 * c <= place + 256 * blk
                scores = jnp.where(visible, scores, FLOOR_SCORE)
            before = mx[s, :, cols]
            peak = jnp.maximum(before, jnp.max(scores, 0, keepdims=True))
            shrink = jnp.exp2(before - peak)
            weights = jnp.exp2(scores - peak)
            mx[s, :, cols] = peak
            tot[s, :, cols] = tot[s, :, cols] * shrink + jnp.sum(weights, 0, keepdims=True)
            mixed = jnp.dot(kt[c], weights.astype(jnp.bfloat16), preferred_element_type=jnp.float32)
            acc[s, :, cols] = acc[s, :, cols] * shrink + mixed

    def attend(s, blk):
        first[...] = score(s, 0, 0)

        def step(c, _):
            chunk(s, c, blk, False)
            return 0

        lax.fori_loop(0, blk // 2, step, 0)
        chunk(s, blk // 2, blk, True)

    def finish(s):
        def value_of(h, _):
            cols = pl.ds(pl.multiple_of(h * VH, VH), VH)
            mixed = (acc[s, :, cols] * (1.0 / tot[s, :, cols])).astype(jnp.bfloat16)
            value = jnp.dot(wvt[h], mixed, preferred_element_type=jnp.float32).T
            ob[s, :, :, cols] = value.astype(jnp.bfloat16).reshape(8, 16, VH)
            return 0

        lax.fori_loop(0, HEADS, value_of, 0)

    attend(1, mirror)
    finish(1)
    send(ob.at[1], out_h.at[:, half], out_sem.at[0], pair)
    attend(0, chain)
    finish(0)
    keep = pltpu.make_async_copy(ob.at[0], out_h.at[:, half], own_sem.at[0])
    keep.start()
    keep.wait()
    arrived(out_h.at[:, 1 - half], out_sem.at[0])
    for copy in sent:
        copy.wait_send()


def hand_over(att_h, cache_h, att_out, cache_out, att, cache, sem):
    pieces = [(cache_h, cache, cache_out)]
    for k in range(4):
        rows = pl.ds(64 * k, 64)
        pieces.append((att_h.at[rows], att.at[rows], att_out.at[rows]))
    into = [pltpu.make_async_copy(p[0], p[1], sem.at[0, k]) for k, p in enumerate(pieces)]
    out = [pltpu.make_async_copy(p[1], p[2], sem.at[1, k]) for k, p in enumerate(pieces)]
    for copy in into:
        copy.start()
    for first, second in zip(into, out):
        first.wait()
        second.start()
    for copy in out:
        copy.wait()


def per_device(tokens, w_down_q, w_down_kv, q_gain, kv_gain, w_up_q, w_absorb, w_value, slot_block):
    bf16, f32 = jnp.bfloat16, jnp.float32
    table = jnp.asarray(rotary_tables())
    hbm = pl.BlockSpec(memory_space=pl.ANY)
    dma = pltpu.SemaphoreType.DMA
    attended, cache = pl.pallas_call(
        kernel,
        out_shape=(
            jax.ShapeDtypeStruct((8, 2, 16, HEADS * VH), bf16),
            jax.ShapeDtypeStruct((2, 16, KV), bf16),
        ),
        in_specs=[hbm] * 8 + [pl.BlockSpec(memory_space=pltpu.SMEM), hbm],
        out_specs=(hbm, pl.BlockSpec(memory_space=pltpu.VMEM)),
        scratch_shapes=[
            pltpu.VMEM((256, 896), bf16),
            pltpu.VMEM((896, QL), bf16),
            pltpu.VMEM((KV, 896), bf16),
            pltpu.VMEM((QL // 128, 128), f32),
            pltpu.VMEM((LAT // 128, 128), f32),
            pltpu.VMEM((QL, HEADS * (NOPE + ROPE)), bf16),
            pltpu.VMEM((HEADS, NOPE, LAT), bf16),
            pltpu.VMEM((HEADS, LAT, VH), bf16),
            pltpu.VMEM((2, 16, 2 * ROPE), f32),
            pltpu.VMEM((2, 8, 16, 2 * ROPE), f32),
            pltpu.VMEM((128, KV), f32),
            pltpu.VMEM((128, KV), f32),
            pltpu.VMEM((128, KV), f32),
            pltpu.VMEM((128, QL), f32),
            pltpu.VMEM((128, QL), f32),
            pltpu.VMEM((128, QL), f32),
            pltpu.VMEM((6, 16, KV), bf16),
            pltpu.VMEM((6, 16, KV), bf16),
            pltpu.VMEM((6, 16, QL), f32),
            pltpu.VMEM((6, 16, QL), f32),
            pltpu.VMEM((2, 16, QL), bf16),
            pltpu.VMEM((2, 8, 16, QL), bf16),
            pltpu.VMEM((32, 128, KEYW), bf16),
            pltpu.VMEM((8, LAT, 512), bf16),
            pltpu.VMEM((2, KEYW, HEADS * 128), bf16),
            pltpu.VMEM((HEADS, LAT, NOPE), bf16),
            pltpu.VMEM((HEADS, VH, LAT), bf16),
            pltpu.VMEM((512, 256), f32),
            pltpu.VMEM((2, LAT, HEADS * 128), f32),
            pltpu.VMEM((2, 1, HEADS * 128), f32),
            pltpu.VMEM((2, 1, HEADS * 128), f32),
            pltpu.VMEM((2, 8, 16, HEADS * VH), bf16),
            dma((11,)),
            dma((N_SEND,)),
            dma((2,)),
            dma((6,)),
            dma((6,)),
            dma((2, 8)),
            dma((4,)),
            dma((16, 2)),
            dma((16,)),
            dma((1,)),
            dma((1,)),
        ],
        compiler_params=pltpu.CompilerParams(
            collective_id=0, has_side_effects=True, vmem_limit_bytes=56 * 2**20
        ),
    )(
        tokens, w_down_q, w_down_kv.T, q_gain.reshape(-1, 128), kv_gain.reshape(-1, 128),
        w_up_q, w_absorb, w_value, slot_block, table,
    )
    attended = attended.reshape(256, HEADS * VH)
    return pl.pallas_call(
        hand_over,
        out_shape=(
            jax.ShapeDtypeStruct(attended.shape, bf16),
            jax.ShapeDtypeStruct(cache.shape, bf16),
        ),
        in_specs=[hbm, hbm],
        out_specs=(hbm, hbm),
        scratch_shapes=[
            pltpu.VMEM(attended.shape, bf16),
            pltpu.VMEM(cache.shape, bf16),
            dma((2, 5)),
        ],
        compiler_params=pltpu.CompilerParams(vmem_limit_bytes=60 * 2**20),
    )(attended, cache)


def solution(mesh):
    placed = (
        P("chain", "tp"),
        P("tp", None),
        P("tp", None),
        P(),
        P(),
        P(None, "tp"),
        P("tp", None, None),
        P("tp", None, None),
        P("chain"),
    )
    return jax.shard_map(
        per_device,
        mesh=mesh,
        in_specs=placed,
        out_specs=(P("chain", "tp"), P("chain", "tp", None)),
        check_vma=False,
    )
```

```python
import functools
import math

import jax
import jax.numpy as jnp
import numpy as np
from jax import lax
from jax.experimental import pallas as pl
from jax.experimental.pallas import tpu as pltpu
from jax.sharding import PartitionSpec as P

MESH = pl.DeviceIdType.MESH
ROPE_BASE = 50000.0
FLOOR_SCORE = -1e30
QL, LAT, ROPE, NOPE, VH, HEADS = 1536, 512, 64, 128, 128, 8
SUMMED = LAT + 16
KEYW = 640
KV = LAT + ROPE
SCALE2 = (NOPE + ROPE) ** -0.5 * math.log2(math.e)
NT = (((1,), (1,)), ((), ()))
N_SEND = 80
RINGS = (
    (0, 0), (3, 0), (1, 0), (0, 3), (0, 1), (2, 0), (3, 3), (3, 1), (1, 3), (1, 1), (0, 2),
    (2, 3), (2, 1), (3, 2), (1, 2), (2, 2),
)


def rotary_tables():
    inverse = ROPE_BASE ** (-2.0 * np.arange(ROPE // 2) / ROPE)
    angles = np.arange(4096)[:, None] * inverse[None, :]
    cosine = np.concatenate([np.cos(angles), np.cos(angles)], 1)
    sine = np.concatenate([-np.sin(angles), np.sin(angles)], 1)
    both = np.concatenate([cosine, sine], 1).astype(np.float32)
    return both.reshape(16, 8, 2, 16, 2 * ROPE)


def rotate(values, table):
    half = ROPE // 2
    swapped = jnp.concatenate([values[:, half:], values[:, :half]], 1)
    return values * table[:, :ROPE] + swapped * table[:, ROPE:]


def normalize(values, gain):
    return values * lax.rsqrt(jnp.mean(values * values, -1, keepdims=True) + 1e-06) * gain


def kernel(
    tok_h, wq_h, wkv_h, qg_h, kvg_h, wu_h, wa_h, wv_h, slot_ref, tab_h,
    out_h, cache_ref,
    tok, wq, wkv, qg, kvg, wu, wa, wv, tabk, tabq,
    psk, pok, prk, psq, poq, prq, rks, rkr, rqs, rqr, cs, cq, kb, kt, qt, wat, wvt, first, acc, mx, ob,
    load_sem, send_sem, sib_sem, rk_sem, rq_sem, cq_sem, ky_sem, kp_sem, ks_sem, out_sem, own_sem,
):
    chain = lax.axis_index("chain")
    tp = lax.axis_index("tp")
    z, x = chain // 4, chain % 4
    y, core = tp // 2, tp % 2
    other = 1 - core
    mirror = 15 - chain
    half = chain // 8
    piece = core * 4 + y
    yp, ym, yf = (y + 1) % 4, (y + 3) % 4, (y + 2) % 4
    sibling = {"chain": chain, "tp": 2 * y + other}
    up = {"chain": chain, "tp": 2 * yp + core}
    down = {"chain": chain, "tp": 2 * ym + core}
    pair = {"chain": mirror, "tp": tp}
    a = x + core * (z - x)
    b = z + core * (x - z)
    stride_a, stride_b = 1 + 3 * core, 4 - 3 * core

    def at(da, db):
        return ((a + da) % 4) * stride_a + ((b + db) % 4) * stride_b

    ap = {"chain": at(1, 0), "tp": tp}
    am = {"chain": at(3, 0), "tp": tp}
    bp = {"chain": at(0, 1), "tp": tp}
    bm = {"chain": at(0, 3), "tp": tp}

    loads = {}
    for k, (name, src, dst) in enumerate(
        [
            ("tok", tok_h, tok), ("wkv", wkv_h, wkv), ("wq", wq_h, wq), ("kvg", kvg_h, kvg),
            ("qg", qg_h, qg), ("tabk", tab_h.at[chain, piece], tabk), ("wa", wa_h, wa),
            ("wu", wu_h, wu), ("wv", wv_h, wv), ("tab0", tab_h.at[chain, :, half], tabq.at[0]),
            ("tab1", tab_h.at[mirror, :, half], tabq.at[1]),
        ]
    ):
        loads[name] = pltpu.make_async_copy(src, dst, load_sem.at[k])
        if k < 6:
            loads[name].start()

    def loaded(*names):
        for name in names:
            loads[name].wait()

    barrier = pltpu.get_barrier_semaphore()
    partners = (sibling, up, down, pair, ap, am, bp, bm)
    for device in partners:
        pl.semaphore_signal(barrier, inc=1, device_id=device, device_id_type=MESH)
    pl.semaphore_wait(barrier, len(partners))

    sent = []

    def send(src, dst, recv, device):
        copy = pltpu.make_async_remote_copy(
            src_ref=src, dst_ref=dst, send_sem=send_sem.at[len(sent)], recv_sem=recv,
            device_id=device, device_id_type=MESH,
        )
        copy.start()
        sent.append(copy)

    def arrived(dst, recv):
        pltpu.make_async_remote_copy(
            src_ref=dst, dst_ref=dst, send_sem=send_sem.at[0], recv_sem=recv,
            device_id=sibling, device_id_type=MESH,
        ).wait_recv()

    def rows_of(c):
        return tok[pl.ds(pl.multiple_of(c * 128, 128), 128), :]

    def project_keys(c, dst):
        dst[...] = lax.dot_general(rows_of(c), wkv[...], NT, preferred_element_type=jnp.float32)

    def project_queries(c, dst):
        left = rows_of(c)

        def tile(i, _):
            cols = pl.ds(pl.multiple_of(i * 512, 512), 512)
            dst[:, cols] = jnp.dot(left, wq[:, cols], preferred_element_type=jnp.float32)
            return 0

        lax.fori_loop(0, 3, tile, 0)

    def ring_of(own, got, out, came, sems):
        def part(yy, h):
            rows = pl.ds(pl.multiple_of(yy * 32 + h * 16, 16), 16)
            return own[rows, :] + got[rows, :]

        def push(k, value, device):
            out[k] = value.astype(out.dtype)
            send(out.at[k], came.at[k], sems.at[k], device)

        def start():
            push(0, part(yf, 0), up)
            push(1, part(yf, 1), down)
            push(2, part(yp, 1), up)
            push(3, part(ym, 0), down)

        def middle():
            arrived(came.at[0], sems.at[0])
            push(4, part(yp, 0) + came[0].astype(jnp.float32), up)
            arrived(came.at[1], sems.at[1])
            push(5, part(ym, 1) + came[1].astype(jnp.float32), down)

        def end():
            for k in (2, 3, 4, 5):
                arrived(came.at[k], sems.at[k])
            totals = []
            for h, first, second in ((0, 4, 3), (1, 2, 5)):
                total = part(y, h) + came[first].astype(jnp.float32)
                totals.append(total + came[second].astype(jnp.float32))
            return totals

        return start, middle, end

    keys_start, keys_middle, keys_end = ring_of(pok, prk, rks, rkr, rk_sem)
    queries_start, queries_middle, queries_end = ring_of(poq, prq, rqs, rqr, rq_sem)

    loaded("tok", "wkv")
    project_keys(other, psk)
    send(psk, prk, sib_sem.at[0], sibling)
    project_keys(core, pok)
    loaded("wq")
    for name in ("wa", "wu", "wv", "tab0", "tab1"):
        loads[name].start()
    project_queries(other, psq)
    send(psq, prq, sib_sem.at[1], sibling)
    arrived(prk, sib_sem.at[0])
    keys_start()
    project_queries(core, poq)
    keys_middle()
    arrived(prq, sib_sem.at[1])
    queries_start()

    loaded("wa")

    def turn_absorb(h, _):
        wat[h] = wa[h].T
        return 0

    lax.fori_loop(0, HEADS, turn_absorb, 0)

    slot_own = 2 * chain + core

    def keys_y(yy, h, n):
        return kb.at[slot_own, pl.ds(pl.multiple_of(yy * 32 + h * 16, 16), n)]

    loaded("kvg", "tabk")
    gain_kv = jnp.concatenate([kvg[k : k + 1, :] for k in range(LAT // 128)], 1)
    for h, total in enumerate(keys_end()):
        latent = normalize(total[:, :LAT], gain_kv)
        turned = rotate(total[:, LAT:], tabk[h])
        rows = pl.ds(pl.multiple_of(y * 32 + h * 16, 16), 16)
        kb[slot_own, rows, :LAT] = latent.astype(jnp.bfloat16)
        kb[slot_own, rows, LAT:] = jnp.concatenate(
            [turned, jnp.zeros_like(turned)], 1
        ).astype(jnp.bfloat16)
    for k, device in enumerate((up, down)):
        send(keys_y(y, 0, 32), keys_y(y, 0, 32), ky_sem.at[k], device)
    queries_middle()
    arrived(keys_y(ym, 0, 32), ky_sem.at[0])
    send(keys_y(ym, 0, 16), keys_y(ym, 0, 16), ky_sem.at[2], up)
    arrived(keys_y(yp, 0, 32), ky_sem.at[1])
    send(keys_y(yp, 1, 16), keys_y(yp, 1, 16), ky_sem.at[3], down)

    def block(n, p=None):
        if p is None:
            return kb.at[2 * n + core]
        return kb.at[2 * n + core, pl.ds(64 * p, 64)]

    def pass_on(n, *devices):
        for device in devices:
            send(block(n), block(n), kp_sem.at[n, 0], device)
        send(block(n), block(n), ks_sem.at[n], sibling)

    def pass_part(n, p, device):
        send(block(n, p), block(n, p), kp_sem.at[n, p], device)

    def turn(n, side):
        cols = pl.ds(pl.multiple_of((n % 4) * 256 + side * 128, 128), 128)
        kt[n // 4, :LAT, cols] = kb[2 * n + side, :, :LAT].T

    def turn_own(steps):
        for u, v in steps:
            turn(at(u, v), core)

    def turn_other(steps):
        for u, v in steps:
            n = at(u, v)
            arrived(kb.at[2 * n + other], ks_sem.at[n])
            turn(n, other)

    def whole(n):
        arrived(block(n), kp_sem.at[n, 0])

    def halves(n):
        for p in range(2):
            arrived(block(n, p), kp_sem.at[n, p])

    def relay(u, v):
        n = at(u, v)
        if v == 2 or (u, v) == (2, 0):
            halves(n)
        else:
            whole(n)
        if v == 0:
            if u != 2:
                pass_part(n, 0 if u == 3 else 1, ap if u == 3 else am)
            pass_on(n, bp, bm)
        else:
            if v != 2:
                pass_part(n, 0 if v == 3 else 1, bp if v == 3 else bm)
            pass_on(n)

    arrived(keys_y(yf, 0, 16), ky_sem.at[2])
    arrived(keys_y(yf, 1, 16), ky_sem.at[3])
    pass_on(at(0, 0), ap, am, bp, bm)
    turn_own(RINGS[:1])

    loaded("qg")
    gain_q = jnp.concatenate([qg[k : k + 1, :] for k in range(QL // 128)], 1)
    for h, total in enumerate(queries_end()):
        cs[h] = normalize(total, gain_q).astype(jnp.bfloat16)

    def give(s, p, *devices):
        for device in devices:
            send(cq.at[s, p], cq.at[s, p], cq_sem.at[s, p], device)

    def take(s, p):
        arrived(cq.at[s, p], cq_sem.at[s, p])

    send(cs.at[1 - half], cq.at[1, piece], cq_sem.at[1, piece], pair)
    cq[0, piece] = cs[half]
    give(0, piece, up, down, sibling)
    pm, pp, pf = core * 4 + ym, core * 4 + yp, core * 4 + yf
    for u, v in RINGS[1:5]:
        relay(u, v)
    take(1, piece)
    give(1, piece, up, down, sibling)
    turn_own(RINGS[1:5])
    turn_other(RINGS[:1])
    take(0, pm)
    give(0, pm, up, sibling)
    take(0, pp)
    give(0, pp, sibling)
    take(1, pp)
    give(1, pp, down, sibling)
    take(1, pm)
    give(1, pm, sibling)
    for u, v in RINGS[5:11]:
        relay(u, v)
    turn_other(RINGS[1:5])
    loaded("wv")

    def turn_value(h, _):
        wvt[h] = wv[h].T
        return 0

    lax.fori_loop(0, HEADS, turn_value, 0)
    take(0, pf)
    give(0, pf, sibling)
    take(1, pf)
    give(1, pf, sibling)
    for s in range(2):
        for yy in range(4):
            take(s, other * 4 + yy)

    loaded("wu", "tab0", "tab1")

    def expand(i, _):
        cols = pl.ds(pl.multiple_of(i * 384, 384), 384)
        rows = cq[...].reshape(256, QL)
        projected = jnp.dot(rows, wu[:, cols], preferred_element_type=jnp.float32)
        table = tabq[...].reshape(256, 2 * ROPE)
        for j in range(2):
            head = 2 * i + j
            base = j * (NOPE + ROPE)
            nope = projected[:, base : base + NOPE].astype(jnp.bfloat16)
            turned = rotate(projected[:, base + NOPE : base + NOPE + ROPE], table)
            turned = jnp.concatenate([turned, jnp.zeros_like(turned)], 1).astype(jnp.bfloat16).T
            absorbed = jnp.dot(wat[head], nope.T, preferred_element_type=jnp.float32)
            absorbed = absorbed.astype(jnp.bfloat16)
            places = pl.ds(pl.multiple_of(head * 128, 128), 128)
            for s in range(2):
                qt[s, :LAT, places] = absorbed[:, s * 128 : s * 128 + 128]
                qt[s, LAT:, places] = turned[:, s * 128 : s * 128 + 128]
        return 0

    expand(0, 0)
    turn_own(RINGS[5:11])
    expand(1, 0)
    for u, v in RINGS[11:15]:
        relay(u, v)
    expand(2, 0)
    turn_own(RINGS[11:15])
    for u, v in RINGS[5:11]:
        arrived(kb.at[2 * at(u, v) + other], ks_sem.at[at(u, v)])
    expand(3, 0)
    for u, v in RINGS[5:11]:
        turn(at(u, v), other)
    acc[...] = jnp.zeros_like(acc)
    kt[:, LAT:, :] = jnp.ones((4, SUMMED - LAT, 1024), jnp.bfloat16)
    mx[...] = jnp.full_like(mx, FLOOR_SCORE)

    def turn(n, side):
        cols = pl.ds(pl.multiple_of((n % 4) * 256 + side * 128, 128), 128)
        kt[n // 4, :LAT, cols] = kb[2 * n + side, :, :LAT].T

    def turn_own(steps):
        for u, v in steps:
            turn(at(u, v), core)

    def turn_other(steps):
        for u, v in steps:
            n = at(u, v)
            arrived(kb.at[2 * n + other], ks_sem.at[n])
            turn(n, other)

    def whole(n):
        arrived(block(n), kp_sem.at[n, 0])

    def halves(n):
        for p in range(2):
            arrived(block(n, p), kp_sem.at[n, p])

    relay(2, 2)
    turn_own(RINGS[15:])
    turn_other(RINGS[11:])
    for j in range(2):
        rows = pl.ds(pl.multiple_of(tp * 16, 16), 16)
        cache_ref[j] = kb[slot_ref[j], rows, :][:, :KV]

    token = lax.broadcasted_iota(jnp.int32, (1, 256), 1) & 127
    place = ((token >> 4) << 5) + (token & 15) + half * 16
    key_iota = lax.broadcasted_iota(jnp.int32, (1024, 1), 0)

    def score(s, c, r, size):
        keys = kb[pl.ds(8 * c, size // 128)].reshape(size, KEYW)
        queries = qt[s, :, 256 * r : 256 * r + 256]
        return jnp.dot(keys, queries, preferred_element_type=jnp.float32)

    def chunk(s, c, blk, size, last):
        ahead = first[:size, :]
        for r in range(4):
            cols = slice(256 * r, 256 * r + 256)
            scores = ahead * SCALE2
            if r < 3:
                ahead = score(s, c, r + 1, size)
            elif not last:
                first[...] = score(s, c + 1, 0, size)
            if last:
                visible = key_iota[:size] + 1024 * c <= place + 256 * blk
                scores = jnp.where(visible, scores, FLOOR_SCORE)
            before = mx[s, :, cols]
            peak = jnp.maximum(before, jnp.max(scores, 0, keepdims=True))
            shrink = jnp.exp2(before - peak)
            weights = jnp.exp2(scores - peak).astype(jnp.bfloat16)
            mx[s, :, cols] = peak
            mixed = jnp.dot(kt[c, :, :size], weights, preferred_element_type=jnp.float32)
            acc[s, :, cols] = acc[s, :, cols] * shrink + mixed

    def attend(s, blk):
        first[...] = score(s, 0, 0, 1024)

        def step(c, _):
            chunk(s, c, blk, 1024, False)
            return 0

        lax.fori_loop(0, blk // 4, step, 0)

        @pl.when(blk % 4 >= 2)
        def _():
            chunk(s, blk // 4, blk, 1024, True)

        @pl.when(blk % 4 < 2)
        def _():
            chunk(s, blk // 4, blk, 512, True)

    def finish(s):
        def value_of(h, _):
            cols = pl.ds(pl.multiple_of(h * VH, VH), VH)
            mixed = acc[s, :LAT, cols] * (1.0 / acc[s, LAT : LAT + 1, cols])
            mixed = mixed.astype(jnp.bfloat16)
            value = jnp.dot(wvt[h], mixed, preferred_element_type=jnp.float32).T
            ob[s, :, :, cols] = value.astype(jnp.bfloat16).reshape(8, 16, VH)
            return 0

        lax.fori_loop(0, HEADS, value_of, 0)

    attend(1, mirror)
    finish(1)
    send(ob.at[1], out_h.at[:, half], out_sem.at[0], pair)
    attend(0, chain)
    finish(0)
    keep = pltpu.make_async_copy(ob.at[0], out_h.at[:, half], own_sem.at[0])
    keep.start()
    keep.wait()
    arrived(out_h.at[:, 1 - half], out_sem.at[0])
    for copy in sent:
        copy.wait_send()


def hand_over(att_h, cache_h, att_out, cache_out, att, cache, sem):
    pieces = [(cache_h, cache, cache_out)]
    for k in range(4):
        rows = pl.ds(64 * k, 64)
        pieces.append((att_h.at[rows], att.at[rows], att_out.at[rows]))
    into = [pltpu.make_async_copy(p[0], p[1], sem.at[0, k]) for k, p in enumerate(pieces)]
    out = [pltpu.make_async_copy(p[1], p[2], sem.at[1, k]) for k, p in enumerate(pieces)]
    for copy in into:
        copy.start()
    for first, second in zip(into, out):
        first.wait()
        second.start()
    for copy in out:
        copy.wait()


def per_device(tokens, w_down_q, w_down_kv, q_gain, kv_gain, w_up_q, w_absorb, w_value, slot_block):
    bf16, f32 = jnp.bfloat16, jnp.float32
    table = jnp.asarray(rotary_tables())
    hbm = pl.BlockSpec(memory_space=pl.ANY)
    dma = pltpu.SemaphoreType.DMA
    attended, cache = pl.pallas_call(
        kernel,
        out_shape=(
            jax.ShapeDtypeStruct((8, 2, 16, HEADS * VH), bf16),
            jax.ShapeDtypeStruct((2, 16, KV), bf16),
        ),
        in_specs=[hbm] * 8 + [pl.BlockSpec(memory_space=pltpu.SMEM), hbm],
        out_specs=(hbm, pl.BlockSpec(memory_space=pltpu.VMEM)),
        scratch_shapes=[
            pltpu.VMEM((256, 896), bf16),
            pltpu.VMEM((896, QL), bf16),
            pltpu.VMEM((KV, 896), bf16),
            pltpu.VMEM((QL // 128, 128), f32),
            pltpu.VMEM((LAT // 128, 128), f32),
            pltpu.VMEM((QL, HEADS * (NOPE + ROPE)), bf16),
            pltpu.VMEM((HEADS, NOPE, LAT), bf16),
            pltpu.VMEM((HEADS, LAT, VH), bf16),
            pltpu.VMEM((2, 16, 2 * ROPE), f32),
            pltpu.VMEM((2, 8, 16, 2 * ROPE), f32),
            pltpu.VMEM((128, KV), f32),
            pltpu.VMEM((128, KV), f32),
            pltpu.VMEM((128, KV), f32),
            pltpu.VMEM((128, QL), f32),
            pltpu.VMEM((128, QL), f32),
            pltpu.VMEM((128, QL), f32),
            pltpu.VMEM((6, 16, KV), bf16),
            pltpu.VMEM((6, 16, KV), bf16),
            pltpu.VMEM((6, 16, QL), f32),
            pltpu.VMEM((6, 16, QL), f32),
            pltpu.VMEM((2, 16, QL), bf16),
            pltpu.VMEM((2, 8, 16, QL), bf16),
            pltpu.VMEM((32, 128, KEYW), bf16),
            pltpu.VMEM((4, SUMMED, 1024), bf16),
            pltpu.VMEM((2, KEYW, HEADS * 128), bf16),
            pltpu.VMEM((HEADS, LAT, NOPE), bf16),
            pltpu.VMEM((HEADS, VH, LAT), bf16),
            pltpu.VMEM((1024, 256), f32),
            pltpu.VMEM((2, SUMMED, HEADS * 128), f32),
            pltpu.VMEM((2, 1, HEADS * 128), f32),
            pltpu.VMEM((2, 8, 16, HEADS * VH), bf16),
            dma((11,)),
            dma((N_SEND,)),
            dma((2,)),
            dma((6,)),
            dma((6,)),
            dma((2, 8)),
            dma((4,)),
            dma((16, 2)),
            dma((16,)),
            dma((1,)),
            dma((1,)),
        ],
        compiler_params=pltpu.CompilerParams(
            collective_id=0, has_side_effects=True, vmem_limit_bytes=56 * 2**20
        ),
    )(
        tokens, w_down_q, w_down_kv.T, q_gain.reshape(-1, 128), kv_gain.reshape(-1, 128),
        w_up_q, w_absorb, w_value, slot_block, table,
    )
    attended = attended.reshape(256, HEADS * VH)
    return pl.pallas_call(
        hand_over,
        out_shape=(
            jax.ShapeDtypeStruct(attended.shape, bf16),
            jax.ShapeDtypeStruct(cache.shape, bf16),
        ),
        in_specs=[hbm, hbm],
        out_specs=(hbm, hbm),
        scratch_shapes=[
            pltpu.VMEM(attended.shape, bf16),
            pltpu.VMEM(cache.shape, bf16),
            dma((2, 5)),
        ],
        compiler_params=pltpu.CompilerParams(vmem_limit_bytes=60 * 2**20),
    )(attended, cache)


def solution(mesh):
    placed = (
        P("chain", "tp"),
        P("tp", None),
        P("tp", None),
        P(),
        P(),
        P(None, "tp"),
        P("tp", None, None),
        P("tp", None, None),
        P("chain"),
    )
    return jax.shard_map(
        per_device,
        mesh=mesh,
        in_specs=placed,
        out_specs=(P("chain", "tp"), P("chain", "tp", None)),
        check_vma=False,
    )
```

```python
import functools
import math

import jax
import jax.numpy as jnp
import numpy as np
from jax import lax
from jax.experimental import pallas as pl
from jax.experimental.pallas import tpu as pltpu
from jax.sharding import PartitionSpec as P

MESH = pl.DeviceIdType.MESH
ROPE_BASE = 50000.0
FLOOR_SCORE = -1e30
QL, LAT, ROPE, NOPE, VH, HEADS = 1536, 512, 64, 128, 128, 8
KEYW = 640
KV = LAT + ROPE
SCALE2 = (NOPE + ROPE) ** -0.5 * math.log2(math.e)
NT = (((1,), (1,)), ((), ()))
N_SEND = 80
RINGS = (
    (0, 0), (3, 0), (1, 0), (0, 3), (0, 1), (2, 0), (3, 3), (3, 1), (1, 3), (1, 1), (0, 2),
    (2, 3), (2, 1), (3, 2), (1, 2), (2, 2),
)


def rotary_tables():
    inverse = ROPE_BASE ** (-2.0 * np.arange(ROPE // 2) / ROPE)
    angles = np.arange(4096)[:, None] * inverse[None, :]
    cosine = np.concatenate([np.cos(angles), np.cos(angles)], 1)
    sine = np.concatenate([-np.sin(angles), np.sin(angles)], 1)
    both = np.concatenate([cosine, sine], 1).astype(np.float32)
    return both.reshape(16, 8, 2, 16, 2 * ROPE)


def rotate(values, table):
    half = ROPE // 2
    swapped = jnp.concatenate([values[:, half:], values[:, :half]], 1)
    return values * table[:, :ROPE] + swapped * table[:, ROPE:]


def normalize(values, gain):
    return values * lax.rsqrt(jnp.mean(values * values, -1, keepdims=True) + 1e-06) * gain


def kernel(
    tok_h, wq_h, wkv_h, qg_h, kvg_h, wu_h, wa_h, wv_h, slot_ref, tab_h,
    out_h, cache_ref,
    tok, wq, wkv, qg, kvg, wu, wa, wv, tabk, tabq,
    psk, pok, prk, psq, poq, prq, rks, rkr, rqs, rqr, cs, cq, kb, qb, first, acc, mx, tot, ob,
    load_sem, send_sem, sib_sem, rk_sem, rq_sem, cq_sem, ky_sem, kp_sem, ks_sem, out_sem, own_sem,
):
    chain = lax.axis_index("chain")
    tp = lax.axis_index("tp")
    z, x = chain // 4, chain % 4
    y, core = tp // 2, tp % 2
    other = 1 - core
    mirror = 15 - chain
    half = chain // 8
    piece = core * 4 + y
    yp, ym, yf = (y + 1) % 4, (y + 3) % 4, (y + 2) % 4
    sibling = {"chain": chain, "tp": 2 * y + other}
    up = {"chain": chain, "tp": 2 * yp + core}
    down = {"chain": chain, "tp": 2 * ym + core}
    pair = {"chain": mirror, "tp": tp}
    a = x + core * (z - x)
    b = z + core * (x - z)
    stride_a, stride_b = 1 + 3 * core, 4 - 3 * core

    def at(da, db):
        return ((a + da) % 4) * stride_a + ((b + db) % 4) * stride_b

    ap = {"chain": at(1, 0), "tp": tp}
    am = {"chain": at(3, 0), "tp": tp}
    bp = {"chain": at(0, 1), "tp": tp}
    bm = {"chain": at(0, 3), "tp": tp}

    loads = {}
    for k, (name, src, dst) in enumerate(
        [
            ("tok", tok_h, tok), ("wkv", wkv_h, wkv), ("wq", wq_h, wq), ("kvg", kvg_h, kvg),
            ("qg", qg_h, qg), ("tabk", tab_h.at[chain, piece], tabk), ("wa", wa_h, wa),
            ("wu", wu_h, wu), ("wv", wv_h, wv), ("tab0", tab_h.at[chain, :, half], tabq.at[0]),
            ("tab1", tab_h.at[mirror, :, half], tabq.at[1]),
        ]
    ):
        loads[name] = pltpu.make_async_copy(src, dst, load_sem.at[k])
        if k < 6:
            loads[name].start()

    def loaded(*names):
        for name in names:
            loads[name].wait()

    barrier = pltpu.get_barrier_semaphore()
    partners = (sibling, up, down, pair, ap, am, bp, bm)
    for device in partners:
        pl.semaphore_signal(barrier, inc=1, device_id=device, device_id_type=MESH)
    pl.semaphore_wait(barrier, len(partners))

    sent = []

    def send(src, dst, recv, device):
        copy = pltpu.make_async_remote_copy(
            src_ref=src, dst_ref=dst, send_sem=send_sem.at[len(sent)], recv_sem=recv,
            device_id=device, device_id_type=MESH,
        )
        copy.start()
        sent.append(copy)

    def arrived(dst, recv):
        pltpu.make_async_remote_copy(
            src_ref=dst, dst_ref=dst, send_sem=send_sem.at[0], recv_sem=recv,
            device_id=sibling, device_id_type=MESH,
        ).wait_recv()

    def rows_of(c):
        return tok[pl.ds(pl.multiple_of(c * 128, 128), 128), :]

    def project_keys(c, dst):
        dst[...] = lax.dot_general(rows_of(c), wkv[...], NT, preferred_element_type=jnp.float32)

    def project_queries(c, dst):
        left = rows_of(c)

        def tile(i, _):
            cols = pl.ds(pl.multiple_of(i * 512, 512), 512)
            dst[:, cols] = jnp.dot(left, wq[:, cols], preferred_element_type=jnp.float32)
            return 0

        lax.fori_loop(0, 3, tile, 0)

    def ring_of(own, got, out, came, sems):
        def part(yy, h):
            rows = pl.ds(pl.multiple_of(yy * 32 + h * 16, 16), 16)
            return own[rows, :] + got[rows, :]

        def push(k, value, device):
            out[k] = value.astype(out.dtype)
            send(out.at[k], came.at[k], sems.at[k], device)

        def start():
            push(0, part(yf, 0), up)
            push(1, part(yf, 1), down)
            push(2, part(yp, 1), up)
            push(3, part(ym, 0), down)

        def middle():
            arrived(came.at[0], sems.at[0])
            push(4, part(yp, 0) + came[0].astype(jnp.float32), up)
            arrived(came.at[1], sems.at[1])
            push(5, part(ym, 1) + came[1].astype(jnp.float32), down)

        def end():
            for k in (2, 3, 4, 5):
                arrived(came.at[k], sems.at[k])
            totals = []
            for h, first, second in ((0, 4, 3), (1, 2, 5)):
                total = part(y, h) + came[first].astype(jnp.float32)
                totals.append(total + came[second].astype(jnp.float32))
            return totals

        return start, middle, end

    keys_start, keys_middle, keys_end = ring_of(pok, prk, rks, rkr, rk_sem)
    queries_start, queries_middle, queries_end = ring_of(poq, prq, rqs, rqr, rq_sem)

    loaded("tok", "wkv")
    project_keys(other, psk)
    send(psk, prk, sib_sem.at[0], sibling)
    project_keys(core, pok)
    loaded("wq")
    for name in ("wa", "wu", "wv", "tab0", "tab1"):
        loads[name].start()
    project_queries(other, psq)
    send(psq, prq, sib_sem.at[1], sibling)
    arrived(prk, sib_sem.at[0])
    keys_start()
    project_queries(core, poq)
    keys_middle()
    arrived(prq, sib_sem.at[1])
    queries_start()

    slot_own = 2 * chain + core

    def keys_y(yy, h, n):
        return kb.at[slot_own, pl.ds(pl.multiple_of(yy * 32 + h * 16, 16), n)]

    loaded("kvg", "tabk")
    gain_kv = jnp.concatenate([kvg[k : k + 1, :] for k in range(LAT // 128)], 1)
    for h, total in enumerate(keys_end()):
        latent = normalize(total[:, :LAT], gain_kv)
        turned = rotate(total[:, LAT:], tabk[h])
        rows = pl.ds(pl.multiple_of(y * 32 + h * 16, 16), 16)
        kb[slot_own, rows, :LAT] = latent.astype(jnp.bfloat16)
        kb[slot_own, rows, LAT:] = jnp.concatenate(
            [turned, jnp.zeros_like(turned)], 1
        ).astype(jnp.bfloat16)
    for k, device in enumerate((up, down)):
        send(keys_y(y, 0, 32), keys_y(y, 0, 32), ky_sem.at[k], device)
    queries_middle()
    arrived(keys_y(ym, 0, 32), ky_sem.at[0])
    send(keys_y(ym, 0, 16), keys_y(ym, 0, 16), ky_sem.at[2], up)
    arrived(keys_y(yp, 0, 32), ky_sem.at[1])
    send(keys_y(yp, 1, 16), keys_y(yp, 1, 16), ky_sem.at[3], down)

    def block(n, p=None):
        if p is None:
            return kb.at[2 * n + core]
        return kb.at[2 * n + core, pl.ds(64 * p, 64)]

    def pass_on(n, *devices):
        for device in devices:
            send(block(n), block(n), kp_sem.at[n, 0], device)
        send(block(n), block(n), ks_sem.at[n], sibling)

    def pass_part(n, p, device):
        send(block(n, p), block(n, p), kp_sem.at[n, p], device)

    def whole(n):
        arrived(block(n), kp_sem.at[n, 0])

    def halves(n):
        for p in range(2):
            arrived(block(n, p), kp_sem.at[n, p])

    def relay(u, v):
        n = at(u, v)
        if v == 2 or (u, v) == (2, 0):
            halves(n)
        else:
            whole(n)
        if v == 0:
            if u != 2:
                pass_part(n, 0 if u == 3 else 1, ap if u == 3 else am)
            pass_on(n, bp, bm)
        else:
            if v != 2:
                pass_part(n, 0 if v == 3 else 1, bp if v == 3 else bm)
            pass_on(n)

    arrived(keys_y(yf, 0, 16), ky_sem.at[2])
    arrived(keys_y(yf, 1, 16), ky_sem.at[3])
    pass_on(at(0, 0), ap, am, bp, bm)

    loaded("qg")
    gain_q = jnp.concatenate([qg[k : k + 1, :] for k in range(QL // 128)], 1)
    for h, total in enumerate(queries_end()):
        cs[h] = normalize(total, gain_q).astype(jnp.bfloat16)

    def give(s, p, *devices):
        for device in devices:
            send(cq.at[s, p], cq.at[s, p], cq_sem.at[s, p], device)

    def take(s, p):
        arrived(cq.at[s, p], cq_sem.at[s, p])

    send(cs.at[1 - half], cq.at[1, piece], cq_sem.at[1, piece], pair)
    cq[0, piece] = cs[half]
    give(0, piece, up, down, sibling)
    pm, pp, pf = core * 4 + ym, core * 4 + yp, core * 4 + yf
    for u, v in RINGS[1:5]:
        relay(u, v)
    take(1, piece)
    give(1, piece, up, down, sibling)
    take(0, pm)
    give(0, pm, up, sibling)
    take(0, pp)
    give(0, pp, sibling)
    take(1, pp)
    give(1, pp, down, sibling)
    take(1, pm)
    give(1, pm, sibling)
    for u, v in RINGS[5:11]:
        relay(u, v)
    take(0, pf)
    give(0, pf, sibling)
    take(1, pf)
    give(1, pf, sibling)
    for s in range(2):
        for yy in range(4):
            take(s, other * 4 + yy)

    loaded("wa", "wu", "tab0", "tab1")

    def expand(i, _):
        cols = pl.ds(pl.multiple_of(i * 384, 384), 384)
        rows = cq[...].reshape(256, QL)
        projected = jnp.dot(rows, wu[:, cols], preferred_element_type=jnp.float32)
        table = tabq[...].reshape(256, 2 * ROPE)
        for j in range(2):
            head = 2 * i + j
            base = j * (NOPE + ROPE)
            nope = projected[:, base : base + NOPE].astype(jnp.bfloat16)
            turned = rotate(projected[:, base + NOPE : base + NOPE + ROPE], table)
            turned = jnp.concatenate([turned, jnp.zeros_like(turned)], 1).astype(jnp.bfloat16)
            absorbed = jnp.dot(nope, wa[head], preferred_element_type=jnp.float32)
            absorbed = absorbed.astype(jnp.bfloat16)
            places = pl.ds(pl.multiple_of(head * 128, 128), 128)
            for s in range(2):
                qb[s, places, :LAT] = absorbed[s * 128 : s * 128 + 128]
                qb[s, places, LAT:] = turned[s * 128 : s * 128 + 128]
        return 0

    lax.fori_loop(0, HEADS // 4, expand, 0)
    for u, v in RINGS[11:15]:
        relay(u, v)
    lax.fori_loop(HEADS // 4, HEADS // 2, expand, 0)
    acc[...] = jnp.zeros_like(acc)
    tot[...] = jnp.zeros_like(tot)
    mx[...] = jnp.full_like(mx, FLOOR_SCORE)

    def turn(n, side):
        cols = pl.ds(pl.multiple_of((n % 4) * 256 + side * 128, 128), 128)
        kt[n // 4, :LAT, cols] = kb[2 * n + side, :, :LAT].T

    def turn_own(steps):
        for u, v in steps:
            turn(at(u, v), core)

    def turn_other(steps):
        for u, v in steps:
            n = at(u, v)
            arrived(kb.at[2 * n + other], ks_sem.at[n])
            turn(n, other)

    def whole(n):
        arrived(block(n), kp_sem.at[n, 0])

    def halves(n):
        for p in range(2):
            arrived(block(n, p), kp_sem.at[n, p])

    relay(2, 2)
    for n in range(16):
        arrived(kb.at[2 * n + other], ks_sem.at[n])
    for j in range(2):
        rows = pl.ds(pl.multiple_of(tp * 16, 16), 16)
        cache_ref[j] = kb[slot_ref[j], rows, :][:, :KV]

    token = lax.broadcasted_iota(jnp.int32, (512, 1), 0) & 127
    place = ((token >> 4) << 5) + (token & 15) + half * 16
    key_iota = lax.broadcasted_iota(jnp.int32, (1, 1024), 1)

    def score(s, c, r, size):
        keys = kb[pl.ds(8 * c, size // 128)].reshape(size, KEYW)
        queries = qb[s, 512 * r : 512 * r + 512, :]
        return lax.dot_general(queries, keys, NT, preferred_element_type=jnp.float32)

    def chunk(s, c, blk, size, last):
        ahead = first[:, :size]
        for r in range(2):
            rows = slice(512 * r, 512 * r + 512)
            scores = ahead * SCALE2
            if r < 1:
                ahead = score(s, c, r + 1, size)
            elif not last:
                first[...] = score(s, c + 1, 0, size)
            if last:
                visible = key_iota[:, :size] + 1024 * c <= place + 256 * blk
                scores = jnp.where(visible, scores, FLOOR_SCORE)
            parts = [scores[:, k : k + 128] for k in range(0, size, 128)]
            before = mx[s, rows, :]
            top = jnp.max(functools.reduce(jnp.maximum, parts), 1, keepdims=True)
            peak = jnp.maximum(before, top)
            shrink = jnp.exp2(before - peak)
            weights = [jnp.exp2(p - peak) for p in parts]
            mx[s, rows, :] = peak
            tot[s, rows, :] = tot[s, rows, :] * shrink + sum(weights[1:], weights[0])
            weights = jnp.concatenate([w.astype(jnp.bfloat16) for w in weights], 1)
            latent = kb[pl.ds(8 * c, size // 128), :, :LAT].reshape(size, LAT)
            mixed = jnp.dot(weights, latent, preferred_element_type=jnp.float32)
            shrink = jnp.concatenate([shrink] * (LAT // 128), 1)
            acc[s, rows, :] = acc[s, rows, :] * shrink + mixed

    def attend(s, blk):
        first[...] = score(s, 0, 0, 1024)

        def step(c, _):
            chunk(s, c, blk, 1024, False)
            return 0

        lax.fori_loop(0, blk // 4, step, 0)

        @pl.when(blk % 4 >= 2)
        def _():
            chunk(s, blk // 4, blk, 1024, True)

        @pl.when(blk % 4 < 2)
        def _():
            chunk(s, blk // 4, blk, 512, True)

    def finish(s):
        def value_of(h, _):
            cols = pl.ds(pl.multiple_of(h * VH, VH), VH)
            total = jnp.sum(tot[s, cols, :], 1, keepdims=True)
            mixed = (acc[s, cols, :] * (1.0 / total)).astype(jnp.bfloat16)
            value = jnp.dot(mixed, wv[h], preferred_element_type=jnp.float32)
            ob[s, :, :, cols] = value.astype(jnp.bfloat16).reshape(8, 16, VH)
            return 0

        lax.fori_loop(0, HEADS, value_of, 0)

    attend(1, mirror)
    loaded("wv")
    finish(1)
    send(ob.at[1], out_h.at[:, half], out_sem.at[0], pair)
    attend(0, chain)
    finish(0)
    keep = pltpu.make_async_copy(ob.at[0], out_h.at[:, half], own_sem.at[0])
    keep.start()
    keep.wait()
    arrived(out_h.at[:, 1 - half], out_sem.at[0])
    for copy in sent:
        copy.wait_send()


def hand_over(att_h, cache_h, att_out, cache_out, att, cache, sem):
    pieces = [(cache_h, cache, cache_out)]
    for k in range(4):
        rows = pl.ds(64 * k, 64)
        pieces.append((att_h.at[rows], att.at[rows], att_out.at[rows]))
    into = [pltpu.make_async_copy(p[0], p[1], sem.at[0, k]) for k, p in enumerate(pieces)]
    out = [pltpu.make_async_copy(p[1], p[2], sem.at[1, k]) for k, p in enumerate(pieces)]
    for copy in into:
        copy.start()
    for first, second in zip(into, out):
        first.wait()
        second.start()
    for copy in out:
        copy.wait()


def per_device(tokens, w_down_q, w_down_kv, q_gain, kv_gain, w_up_q, w_absorb, w_value, slot_block):
    bf16, f32 = jnp.bfloat16, jnp.float32
    table = jnp.asarray(rotary_tables())
    hbm = pl.BlockSpec(memory_space=pl.ANY)
    dma = pltpu.SemaphoreType.DMA
    attended, cache = pl.pallas_call(
        kernel,
        out_shape=(
            jax.ShapeDtypeStruct((8, 2, 16, HEADS * VH), bf16),
            jax.ShapeDtypeStruct((2, 16, KV), bf16),
        ),
        in_specs=[hbm] * 8 + [pl.BlockSpec(memory_space=pltpu.SMEM), hbm],
        out_specs=(hbm, pl.BlockSpec(memory_space=pltpu.VMEM)),
        scratch_shapes=[
            pltpu.VMEM((256, 896), bf16),
            pltpu.VMEM((896, QL), bf16),
            pltpu.VMEM((KV, 896), bf16),
            pltpu.VMEM((QL // 128, 128), f32),
            pltpu.VMEM((LAT // 128, 128), f32),
            pltpu.VMEM((QL, HEADS * (NOPE + ROPE)), bf16),
            pltpu.VMEM((HEADS, NOPE, LAT), bf16),
            pltpu.VMEM((HEADS, LAT, VH), bf16),
            pltpu.VMEM((2, 16, 2 * ROPE), f32),
            pltpu.VMEM((2, 8, 16, 2 * ROPE), f32),
            pltpu.VMEM((128, KV), f32),
            pltpu.VMEM((128, KV), f32),
            pltpu.VMEM((128, KV), f32),
            pltpu.VMEM((128, QL), f32),
            pltpu.VMEM((128, QL), f32),
            pltpu.VMEM((128, QL), f32),
            pltpu.VMEM((6, 16, KV), bf16),
            pltpu.VMEM((6, 16, KV), bf16),
            pltpu.VMEM((6, 16, QL), f32),
            pltpu.VMEM((6, 16, QL), f32),
            pltpu.VMEM((2, 16, QL), bf16),
            pltpu.VMEM((2, 8, 16, QL), bf16),
            pltpu.VMEM((32, 128, KEYW), bf16),
            pltpu.VMEM((2, HEADS * 128, KEYW), bf16),
            pltpu.VMEM((512, 1024), f32),
            pltpu.VMEM((2, HEADS * 128, LAT), f32),
            pltpu.VMEM((2, HEADS * 128, 128), f32),
            pltpu.VMEM((2, HEADS * 128, 128), f32),
            pltpu.VMEM((2, 8, 16, HEADS * VH), bf16),
            dma((11,)),
            dma((N_SEND,)),
            dma((2,)),
            dma((6,)),
            dma((6,)),
            dma((2, 8)),
            dma((4,)),
            dma((16, 2)),
            dma((16,)),
            dma((1,)),
            dma((1,)),
        ],
        compiler_params=pltpu.CompilerParams(
            collective_id=0, has_side_effects=True, vmem_limit_bytes=56 * 2**20
        ),
    )(
        tokens, w_down_q, w_down_kv.T, q_gain.reshape(-1, 128), kv_gain.reshape(-1, 128),
        w_up_q, w_absorb, w_value, slot_block, table,
    )
    attended = attended.reshape(256, HEADS * VH)
    return pl.pallas_call(
        hand_over,
        out_shape=(
            jax.ShapeDtypeStruct(attended.shape, bf16),
            jax.ShapeDtypeStruct(cache.shape, bf16),
        ),
        in_specs=[hbm, hbm],
        out_specs=(hbm, hbm),
        scratch_shapes=[
            pltpu.VMEM(attended.shape, bf16),
            pltpu.VMEM(cache.shape, bf16),
            dma((2, 5)),
        ],
        compiler_params=pltpu.CompilerParams(vmem_limit_bytes=60 * 2**20),
    )(attended, cache)


def solution(mesh):
    placed = (
        P("chain", "tp"),
        P("tp", None),
        P("tp", None),
        P(),
        P(),
        P(None, "tp"),
        P("tp", None, None),
        P("tp", None, None),
        P("chain"),
    )
    return jax.shard_map(
        per_device,
        mesh=mesh,
        in_specs=placed,
        out_specs=(P("chain", "tp"), P("chain", "tp", None)),
        check_vma=False,
    )
```

```python
import functools
import math

import jax
import jax.numpy as jnp
import numpy as np
from jax import lax
from jax.experimental import pallas as pl
from jax.experimental.pallas import tpu as pltpu
from jax.sharding import PartitionSpec as P

MESH = pl.DeviceIdType.MESH
ROPE_BASE = 50000.0
FLOOR_SCORE = -1e30
QL, LAT, ROPE, NOPE, VH, HEADS = 1536, 512, 64, 128, 128, 8
KEYW = 640
KV = LAT + ROPE
SCALE2 = (NOPE + ROPE) ** -0.5 * math.log2(math.e)
NT = (((1,), (1,)), ((), ()))
N_SEND = 80
RINGS = (
    (0, 0), (3, 0), (1, 0), (0, 3), (0, 1), (2, 0), (0, 2), (3, 3), (3, 1), (1, 3), (1, 1),
    (2, 3), (2, 1), (3, 2), (1, 2), (2, 2),
)


def rotary_tables():
    inverse = ROPE_BASE ** (-2.0 * np.arange(ROPE // 2) / ROPE)
    angles = np.arange(4096)[:, None] * inverse[None, :]
    cosine = np.concatenate([np.cos(angles), np.cos(angles)], 1)
    sine = np.concatenate([-np.sin(angles), np.sin(angles)], 1)
    both = np.concatenate([cosine, sine], 1).astype(np.float32)
    return both.reshape(16, 8, 2, 16, 2 * ROPE)


def rotate(values, table):
    half = ROPE // 2
    swapped = jnp.concatenate([values[:, half:], values[:, :half]], 1)
    return values * table[:, :ROPE] + swapped * table[:, ROPE:]


def normalize(values, gain):
    return values * lax.rsqrt(jnp.mean(values * values, -1, keepdims=True) + 1e-06) * gain


def kernel(
    tok_h, wq_h, wkv_h, qg_h, kvg_h, wu_h, wa_h, wv_h, slot_ref, tab_h,
    out_h, cache_ref,
    tok, wq, wkv, qg, kvg, wu, wa, wv, tabk, tabq,
    psk, pok, prk, psq, poq, prq, rks, rkr, rqs, rqr, cs, cq, kb, qb, acc, mx, tot, ob,
    load_sem, send_sem, sib_sem, rk_sem, rq_sem, cq_sem, ky_sem, kp_sem, ks_sem, out_sem, own_sem,
):
    chain = lax.axis_index("chain")
    tp = lax.axis_index("tp")
    z, x = chain // 4, chain % 4
    y, core = tp // 2, tp % 2
    other = 1 - core
    mirror = 15 - chain
    half = chain // 8
    piece = core * 4 + y
    yp, ym, yf = (y + 1) % 4, (y + 3) % 4, (y + 2) % 4
    sibling = {"chain": chain, "tp": 2 * y + other}
    up = {"chain": chain, "tp": 2 * yp + core}
    down = {"chain": chain, "tp": 2 * ym + core}
    pair = {"chain": mirror, "tp": tp}
    a = x + core * (z - x)
    b = z + core * (x - z)
    stride_a, stride_b = 1 + 3 * core, 4 - 3 * core

    def at(da, db):
        return ((a + da) % 4) * stride_a + ((b + db) % 4) * stride_b

    ap = {"chain": at(1, 0), "tp": tp}
    am = {"chain": at(3, 0), "tp": tp}
    bp = {"chain": at(0, 1), "tp": tp}
    bm = {"chain": at(0, 3), "tp": tp}

    loads = {}
    for k, (name, src, dst) in enumerate(
        [
            ("tok", tok_h, tok), ("wkv", wkv_h, wkv), ("wq", wq_h, wq), ("kvg", kvg_h, kvg),
            ("qg", qg_h, qg), ("tabk", tab_h.at[chain, piece], tabk), ("wa", wa_h, wa),
            ("wu", wu_h, wu), ("wv", wv_h, wv), ("tab0", tab_h.at[chain, :, half], tabq.at[0]),
            ("tab1", tab_h.at[mirror, :, half], tabq.at[1]),
        ]
    ):
        loads[name] = pltpu.make_async_copy(src, dst, load_sem.at[k])
        if k < 6:
            loads[name].start()

    def loaded(*names):
        for name in names:
            loads[name].wait()

    barrier = pltpu.get_barrier_semaphore()
    partners = (sibling, up, down, pair, ap, am, bp, bm)
    for device in partners:
        pl.semaphore_signal(barrier, inc=1, device_id=device, device_id_type=MESH)
    pl.semaphore_wait(barrier, len(partners))

    sent = []

    def send(src, dst, recv, device):
        slot = len(sent)

        def build():
            return pltpu.make_async_remote_copy(
                src_ref=src(), dst_ref=dst(), send_sem=send_sem.at[slot], recv_sem=recv(),
                device_id=device, device_id_type=MESH,
            )

        build().start()
        sent.append(build)

    def arrived(dst, recv):
        pltpu.make_async_remote_copy(
            src_ref=dst, dst_ref=dst, send_sem=send_sem.at[0], recv_sem=recv,
            device_id=sibling, device_id_type=MESH,
        ).wait_recv()

    def rows_of(c):
        return tok[pl.ds(pl.multiple_of(c * 128, 128), 128), :]

    def project_keys(c, dst):
        dst[...] = lax.dot_general(rows_of(c), wkv[...], NT, preferred_element_type=jnp.float32)

    def project_queries(c, dst):
        left = rows_of(c)

        def tile(i, _):
            cols = pl.ds(pl.multiple_of(i * 512, 512), 512)
            dst[:, cols] = jnp.dot(left, wq[:, cols], preferred_element_type=jnp.float32)
            return 0

        lax.fori_loop(0, 3, tile, 0)

    def ring_of(own, got, out, came, sems):
        def part(yy, h):
            rows = pl.ds(pl.multiple_of(yy * 32 + h * 16, 16), 16)
            return own[rows, :] + got[rows, :]

        def push(k, value, device):
            out[k] = value.astype(out.dtype)
            send(lambda: out.at[k], lambda: came.at[k], lambda: sems.at[k], device)

        def start():
            push(0, part(yf, 0), up)
            push(1, part(yf, 1), down)
            push(2, part(yp, 1), up)
            push(3, part(ym, 0), down)

        def middle():
            arrived(came.at[0], sems.at[0])
            push(4, part(yp, 0) + came[0].astype(jnp.float32), up)
            arrived(came.at[1], sems.at[1])
            push(5, part(ym, 1) + came[1].astype(jnp.float32), down)

        def end():
            for k in (2, 3, 4, 5):
                arrived(came.at[k], sems.at[k])
            totals = []
            for h, first, second in ((0, 4, 3), (1, 2, 5)):
                total = part(y, h) + came[first].astype(jnp.float32)
                totals.append(total + came[second].astype(jnp.float32))
            return totals

        return start, middle, end

    keys_start, keys_middle, keys_end = ring_of(pok, prk, rks, rkr, rk_sem)
    queries_start, queries_middle, queries_end = ring_of(poq, prq, rqs, rqr, rq_sem)

    loaded("tok", "wkv")
    project_keys(other, psk)
    send(lambda: psk, lambda: prk, lambda: sib_sem.at[0], sibling)
    project_keys(core, pok)
    loaded("wq")
    for name in ("wa", "wu", "wv", "tab0", "tab1"):
        loads[name].start()
    arrived(prk, sib_sem.at[0])
    keys_start()
    project_queries(other, psq)
    send(lambda: psq, lambda: prq, lambda: sib_sem.at[1], sibling)
    keys_middle()
    project_queries(core, poq)
    arrived(prq, sib_sem.at[1])
    queries_start()

    slot_own = 2 * chain + core

    def keys_y(yy, h, n):
        return kb.at[slot_own, pl.ds(pl.multiple_of(yy * 32 + h * 16, 16), n)]

    loaded("kvg", "tabk")
    gain_kv = jnp.concatenate([kvg[k : k + 1, :] for k in range(LAT // 128)], 1)
    for h, total in enumerate(keys_end()):
        latent = normalize(total[:, :LAT], gain_kv)
        turned = rotate(total[:, LAT:], tabk[h])
        rows = pl.ds(pl.multiple_of(y * 32 + h * 16, 16), 16)
        kb[slot_own, rows, :LAT] = latent.astype(jnp.bfloat16)
        kb[slot_own, rows, LAT:] = jnp.concatenate(
            [turned, jnp.zeros_like(turned)], 1
        ).astype(jnp.bfloat16)
    def send_y(yy, h, n, k, device):
        send(lambda: keys_y(yy, h, n), lambda: keys_y(yy, h, n), lambda: ky_sem.at[k], device)

    send_y(y, 0, 32, 0, up)
    send_y(y, 0, 32, 1, down)
    queries_middle()
    arrived(keys_y(ym, 0, 32), ky_sem.at[0])
    send_y(ym, 0, 16, 2, up)
    arrived(keys_y(yp, 0, 32), ky_sem.at[1])
    send_y(yp, 1, 16, 3, down)

    def block(n, p=None):
        if p is None:
            return kb.at[2 * n + core]
        return kb.at[2 * n + core, pl.ds(64 * p, 64)]

    def pass_on(n, *devices):
        for device in devices:
            send(lambda: block(n), lambda: block(n), lambda: kp_sem.at[n, 0], device)
        send(lambda: block(n), lambda: block(n), lambda: ks_sem.at[n], sibling)

    def pass_part(n, p, device):
        send(lambda: block(n, p), lambda: block(n, p), lambda: kp_sem.at[n, p], device)

    places_of = {step: at(*step) for step in RINGS}

    def whole(n):
        arrived(block(n), kp_sem.at[n, 0])

    def halves(n):
        for p in range(2):
            arrived(block(n, p), kp_sem.at[n, p])

    def relay(u, v):
        n = places_of[u, v]
        if v == 2 or (u, v) == (2, 0):
            halves(n)
        else:
            whole(n)
        if v == 0:
            if u != 2:
                pass_part(n, 0 if u == 3 else 1, ap if u == 3 else am)
            pass_on(n, bp, bm)
        else:
            if v != 2:
                pass_part(n, 0 if v == 3 else 1, bp if v == 3 else bm)
            pass_on(n)

    arrived(keys_y(yf, 0, 16), ky_sem.at[2])
    arrived(keys_y(yf, 1, 16), ky_sem.at[3])
    pass_on(at(0, 0), ap, am, bp, bm)

    loaded("qg")
    gain_q = jnp.concatenate([qg[k : k + 1, :] for k in range(QL // 128)], 1)
    for h, total in enumerate(queries_end()):
        cs[h] = normalize(total, gain_q).astype(jnp.bfloat16)

    def give(s, p, *devices):
        for device in devices:
            send(lambda: cq.at[s, p], lambda: cq.at[s, p], lambda: cq_sem.at[s, p], device)

    def take(s, p):
        arrived(cq.at[s, p], cq_sem.at[s, p])

    send(lambda: cs.at[1 - half], lambda: cq.at[1, piece], lambda: cq_sem.at[1, piece], pair)
    cq[0, piece] = cs[half]
    give(0, piece, up, down, sibling)
    pm, pp, pf = core * 4 + ym, core * 4 + yp, core * 4 + yf
    for u, v in RINGS[1:5]:
        relay(u, v)
    take(1, piece)
    give(1, piece, up, down, sibling)
    take(0, pm)
    give(0, pm, up, sibling)
    take(0, pp)
    give(0, pp, sibling)
    take(1, pp)
    give(1, pp, down, sibling)
    take(1, pm)
    give(1, pm, sibling)
    for u, v in RINGS[5:7]:
        relay(u, v)
    take(0, pf)
    give(0, pf, sibling)
    take(1, pf)
    give(1, pf, sibling)
    for s in range(2):
        for yy in range(4):
            take(s, other * 4 + yy)

    loaded("wa", "wu", "tab0", "tab1")

    def expand(i, _):
        cols = pl.ds(pl.multiple_of(i * 384, 384), 384)
        rows = cq[...].reshape(256, QL)
        projected = jnp.dot(rows, wu[:, cols], preferred_element_type=jnp.float32)
        table = tabq[...].reshape(256, 2 * ROPE)
        for j in range(2):
            head = 2 * i + j
            base = j * (NOPE + ROPE)
            nope = projected[:, base : base + NOPE].astype(jnp.bfloat16)
            turned = rotate(projected[:, base + NOPE : base + NOPE + ROPE], table)
            turned = jnp.concatenate([turned, jnp.zeros_like(turned)], 1).astype(jnp.bfloat16)
            absorbed = jnp.dot(nope, wa[head], preferred_element_type=jnp.float32)
            absorbed = absorbed.astype(jnp.bfloat16)
            places = pl.ds(pl.multiple_of(head * 128, 128), 128)
            for s in range(2):
                qb[s, places, :LAT] = absorbed[s * 128 : s * 128 + 128]
                qb[s, places, LAT:] = turned[s * 128 : s * 128 + 128]
        return 0

    lax.fori_loop(0, HEADS // 4, expand, 0)
    for u, v in RINGS[7:11]:
        relay(u, v)
    lax.fori_loop(HEADS // 4, HEADS // 2, expand, 0)
    acc[...] = jnp.zeros_like(acc)
    tot[...] = jnp.zeros_like(tot)
    mx[...] = jnp.full_like(mx, FLOOR_SCORE)

    def turn(n, side):
        cols = pl.ds(pl.multiple_of((n % 4) * 256 + side * 128, 128), 128)
        kt[n // 4, :LAT, cols] = kb[2 * n + side, :, :LAT].T

    def turn_own(steps):
        for u, v in steps:
            turn(at(u, v), core)

    def turn_other(steps):
        for u, v in steps:
            n = at(u, v)
            arrived(kb.at[2 * n + other], ks_sem.at[n])
            turn(n, other)

    def whole(n):
        arrived(block(n), kp_sem.at[n, 0])

    def halves(n):
        for p in range(2):
            arrived(block(n, p), kp_sem.at[n, p])

    token = lax.broadcasted_iota(jnp.int32, (512, 1), 0) & 127
    place = ((token >> 4) << 5) + (token & 15) + half * 16
    key_iota = lax.broadcasted_iota(jnp.int32, (1, 1024), 1)

    def score(s, c, r, size):
        keys = kb[pl.ds(8 * c, size // 128)].reshape(size, KEYW)
        queries = qb[s, 512 * r : 512 * r + 512, :]
        return lax.dot_general(queries, keys, NT, preferred_element_type=jnp.float32)

    def chunk(s, c, blk, size, last):
        ahead = score(s, c, 0, size)
        for r in range(2):
            rows = pl.ds(512 * r, 512)
            scores = ahead * SCALE2
            if r < 1:
                ahead = score(s, c, r + 1, size)
            if last:
                visible = key_iota[:, :size] + 1024 * c <= place + 256 * blk
                scores = jnp.where(visible, scores, FLOOR_SCORE)
            parts = [scores[:, k : k + 128] for k in range(0, size, 128)]
            before = mx[s, rows, :]
            top = jnp.max(functools.reduce(jnp.maximum, parts), 1, keepdims=True)
            peak = jnp.maximum(before, top)
            shrink = jnp.exp2(before - peak)
            weights = [jnp.exp2(p - peak) for p in parts]
            mx[s, rows, :] = peak
            tot[s, rows, :] = tot[s, rows, :] * shrink + sum(weights[1:], weights[0])
            weights = jnp.concatenate([w.astype(jnp.bfloat16) for w in weights], 1)
            latent = kb[pl.ds(8 * c, size // 128), :, :LAT].reshape(size, LAT)
            mixed = jnp.dot(weights, latent, preferred_element_type=jnp.float32)
            shrink = jnp.concatenate([shrink] * (LAT // 128), 1)
            acc[s, rows, :] = acc[s, rows, :] * shrink + mixed

    def finish(s):
        def value_of(h, _):
            cols = pl.ds(pl.multiple_of(h * VH, VH), VH)
            total = jnp.sum(tot[s, cols, :], 1, keepdims=True)
            mixed = (acc[s, cols, :] * (1.0 / total)).astype(jnp.bfloat16)
            value = jnp.dot(mixed, wv[h], preferred_element_type=jnp.float32)
            ob[s, :, :, cols] = value.astype(jnp.bfloat16).reshape(8, 16, VH)
            return 0

        lax.fori_loop(0, HEADS, value_of, 0)

    loaded("wv")

    def row(j, _):
        @pl.when(j == 1)
        def _():
            for u, v in RINGS[11:15]:
                relay(u, v)

        @pl.when(j == 3)
        def _():
            relay(2, 2)

        c = (z + j + (j == 2).astype(jnp.int32) - (j == 3).astype(jnp.int32)) % 4
        for k in range(4):
            arrived(kb.at[2 * (4 * c + k) + other], ks_sem.at[4 * c + k])

        def side(q, _):
            s = 1 - q
            blk = chain + s * (mirror - chain)
            edge = blk // 4

            @pl.when(c < edge)
            def _():
                chunk(s, c, blk, 1024, False)

            @pl.when((c == edge) & (blk % 4 >= 2))
            def _():
                chunk(s, c, blk, 1024, True)

            @pl.when((c == edge) & (blk % 4 < 2))
            def _():
                chunk(s, c, blk, 512, True)

            @pl.when((j == 3) & (q == 0))
            def _():
                finish(1)
                send(lambda: ob.at[1], lambda: out_h.at[:, half], lambda: out_sem.at[0], pair)

            return 0

        lax.fori_loop(0, 2, side, 0)
        return 0

    lax.fori_loop(0, 4, row, 0)
    finish(0)
    keep = pltpu.make_async_copy(ob.at[0], out_h.at[:, half], own_sem.at[0])
    keep.start()
    for j in range(2):
        rows = pl.ds(pl.multiple_of(tp * 16, 16), 16)
        cache_ref[j] = kb[slot_ref[j], rows, :][:, :KV]
    keep.wait()
    arrived(out_h.at[:, 1 - half], out_sem.at[0])
    for build in sent:
        build().wait_send()


def hand_over(att_h, cache_h, att_out, cache_out, att, cache, sem):
    pieces = [(cache_h, cache, cache_out)]
    for k in range(4):
        rows = pl.ds(64 * k, 64)
        pieces.append((att_h.at[rows], att.at[rows], att_out.at[rows]))
    into = [pltpu.make_async_copy(p[0], p[1], sem.at[0, k]) for k, p in enumerate(pieces)]
    out = [pltpu.make_async_copy(p[1], p[2], sem.at[1, k]) for k, p in enumerate(pieces)]
    for copy in into:
        copy.start()
    for first, second in zip(into, out):
        first.wait()
        second.start()
    for copy in out:
        copy.wait()


def per_device(tokens, w_down_q, w_down_kv, q_gain, kv_gain, w_up_q, w_absorb, w_value, slot_block):
    bf16, f32 = jnp.bfloat16, jnp.float32
    table = jnp.asarray(rotary_tables())
    hbm = pl.BlockSpec(memory_space=pl.ANY)
    dma = pltpu.SemaphoreType.DMA
    attended, cache = pl.pallas_call(
        kernel,
        out_shape=(
            jax.ShapeDtypeStruct((8, 2, 16, HEADS * VH), bf16),
            jax.ShapeDtypeStruct((2, 16, KV), bf16),
        ),
        in_specs=[hbm] * 8 + [pl.BlockSpec(memory_space=pltpu.SMEM), hbm],
        out_specs=(hbm, pl.BlockSpec(memory_space=pltpu.VMEM)),
        scratch_shapes=[
            pltpu.VMEM((256, 896), bf16),
            pltpu.VMEM((896, QL), bf16),
            pltpu.VMEM((KV, 896), bf16),
            pltpu.VMEM((QL // 128, 128), f32),
            pltpu.VMEM((LAT // 128, 128), f32),
            pltpu.VMEM((QL, HEADS * (NOPE + ROPE)), bf16),
            pltpu.VMEM((HEADS, NOPE, LAT), bf16),
            pltpu.VMEM((HEADS, LAT, VH), bf16),
            pltpu.VMEM((2, 16, 2 * ROPE), f32),
            pltpu.VMEM((2, 8, 16, 2 * ROPE), f32),
            pltpu.VMEM((128, KV), f32),
            pltpu.VMEM((128, KV), f32),
            pltpu.VMEM((128, KV), f32),
            pltpu.VMEM((128, QL), f32),
            pltpu.VMEM((128, QL), f32),
            pltpu.VMEM((128, QL), f32),
            pltpu.VMEM((6, 16, KV), bf16),
            pltpu.VMEM((6, 16, KV), bf16),
            pltpu.VMEM((6, 16, QL), f32),
            pltpu.VMEM((6, 16, QL), f32),
            pltpu.VMEM((2, 16, QL), bf16),
            pltpu.VMEM((2, 8, 16, QL), bf16),
            pltpu.VMEM((32, 128, KEYW), bf16),
            pltpu.VMEM((2, HEADS * 128, KEYW), bf16),
            pltpu.VMEM((2, HEADS * 128, LAT), f32),
            pltpu.VMEM((2, HEADS * 128, 128), f32),
            pltpu.VMEM((2, HEADS * 128, 128), f32),
            pltpu.VMEM((2, 8, 16, HEADS * VH), bf16),
            dma((11,)),
            dma((N_SEND,)),
            dma((2,)),
            dma((6,)),
            dma((6,)),
            dma((2, 8)),
            dma((4,)),
            dma((16, 2)),
            dma((16,)),
            dma((1,)),
            dma((1,)),
        ],
        compiler_params=pltpu.CompilerParams(
            collective_id=0, has_side_effects=True, vmem_limit_bytes=56 * 2**20
        ),
    )(
        tokens, w_down_q, w_down_kv.T, q_gain.reshape(-1, 128), kv_gain.reshape(-1, 128),
        w_up_q, w_absorb, w_value, slot_block, table,
    )
    attended = attended.reshape(256, HEADS * VH)
    return pl.pallas_call(
        hand_over,
        out_shape=(
            jax.ShapeDtypeStruct(attended.shape, bf16),
            jax.ShapeDtypeStruct(cache.shape, bf16),
        ),
        in_specs=[hbm, hbm],
        out_specs=(hbm, hbm),
        scratch_shapes=[
            pltpu.VMEM(attended.shape, bf16),
            pltpu.VMEM(cache.shape, bf16),
            dma((2, 5)),
        ],
        compiler_params=pltpu.CompilerParams(vmem_limit_bytes=60 * 2**20),
    )(attended, cache)


def solution(mesh):
    placed = (
        P("chain", "tp"),
        P("tp", None),
        P("tp", None),
        P(),
        P(),
        P(None, "tp"),
        P("tp", None, None),
        P("tp", None, None),
        P("chain"),
    )
    return jax.shard_map(
        per_device,
        mesh=mesh,
        in_specs=placed,
        out_specs=(P("chain", "tp"), P("chain", "tp", None)),
        check_vma=False,
    )
```

```python
import functools
import math

import jax
import jax.numpy as jnp
import numpy as np
from jax import lax
from jax.experimental import pallas as pl
from jax.experimental.pallas import tpu as pltpu
from jax.sharding import PartitionSpec as P

MESH = pl.DeviceIdType.MESH
ROPE_BASE = 50000.0
FLOOR_SCORE = -1e30
QL, LAT, ROPE, NOPE, VH, HEADS = 1536, 512, 64, 128, 128, 8
KEYW = 640
KV = LAT + ROPE
SCALE2 = (NOPE + ROPE) ** -0.5 * math.log2(math.e)
NT = (((1,), (1,)), ((), ()))
N_SEND = 80
RINGS = (
    (0, 0), (3, 0), (1, 0), (0, 3), (0, 1), (2, 0), (0, 2), (3, 3), (3, 1), (1, 3), (1, 1),
    (2, 3), (2, 1), (3, 2), (1, 2), (2, 2),
)


def rotary_tables():
    inverse = ROPE_BASE ** (-2.0 * np.arange(ROPE // 2) / ROPE)
    angles = np.arange(4096)[:, None] * inverse[None, :]
    cosine = np.concatenate([np.cos(angles), np.cos(angles)], 1)
    sine = np.concatenate([-np.sin(angles), np.sin(angles)], 1)
    both = np.concatenate([cosine, sine], 1).astype(np.float32)
    return both.reshape(16, 8, 2, 16, 2 * ROPE)


def rotate(values, table):
    half = ROPE // 2
    swapped = jnp.concatenate([values[:, half:], values[:, :half]], 1)
    return values * table[:, :ROPE] + swapped * table[:, ROPE:]


def normalize(values, gain):
    return values * lax.rsqrt(jnp.mean(values * values, -1, keepdims=True) + 1e-06) * gain


def kernel(
    tok_h, wq_h, wkv_h, qg_h, kvg_h, wu_h, wa_h, wv_h, slot_ref, tab_h,
    out_h, cache_ref,
    tok, wq, wkv, qg, kvg, wu, wa, wv, tabk, tabq,
    psk, pok, prk, psq, poq, prq, rks, rkr, rqs, rqr, cs, cq, kb, qb, first, second, acc, mx, tot, ob,
    load_sem, send_sem, sib_sem, rk_sem, rq_sem, cq_sem, ky_sem, kp_sem, ks_sem, out_sem, outs_sem, own_sem,
):
    chain = lax.axis_index("chain")
    tp = lax.axis_index("tp")
    z, x = chain // 4, chain % 4
    y, core = tp // 2, tp % 2
    other = 1 - core
    mirror = 15 - chain
    half = chain // 8
    piece = core * 4 + y
    yp, ym, yf = (y + 1) % 4, (y + 3) % 4, (y + 2) % 4
    sibling = {"chain": chain, "tp": 2 * y + other}
    up = {"chain": chain, "tp": 2 * yp + core}
    down = {"chain": chain, "tp": 2 * ym + core}
    pair = {"chain": mirror, "tp": tp}
    a = x + core * (z - x)
    b = z + core * (x - z)
    stride_a, stride_b = 1 + 3 * core, 4 - 3 * core

    def at(da, db):
        return ((a + da) % 4) * stride_a + ((b + db) % 4) * stride_b

    ap = {"chain": at(1, 0), "tp": tp}
    am = {"chain": at(3, 0), "tp": tp}
    bp = {"chain": at(0, 1), "tp": tp}
    bm = {"chain": at(0, 3), "tp": tp}

    loads = {}
    for k, (name, src, dst) in enumerate(
        [
            ("tok", tok_h, tok), ("wkv", wkv_h, wkv), ("wq", wq_h, wq), ("kvg", kvg_h, kvg),
            ("qg", qg_h, qg), ("tabk", tab_h.at[chain, piece], tabk), ("wa", wa_h, wa),
            ("wu", wu_h, wu), ("wv", wv_h, wv), ("tab0", tab_h.at[chain, :, half], tabq.at[0]),
            ("tab1", tab_h.at[mirror, :, half], tabq.at[1]),
        ]
    ):
        loads[name] = pltpu.make_async_copy(src, dst, load_sem.at[k])
        if k < 6:
            loads[name].start()

    def loaded(*names):
        for name in names:
            loads[name].wait()

    barrier = pltpu.get_barrier_semaphore()
    partners = (sibling, up, down, pair, ap, am, bp, bm)
    for device in partners:
        pl.semaphore_signal(barrier, inc=1, device_id=device, device_id_type=MESH)
    pl.semaphore_wait(barrier, len(partners))

    sent = {}

    def send(src, dst, recv, device, key=None):
        if key is None or key not in sent:
            slot = len(sent)

            def build():
                return pltpu.make_async_remote_copy(
                    src_ref=src(), dst_ref=dst(), send_sem=send_sem.at[slot], recv_sem=recv(),
                    device_id=device, device_id_type=MESH,
                )

            key = slot if key is None else key
            sent[key] = build
        sent[key]().start()

    def arrived(dst, recv):
        pltpu.make_async_remote_copy(
            src_ref=dst, dst_ref=dst, send_sem=send_sem.at[0], recv_sem=recv,
            device_id=sibling, device_id_type=MESH,
        ).wait_recv()

    def rows_of(c):
        return tok[pl.ds(pl.multiple_of(c * 128, 128), 128), :]

    def project_keys(c, dst):
        dst[...] = lax.dot_general(rows_of(c), wkv[...], NT, preferred_element_type=jnp.float32)

    def project_queries(c, dst):
        left = rows_of(c)

        def tile(i, _):
            cols = pl.ds(pl.multiple_of(i * 512, 512), 512)
            dst[:, cols] = jnp.dot(left, wq[:, cols], preferred_element_type=jnp.float32)
            return 0

        lax.fori_loop(0, 3, tile, 0)

    def ring_of(own, got, out, came, sems):
        def part(yy, h):
            rows = pl.ds(pl.multiple_of(yy * 32 + h * 16, 16), 16)
            return own[rows, :] + got[rows, :]

        def push(k, value, device):
            out[k] = value.astype(out.dtype)
            send(lambda: out.at[k], lambda: came.at[k], lambda: sems.at[k], device)

        def start():
            push(0, part(yf, 0), up)
            push(1, part(yf, 1), down)
            push(2, part(yp, 1), up)
            push(3, part(ym, 0), down)

        def middle():
            arrived(came.at[0], sems.at[0])
            push(4, part(yp, 0) + came[0].astype(jnp.float32), up)
            arrived(came.at[1], sems.at[1])
            push(5, part(ym, 1) + came[1].astype(jnp.float32), down)

        def end():
            for k in (2, 3, 4, 5):
                arrived(came.at[k], sems.at[k])
            totals = []
            for h, first, second in ((0, 4, 3), (1, 2, 5)):
                total = part(y, h) + came[first].astype(jnp.float32)
                totals.append(total + came[second].astype(jnp.float32))
            return totals

        return start, middle, end

    keys_start, keys_middle, keys_end = ring_of(pok, prk, rks, rkr, rk_sem)
    queries_start, queries_middle, queries_end = ring_of(poq, prq, rqs, rqr, rq_sem)

    loaded("tok", "wkv")
    project_keys(other, psk)
    send(lambda: psk, lambda: prk, lambda: sib_sem.at[0], sibling)
    project_keys(core, pok)
    loaded("wq")
    for name in ("wa", "wu", "wv", "tab0", "tab1"):
        loads[name].start()
    arrived(prk, sib_sem.at[0])
    keys_start()
    project_queries(other, psq)
    send(lambda: psq, lambda: prq, lambda: sib_sem.at[1], sibling)
    keys_middle()
    project_queries(core, poq)
    arrived(prq, sib_sem.at[1])
    queries_start()
    acc[...] = jnp.zeros_like(acc)
    tot[...] = jnp.zeros_like(tot)
    mx[...] = jnp.full_like(mx, FLOOR_SCORE)

    slot_own = 2 * chain + core

    def keys_y(yy, h, n):
        return kb.at[slot_own, pl.ds(pl.multiple_of(yy * 32 + h * 16, 16), n)]

    loaded("kvg", "tabk")
    gain_kv = jnp.concatenate([kvg[k : k + 1, :] for k in range(LAT // 128)], 1)
    for h, total in enumerate(keys_end()):
        latent = normalize(total[:, :LAT], gain_kv)
        turned = rotate(total[:, LAT:], tabk[h])
        rows = pl.ds(pl.multiple_of(y * 32 + h * 16, 16), 16)
        kb[slot_own, rows, :LAT] = latent.astype(jnp.bfloat16)
        kb[slot_own, rows, LAT:] = jnp.concatenate(
            [turned, jnp.zeros_like(turned)], 1
        ).astype(jnp.bfloat16)
    def send_y(yy, h, n, k, device):
        send(lambda: keys_y(yy, h, n), lambda: keys_y(yy, h, n), lambda: ky_sem.at[k], device)

    send_y(y, 0, 32, 0, up)
    send_y(y, 0, 32, 1, down)
    queries_middle()
    arrived(keys_y(ym, 0, 32), ky_sem.at[0])
    send_y(ym, 0, 16, 2, up)
    arrived(keys_y(yp, 0, 32), ky_sem.at[1])
    send_y(yp, 1, 16, 3, down)

    def block(n, p=None):
        if p is None:
            return kb.at[2 * n + core]
        return kb.at[2 * n + core, pl.ds(64 * p, 64)]

    def pass_on(step, n, *devices):
        for k, device in enumerate(devices):
            send(lambda: block(n), lambda: block(n), lambda: kp_sem.at[n, 0], device, (step, k))
        send(lambda: block(n), lambda: block(n), lambda: ks_sem.at[n], sibling, (step, 4))

    def pass_part(step, n, p, device):
        send(lambda: block(n, p), lambda: block(n, p), lambda: kp_sem.at[n, p], device, (step, 5))

    places_of = {step: at(*step) for step in RINGS}

    def whole(n):
        arrived(block(n), kp_sem.at[n, 0])

    def halves(n):
        for p in range(2):
            arrived(block(n, p), kp_sem.at[n, p])

    def relay(u, v):
        n = places_of[u, v]
        if v == 2 or (u, v) == (2, 0):
            halves(n)
        else:
            whole(n)
        if v == 0:
            if u != 2:
                pass_part((u, v), n, 0 if u == 3 else 1, ap if u == 3 else am)
            pass_on((u, v), n, bp, bm)
        else:
            if v != 2:
                pass_part((u, v), n, 0 if v == 3 else 1, bp if v == 3 else bm)
            pass_on((u, v), n)

    arrived(keys_y(yf, 0, 16), ky_sem.at[2])
    arrived(keys_y(yf, 1, 16), ky_sem.at[3])
    pass_on((0, 0), places_of[0, 0], ap, am, bp, bm)

    loaded("qg")
    gain_q = jnp.concatenate([qg[k : k + 1, :] for k in range(QL // 128)], 1)
    for h, total in enumerate(queries_end()):
        cs[h] = normalize(total, gain_q).astype(jnp.bfloat16)

    def give(s, p, *devices):
        for device in devices:
            send(lambda: cq.at[s, p], lambda: cq.at[s, p], lambda: cq_sem.at[s, p], device)

    def take(s, p):
        arrived(cq.at[s, p], cq_sem.at[s, p])

    send(lambda: cs.at[1 - half], lambda: cq.at[1, piece], lambda: cq_sem.at[1, piece], pair)
    cq[0, piece] = cs[half]
    give(0, piece, up, down, sibling)
    pm, pp, pf = core * 4 + ym, core * 4 + yp, core * 4 + yf
    for u, v in RINGS[1:5]:
        relay(u, v)
    take(1, piece)
    give(1, piece, up, down, sibling)
    take(0, pm)
    give(0, pm, up, sibling)
    take(0, pp)
    give(0, pp, sibling)
    take(1, pp)
    give(1, pp, down, sibling)
    take(1, pm)
    give(1, pm, sibling)
    for u, v in RINGS[5:7]:
        relay(u, v)
    take(0, pf)
    give(0, pf, sibling)
    take(1, pf)
    give(1, pf, sibling)
    for s in range(2):
        for yy in range(4):
            take(s, other * 4 + yy)

    loaded("wa", "wu", "tab0", "tab1")

    def expand(i, _):
        cols = pl.ds(pl.multiple_of(i * 384, 384), 384)
        rows = cq[...].reshape(256, QL)
        projected = jnp.dot(rows, wu[:, cols], preferred_element_type=jnp.float32)
        table = tabq[...].reshape(256, 2 * ROPE)
        for j in range(2):
            head = 2 * i + j
            base = j * (NOPE + ROPE)
            nope = projected[:, base : base + NOPE].astype(jnp.bfloat16)
            turned = rotate(projected[:, base + NOPE : base + NOPE + ROPE], table)
            turned = jnp.concatenate([turned, jnp.zeros_like(turned)], 1).astype(jnp.bfloat16)
            absorbed = jnp.dot(nope, wa[head], preferred_element_type=jnp.float32)
            absorbed = absorbed.astype(jnp.bfloat16)
            places = pl.ds(pl.multiple_of(head * 128, 128), 128)
            for s in range(2):
                qb[s, places, :LAT] = absorbed[s * 128 : s * 128 + 128]
                qb[s, places, LAT:] = turned[s * 128 : s * 128 + 128]
        return 0

    lax.fori_loop(0, HEADS // 4, expand, 0)
    for u, v in RINGS[7:11]:
        relay(u, v)
    lax.fori_loop(HEADS // 4, HEADS // 2, expand, 0)

    def meet(c):
        for k in range(4):
            n = 4 * (c % 4) + k
            arrived(kb.at[2 * n + other], ks_sem.at[n])

    def second_rows():
        for u, v in RINGS[11:15]:
            relay(u, v)
        meet(z + 1)
        meet(z + 3)

    def last_row():
        relay(2, 2)
        meet(z + 2)

    def turn(n, side):
        cols = pl.ds(pl.multiple_of((n % 4) * 256 + side * 128, 128), 128)
        kt[n // 4, :LAT, cols] = kb[2 * n + side, :, :LAT].T

    def turn_own(steps):
        for u, v in steps:
            turn(at(u, v), core)

    def turn_other(steps):
        for u, v in steps:
            n = at(u, v)
            arrived(kb.at[2 * n + other], ks_sem.at[n])
            turn(n, other)

    def whole(n):
        arrived(block(n), kp_sem.at[n, 0])

    def halves(n):
        for p in range(2):
            arrived(block(n, p), kp_sem.at[n, p])

    token = lax.broadcasted_iota(jnp.int32, (512, 1), 0) & 127
    place = ((token >> 4) << 5) + (token & 15) + half * 16
    key_iota = lax.broadcasted_iota(jnp.int32, (1, 512), 1)
    early = 1 - z // 2
    n_own, n_far = chain // 2 + 1, mirror // 2 + 1
    ends = (n_own + early * (n_far - n_own), n_own + n_far, 18 - n_own, 18)
    ends = (ends[0], ends[0] + n_far, ends[2], ends[3])
    own_steps = 2 - (1 - early) * (1 - (chain % 4) // 2)

    def plan(t):
        p1 = (t >= ends[0]).astype(jnp.int32)
        p2 = (t >= ends[1]).astype(jnp.int32)
        p3 = (t >= ends[2]).astype(jnp.int32)
        p = p1 + p2 + p3
        j = t - p1 * ends[0] - p2 * (ends[1] - ends[0]) - p3 * (ends[2] - ends[1])
        s = jnp.where(p == 0, early, jnp.where(p == 1, 1, jnp.where(p == 2, 1 - early, 0)))
        r = jnp.where(p == 0, 0, jnp.where(p == 1, early, jnp.where(p == 2, 1 - early, 1)))
        chunks = n_own + s * (n_far - n_own)
        ahead = (2 * z + j) % chunks
        back = chunks - 1 - j
        c = back + s * early * (ahead - back)
        return s, r, c, c == chunks - 1

    def rows_of_pass(r):
        return pl.ds(pl.multiple_of(r * 512, 512), 512)

    def score(t, dst):
        s, r, c, _ = plan(t)
        keys = kb[pl.ds(4 * c, 4)].reshape(512, KEYW)
        dst[...] = lax.dot_general(
            qb[s, rows_of_pass(r), :], keys, NT, preferred_element_type=jnp.float32
        )

    def hide(t, dst):
        s, _, c, last = plan(t)

        @pl.when(last)
        def _():
            blk = chain + s * (mirror - chain)
            visible = key_iota + 512 * c <= place + 256 * blk
            dst[...] = jnp.where(visible, dst[...], FLOOR_SCORE)

    def out_cols(r):
        return pl.ds(pl.multiple_of(r * 512, 512), 512)

    def out_copy(r):
        return pltpu.make_async_remote_copy(
            src_ref=ob.at[1, :, :, out_cols(r)], dst_ref=out_h.at[:, half, :, out_cols(r)],
            send_sem=outs_sem.at[r], recv_sem=out_sem.at[r], device_id=pair, device_id_type=MESH,
        )

    def own_copy(r):
        return pltpu.make_async_copy(
            ob.at[0, :, :, out_cols(r)], out_h.at[:, half, :, out_cols(r)], own_sem.at[r]
        )

    def step(t, now, later):
        s, r, c, _ = plan(t)
        rows = rows_of_pass(r)
        score(jnp.minimum(t + 1, 17), later)
        parts = [now[:, k : k + 128] * SCALE2 for k in range(0, 512, 128)]
        before = mx[s, rows, :]
        top = jnp.max(functools.reduce(jnp.maximum, parts), 1, keepdims=True)
        peak = jnp.maximum(before, top)
        shrink = jnp.exp2(before - peak)
        weights = [jnp.exp2(p - peak) for p in parts]
        mx[s, rows, :] = peak
        tot[s, rows, :] = tot[s, rows, :] * shrink + sum(weights[1:], weights[0])
        weights = jnp.concatenate([w.astype(jnp.bfloat16) for w in weights], 1)
        latent = kb[pl.ds(4 * c, 4), :, :LAT].reshape(512, LAT)
        mixed = jnp.dot(weights, latent, preferred_element_type=jnp.float32)
        shrink = jnp.concatenate([shrink] * (LAT // 128), 1)
        acc[s, rows, :] = acc[s, rows, :] * shrink + mixed
        hide(jnp.minimum(t + 1, 17), later)

        @pl.when((t + 1 == ends[0]) | (t + 1 == ends[1]) | (t + 1 == ends[2]) | (t + 1 == ends[3]))
        def _():
            for k in range(4):
                part = pl.ds(pl.multiple_of(r * 512 + k * 128, 128), 128)
                total = jnp.sum(tot[s, part, :], 1, keepdims=True)
                mixed = (acc[s, part, :] * (1.0 / total)).astype(jnp.bfloat16)
                value = jnp.dot(mixed, wv[4 * r + k], preferred_element_type=jnp.float32)
                ob[s, :, :, part] = value.astype(jnp.bfloat16).reshape(8, 16, VH)

            @pl.when(s == 1)
            def _():
                out_copy(r).start()

            @pl.when(s == 0)
            def _():
                own_copy(r).start()

    loaded("wv")
    meet(z)
    score(0, first)
    hide(0, first)

    def two_steps(i, _):
        @pl.when((i == 0) & (own_steps == 1))
        def _():
            second_rows()

        @pl.when(i == 1)
        def _():
            last_row()

        step(2 * i, first, second)

        @pl.when((i == 0) & (own_steps == 2))
        def _():
            second_rows()

        step(2 * i + 1, second, first)
        return 0

    lax.fori_loop(0, 9, two_steps, 0)
    for j in range(2):
        rows = pl.ds(pl.multiple_of(tp * 16, 16), 16)
        cache_ref[j] = kb[slot_ref[j], rows, :][:, :KV]
    for r in range(2):
        own_copy(r).wait()
        out_copy(r).wait_send()
        arrived(out_h.at[:, 1 - half, :, out_cols(r)], out_sem.at[r])
    for build in sent.values():
        build().wait_send()


def hand_over(att_h, cache_h, att_out, cache_out, att, cache, sem):
    pieces = [(cache_h, cache, cache_out)]
    for k in range(4):
        rows = pl.ds(64 * k, 64)
        pieces.append((att_h.at[rows], att.at[rows], att_out.at[rows]))
    into = [pltpu.make_async_copy(p[0], p[1], sem.at[0, k]) for k, p in enumerate(pieces)]
    out = [pltpu.make_async_copy(p[1], p[2], sem.at[1, k]) for k, p in enumerate(pieces)]
    for copy in into:
        copy.start()
    for first, second in zip(into, out):
        first.wait()
        second.start()
    for copy in out:
        copy.wait()


def per_device(tokens, w_down_q, w_down_kv, q_gain, kv_gain, w_up_q, w_absorb, w_value, slot_block):
    bf16, f32 = jnp.bfloat16, jnp.float32
    table = jnp.asarray(rotary_tables())
    hbm = pl.BlockSpec(memory_space=pl.ANY)
    dma = pltpu.SemaphoreType.DMA
    attended, cache = pl.pallas_call(
        kernel,
        out_shape=(
            jax.ShapeDtypeStruct((8, 2, 16, HEADS * VH), bf16),
            jax.ShapeDtypeStruct((2, 16, KV), bf16),
        ),
        in_specs=[hbm] * 8 + [pl.BlockSpec(memory_space=pltpu.SMEM), hbm],
        out_specs=(hbm, pl.BlockSpec(memory_space=pltpu.VMEM)),
        scratch_shapes=[
            pltpu.VMEM((256, 896), bf16),
            pltpu.VMEM((896, QL), bf16),
            pltpu.VMEM((KV, 896), bf16),
            pltpu.VMEM((QL // 128, 128), f32),
            pltpu.VMEM((LAT // 128, 128), f32),
            pltpu.VMEM((QL, HEADS * (NOPE + ROPE)), bf16),
            pltpu.VMEM((HEADS, NOPE, LAT), bf16),
            pltpu.VMEM((HEADS, LAT, VH), bf16),
            pltpu.VMEM((2, 16, 2 * ROPE), f32),
            pltpu.VMEM((2, 8, 16, 2 * ROPE), f32),
            pltpu.VMEM((128, KV), f32),
            pltpu.VMEM((128, KV), f32),
            pltpu.VMEM((128, KV), f32),
            pltpu.VMEM((128, QL), f32),
            pltpu.VMEM((128, QL), f32),
            pltpu.VMEM((128, QL), f32),
            pltpu.VMEM((6, 16, KV), bf16),
            pltpu.VMEM((6, 16, KV), bf16),
            pltpu.VMEM((6, 16, QL), f32),
            pltpu.VMEM((6, 16, QL), f32),
            pltpu.VMEM((2, 16, QL), bf16),
            pltpu.VMEM((2, 8, 16, QL), bf16),
            pltpu.VMEM((32, 128, KEYW), bf16),
            pltpu.VMEM((2, HEADS * 128, KEYW), bf16),
            pltpu.VMEM((512, 512), f32),
            pltpu.VMEM((512, 512), f32),
            pltpu.VMEM((2, HEADS * 128, LAT), f32),
            pltpu.VMEM((2, HEADS * 128, 128), f32),
            pltpu.VMEM((2, HEADS * 128, 128), f32),
            pltpu.VMEM((2, 8, 16, HEADS * VH), bf16),
            dma((11,)),
            dma((N_SEND,)),
            dma((2,)),
            dma((6,)),
            dma((6,)),
            dma((2, 8)),
            dma((4,)),
            dma((16, 2)),
            dma((16,)),
            dma((2,)),
            dma((2,)),
            dma((2,)),
        ],
        compiler_params=pltpu.CompilerParams(
            collective_id=0, has_side_effects=True, vmem_limit_bytes=56 * 2**20
        ),
    )(
        tokens, w_down_q, w_down_kv.T, q_gain.reshape(-1, 128), kv_gain.reshape(-1, 128),
        w_up_q, w_absorb, w_value, slot_block, table,
    )
    attended = attended.reshape(256, HEADS * VH)
    return pl.pallas_call(
        hand_over,
        out_shape=(
            jax.ShapeDtypeStruct(attended.shape, bf16),
            jax.ShapeDtypeStruct(cache.shape, bf16),
        ),
        in_specs=[hbm, hbm],
        out_specs=(hbm, hbm),
        scratch_shapes=[
            pltpu.VMEM(attended.shape, bf16),
            pltpu.VMEM(cache.shape, bf16),
            dma((2, 5)),
        ],
        compiler_params=pltpu.CompilerParams(vmem_limit_bytes=60 * 2**20),
    )(attended, cache)


def solution(mesh):
    placed = (
        P("chain", "tp"),
        P("tp", None),
        P("tp", None),
        P(),
        P(),
        P(None, "tp"),
        P("tp", None, None),
        P("tp", None, None),
        P("chain"),
    )
    return jax.shard_map(
        per_device,
        mesh=mesh,
        in_specs=placed,
        out_specs=(P("chain", "tp"), P("chain", "tp", None)),
        check_vma=False,
    )
```

```python
import functools
import math

import jax
import jax.numpy as jnp
import numpy as np
from jax import lax
from jax.experimental import pallas as pl
from jax.experimental.pallas import tpu as pltpu
from jax.sharding import PartitionSpec as P

MESH = pl.DeviceIdType.MESH
ROPE_BASE = 50000.0
FLOOR_SCORE = -1e30
QL, LAT, ROPE, NOPE, VH, HEADS = 1536, 512, 64, 128, 128, 8
KEYW = 640
KV = LAT + ROPE
SCALE2 = (NOPE + ROPE) ** -0.5 * math.log2(math.e)
NT = (((1,), (1,)), ((), ()))
N_SEND = 80
RINGS = (
    (0, 0), (3, 0), (1, 0), (0, 3), (0, 1), (2, 0), (0, 2), (3, 3), (3, 1), (1, 3), (1, 1),
    (2, 3), (2, 1), (3, 2), (1, 2), (2, 2),
)


def rotary_tables():
    inverse = ROPE_BASE ** (-2.0 * np.arange(ROPE // 2) / ROPE)
    angles = np.arange(4096)[:, None] * inverse[None, :]
    cosine = np.concatenate([np.cos(angles), np.cos(angles)], 1)
    sine = np.concatenate([-np.sin(angles), np.sin(angles)], 1)
    both = np.concatenate([cosine, sine], 1).astype(np.float32)
    return both.reshape(16, 8, 2, 16, 2 * ROPE)


def rotate(values, table):
    half = ROPE // 2
    swapped = jnp.concatenate([values[:, half:], values[:, :half]], 1)
    return values * table[:, :ROPE] + swapped * table[:, ROPE:]


def normalize(values, gain):
    return values * lax.rsqrt(jnp.mean(values * values, -1, keepdims=True) + 1e-06) * gain


def kernel(
    tok_h, wq_h, wkv_h, qg_h, kvg_h, wu_h, wa_h, wv_h, slot_ref, tab_h,
    out_h, cache_ref,
    tok, wq, wkv, qg, kvg, wu, wa, wv, tabk, tabq,
    psk, pok, prk, psq, poq, prq, rks, rkr, rqs, rqr, cs, cq, kb, qb, first, second, acc, mx, tot, ob,
    load_sem, send_sem, sib_sem, rk_sem, rq_sem, cq_sem, ky_sem, kp_sem, ks_sem, out_sem, outs_sem, own_sem,
):
    chain = lax.axis_index("chain")
    tp = lax.axis_index("tp")
    z, x = chain // 4, chain % 4
    y, core = tp // 2, tp % 2
    other = 1 - core
    mirror = 15 - chain
    half = chain // 8
    piece = core * 4 + y
    yp, ym, yf = (y + 1) % 4, (y + 3) % 4, (y + 2) % 4
    sibling = {"chain": chain, "tp": 2 * y + other}
    up = {"chain": chain, "tp": 2 * yp + core}
    down = {"chain": chain, "tp": 2 * ym + core}
    pair = {"chain": mirror, "tp": tp}
    a = x + core * (z - x)
    b = z + core * (x - z)
    stride_a, stride_b = 1 + 3 * core, 4 - 3 * core

    def at(da, db):
        return ((a + da) % 4) * stride_a + ((b + db) % 4) * stride_b

    ap = {"chain": at(1, 0), "tp": tp}
    am = {"chain": at(3, 0), "tp": tp}
    bp = {"chain": at(0, 1), "tp": tp}
    bm = {"chain": at(0, 3), "tp": tp}

    loads = {}
    for k, (name, src, dst) in enumerate(
        [
            ("tok", tok_h, tok), ("wkv", wkv_h, wkv), ("wq", wq_h, wq), ("kvg", kvg_h, kvg),
            ("qg", qg_h, qg), ("tabk", tab_h.at[chain, piece], tabk), ("wa", wa_h, wa),
            ("wu", wu_h, wu), ("wv", wv_h, wv), ("tab0", tab_h.at[chain, :, half], tabq.at[0]),
            ("tab1", tab_h.at[mirror, :, half], tabq.at[1]),
        ]
    ):
        loads[name] = pltpu.make_async_copy(src, dst, load_sem.at[k])
        if k < 6:
            loads[name].start()

    def loaded(*names):
        for name in names:
            loads[name].wait()

    barrier = pltpu.get_barrier_semaphore()
    partners = (sibling, up, down, pair, ap, am, bp, bm)
    for device in partners:
        pl.semaphore_signal(barrier, inc=1, device_id=device, device_id_type=MESH)
    pl.semaphore_wait(barrier, len(partners))

    sent = {}

    def send(src, dst, recv, device, key=None):
        if key is None or key not in sent:
            slot = len(sent)

            def build():
                return pltpu.make_async_remote_copy(
                    src_ref=src(), dst_ref=dst(), send_sem=send_sem.at[slot], recv_sem=recv(),
                    device_id=device, device_id_type=MESH,
                )

            key = slot if key is None else key
            sent[key] = build
        sent[key]().start()

    def arrived(dst, recv):
        pltpu.make_async_remote_copy(
            src_ref=dst, dst_ref=dst, send_sem=send_sem.at[0], recv_sem=recv,
            device_id=sibling, device_id_type=MESH,
        ).wait_recv()

    def rows_of(c):
        return tok[pl.ds(pl.multiple_of(c * 128, 128), 128), :]

    def project_keys(c, dst):
        dst[...] = lax.dot_general(rows_of(c), wkv[...], NT, preferred_element_type=jnp.float32)

    def project_queries(c, dst):
        left = rows_of(c)

        def tile(i, _):
            cols = pl.ds(pl.multiple_of(i * 512, 512), 512)
            dst[:, cols] = jnp.dot(left, wq[:, cols], preferred_element_type=jnp.float32)
            return 0

        lax.fori_loop(0, 3, tile, 0)

    def ring_of(own, got, out, came, sems):
        def part(yy, h):
            rows = pl.ds(pl.multiple_of(yy * 32 + h * 16, 16), 16)
            return own[rows, :] + got[rows, :]

        def push(k, value, device):
            out[k] = value.astype(out.dtype)
            send(lambda: out.at[k], lambda: came.at[k], lambda: sems.at[k], device)

        def start():
            push(0, part(yf, 0), up)
            push(1, part(yf, 1), down)
            push(2, part(yp, 1), up)
            push(3, part(ym, 0), down)

        def middle():
            arrived(came.at[0], sems.at[0])
            push(4, part(yp, 0) + came[0].astype(jnp.float32), up)
            arrived(came.at[1], sems.at[1])
            push(5, part(ym, 1) + came[1].astype(jnp.float32), down)

        def end():
            for k in (2, 3, 4, 5):
                arrived(came.at[k], sems.at[k])
            totals = []
            for h, first, second in ((0, 4, 3), (1, 2, 5)):
                total = part(y, h) + came[first].astype(jnp.float32)
                totals.append(total + came[second].astype(jnp.float32))
            return totals

        return start, middle, end

    keys_start, keys_middle, keys_end = ring_of(pok, prk, rks, rkr, rk_sem)
    queries_start, queries_middle, queries_end = ring_of(poq, prq, rqs, rqr, rq_sem)

    loaded("tok", "wkv")
    project_keys(other, psk)
    send(lambda: psk, lambda: prk, lambda: sib_sem.at[0], sibling)
    project_keys(core, pok)
    loaded("wq")
    for name in ("wa", "wu", "wv", "tab0", "tab1"):
        loads[name].start()
    arrived(prk, sib_sem.at[0])
    keys_start()
    project_queries(other, psq)
    send(lambda: psq, lambda: prq, lambda: sib_sem.at[1], sibling)
    keys_middle()
    project_queries(core, poq)
    arrived(prq, sib_sem.at[1])
    queries_start()
    acc[...] = jnp.zeros_like(acc)
    tot[...] = jnp.zeros_like(tot)
    mx[...] = jnp.full_like(mx, FLOOR_SCORE)

    slot_own = 2 * chain + core

    def keys_y(yy, h, n):
        return kb.at[slot_own, pl.ds(pl.multiple_of(yy * 32 + h * 16, 16), n)]

    loaded("kvg", "tabk")
    gain_kv = jnp.concatenate([kvg[k : k + 1, :] for k in range(LAT // 128)], 1)
    for h, total in enumerate(keys_end()):
        latent = normalize(total[:, :LAT], gain_kv)
        turned = rotate(total[:, LAT:], tabk[h])
        rows = pl.ds(pl.multiple_of(y * 32 + h * 16, 16), 16)
        kb[slot_own, rows, :LAT] = latent.astype(jnp.bfloat16)
        kb[slot_own, rows, LAT:] = jnp.concatenate(
            [turned, jnp.zeros_like(turned)], 1
        ).astype(jnp.bfloat16)
    def send_y(yy, h, n, k, device):
        send(lambda: keys_y(yy, h, n), lambda: keys_y(yy, h, n), lambda: ky_sem.at[k], device)

    send_y(y, 0, 32, 0, up)
    send_y(y, 0, 32, 1, down)
    queries_middle()
    arrived(keys_y(ym, 0, 32), ky_sem.at[0])
    send_y(ym, 0, 16, 2, up)
    arrived(keys_y(yp, 0, 32), ky_sem.at[1])
    send_y(yp, 1, 16, 3, down)

    def block(n, p=None):
        if p is None:
            return kb.at[2 * n + core]
        return kb.at[2 * n + core, pl.ds(64 * p, 64)]

    def pass_on(step, n, *devices):
        for k, device in enumerate(devices):
            send(lambda: block(n), lambda: block(n), lambda: kp_sem.at[n, 0], device, (step, k))
        send(lambda: block(n), lambda: block(n), lambda: ks_sem.at[n], sibling, (step, 4))

    def pass_part(step, n, p, device):
        send(lambda: block(n, p), lambda: block(n, p), lambda: kp_sem.at[n, p], device, (step, 5))

    places_of = {step: at(*step) for step in RINGS}

    def whole(n):
        arrived(block(n), kp_sem.at[n, 0])

    def halves(n):
        for p in range(2):
            arrived(block(n, p), kp_sem.at[n, p])

    def relay(u, v):
        n = places_of[u, v]
        if v == 2 or (u, v) == (2, 0):
            halves(n)
        else:
            whole(n)
        if v == 0:
            if u != 2:
                pass_part((u, v), n, 0 if u == 3 else 1, ap if u == 3 else am)
            pass_on((u, v), n, bp, bm)
        else:
            if v != 2:
                pass_part((u, v), n, 0 if v == 3 else 1, bp if v == 3 else bm)
            pass_on((u, v), n)

    arrived(keys_y(yf, 0, 16), ky_sem.at[2])
    arrived(keys_y(yf, 1, 16), ky_sem.at[3])

    loaded("qg")
    gain_q = jnp.concatenate([qg[k : k + 1, :] for k in range(QL // 128)], 1)
    for h, total in enumerate(queries_end()):
        cs[h] = normalize(total, gain_q).astype(jnp.bfloat16)

    def give(s, p, *devices):
        for device in devices:
            send(lambda: cq.at[s, p], lambda: cq.at[s, p], lambda: cq_sem.at[s, p], device)

    def take(s, p):
        arrived(cq.at[s, p], cq_sem.at[s, p])

    send(lambda: cs.at[1 - half], lambda: cq.at[1, piece], lambda: cq_sem.at[1, piece], pair)
    cq[0, piece] = cs[half]
    give(0, piece, up, down, sibling)
    pm, pp, pf = core * 4 + ym, core * 4 + yp, core * 4 + yf
    take(0, pm)
    give(0, pm, up, sibling)
    take(0, pp)
    give(0, pp, sibling)
    take(1, piece)
    give(1, piece, up, down, sibling)
    take(1, pp)
    give(1, pp, down, sibling)
    take(1, pm)
    give(1, pm, sibling)
    take(0, pf)
    give(0, pf, sibling)
    take(1, pf)
    give(1, pf, sibling)
    pass_on((0, 0), places_of[0, 0], ap, am, bp, bm)
    for s in range(2):
        for yy in range(4):
            take(s, other * 4 + yy)

    loaded("wa", "wu", "tab0", "tab1")

    def expand(i, _):
        cols = pl.ds(pl.multiple_of(i * 384, 384), 384)
        rows = cq[...].reshape(256, QL)
        projected = jnp.dot(rows, wu[:, cols], preferred_element_type=jnp.float32)
        table = tabq[...].reshape(256, 2 * ROPE)
        for j in range(2):
            head = 2 * i + j
            base = j * (NOPE + ROPE)
            nope = projected[:, base : base + NOPE].astype(jnp.bfloat16)
            turned = rotate(projected[:, base + NOPE : base + NOPE + ROPE], table)
            turned = jnp.concatenate([turned, jnp.zeros_like(turned)], 1).astype(jnp.bfloat16)
            absorbed = jnp.dot(nope, wa[head], preferred_element_type=jnp.float32)
            absorbed = absorbed.astype(jnp.bfloat16)
            places = pl.ds(pl.multiple_of(head * 128, 128), 128)
            for s in range(2):
                qb[s, places, :LAT] = absorbed[s * 128 : s * 128 + 128]
                qb[s, places, LAT:] = turned[s * 128 : s * 128 + 128]
        return 0

    lax.fori_loop(0, HEADS // 4, expand, 0)
    for u, v in RINGS[1:5]:
        relay(u, v)
    lax.fori_loop(HEADS // 4, HEADS // 2, expand, 0)
    for u, v in RINGS[5:11]:
        relay(u, v)

    def meet(c):
        for k in range(4):
            n = 4 * (c % 4) + k
            arrived(kb.at[2 * n + other], ks_sem.at[n])

    def second_rows():
        for u, v in RINGS[11:15]:
            relay(u, v)
        meet(z + 1)
        meet(z + 3)

    def last_row():
        relay(2, 2)
        meet(z + 2)

    def turn(n, side):
        cols = pl.ds(pl.multiple_of((n % 4) * 256 + side * 128, 128), 128)
        kt[n // 4, :LAT, cols] = kb[2 * n + side, :, :LAT].T

    def turn_own(steps):
        for u, v in steps:
            turn(at(u, v), core)

    def turn_other(steps):
        for u, v in steps:
            n = at(u, v)
            arrived(kb.at[2 * n + other], ks_sem.at[n])
            turn(n, other)

    def whole(n):
        arrived(block(n), kp_sem.at[n, 0])

    def halves(n):
        for p in range(2):
            arrived(block(n, p), kp_sem.at[n, p])

    token = lax.broadcasted_iota(jnp.int32, (512, 1), 0) & 127
    place = ((token >> 4) << 5) + (token & 15) + half * 16
    key_iota = lax.broadcasted_iota(jnp.int32, (1, 512), 1)
    early = 1 - z // 2
    n_own, n_far = chain // 2 + 1, mirror // 2 + 1
    ends = (n_own + early * (n_far - n_own), n_own + n_far, 18 - n_own, 18)
    ends = (ends[0], ends[0] + n_far, ends[2], ends[3])
    own_steps = 2 - (1 - early) * (1 - (chain % 4) // 2)

    def plan(t):
        p1 = (t >= ends[0]).astype(jnp.int32)
        p2 = (t >= ends[1]).astype(jnp.int32)
        p3 = (t >= ends[2]).astype(jnp.int32)
        p = p1 + p2 + p3
        j = t - p1 * ends[0] - p2 * (ends[1] - ends[0]) - p3 * (ends[2] - ends[1])
        s = jnp.where(p == 0, early, jnp.where(p == 1, 1, jnp.where(p == 2, 1 - early, 0)))
        r = jnp.where(p == 0, 0, jnp.where(p == 1, early, jnp.where(p == 2, 1 - early, 1)))
        chunks = n_own + s * (n_far - n_own)
        ahead = (2 * z + j) % chunks
        back = chunks - 1 - j
        c = back + s * early * (ahead - back)
        return s, r, c, c == chunks - 1

    def rows_of_pass(r):
        return pl.ds(pl.multiple_of(r * 512, 512), 512)

    def score(t, dst):
        s, r, c, _ = plan(t)
        keys = kb[pl.ds(4 * c, 4)].reshape(512, KEYW)
        dst[...] = lax.dot_general(
            qb[s, rows_of_pass(r), :], keys, NT, preferred_element_type=jnp.float32
        )

    def hide(t, dst):
        s, _, c, last = plan(t)

        @pl.when(last)
        def _():
            blk = chain + s * (mirror - chain)
            visible = key_iota + 512 * c <= place + 256 * blk
            dst[...] = jnp.where(visible, dst[...], FLOOR_SCORE)

    def out_cols(r):
        return pl.ds(pl.multiple_of(r * 512, 512), 512)

    def out_copy(r):
        return pltpu.make_async_remote_copy(
            src_ref=ob.at[1, :, :, out_cols(r)], dst_ref=out_h.at[:, half, :, out_cols(r)],
            send_sem=outs_sem.at[r], recv_sem=out_sem.at[r], device_id=pair, device_id_type=MESH,
        )

    def own_copy(r):
        return pltpu.make_async_copy(
            ob.at[0, :, :, out_cols(r)], out_h.at[:, half, :, out_cols(r)], own_sem.at[r]
        )

    def step(t, now, later):
        s, r, c, _ = plan(t)
        rows = rows_of_pass(r)
        score(jnp.minimum(t + 1, 17), later)
        parts = [now[:, k : k + 128] * SCALE2 for k in range(0, 512, 128)]
        before = mx[s, rows, :]
        top = jnp.max(functools.reduce(jnp.maximum, parts), 1, keepdims=True)
        peak = jnp.maximum(before, top)
        shrink = jnp.exp2(before - peak)
        weights = [jnp.exp2(p - peak) for p in parts]
        mx[s, rows, :] = peak
        tot[s, rows, :] = tot[s, rows, :] * shrink + sum(weights[1:], weights[0])
        weights = jnp.concatenate([w.astype(jnp.bfloat16) for w in weights], 1)
        latent = kb[pl.ds(4 * c, 4), :, :LAT].reshape(512, LAT)
        mixed = jnp.dot(weights, latent, preferred_element_type=jnp.float32)
        shrink = jnp.concatenate([shrink] * (LAT // 128), 1)
        acc[s, rows, :] = acc[s, rows, :] * shrink + mixed
        hide(jnp.minimum(t + 1, 17), later)

        @pl.when((t + 1 == ends[0]) | (t + 1 == ends[1]) | (t + 1 == ends[2]) | (t + 1 == ends[3]))
        def _():
            for k in range(4):
                part = pl.ds(pl.multiple_of(r * 512 + k * 128, 128), 128)
                total = jnp.sum(tot[s, part, :], 1, keepdims=True)
                mixed = (acc[s, part, :] * (1.0 / total)).astype(jnp.bfloat16)
                value = jnp.dot(mixed, wv[4 * r + k], preferred_element_type=jnp.float32)
                ob[s, :, :, part] = value.astype(jnp.bfloat16).reshape(8, 16, VH)

            @pl.when(s == 1)
            def _():
                out_copy(r).start()

            @pl.when(s == 0)
            def _():
                own_copy(r).start()

    loaded("wv")
    meet(z)
    score(0, first)
    hide(0, first)

    def two_steps(i, _):
        @pl.when((i == 0) & (own_steps == 1))
        def _():
            second_rows()

        @pl.when(i == 1)
        def _():
            last_row()

        step(2 * i, first, second)

        @pl.when((i == 0) & (own_steps == 2))
        def _():
            second_rows()

        step(2 * i + 1, second, first)
        return 0

    lax.fori_loop(0, 9, two_steps, 0)
    for j in range(2):
        rows = pl.ds(pl.multiple_of(tp * 16, 16), 16)
        cache_ref[j] = kb[slot_ref[j], rows, :][:, :KV]
    for r in range(2):
        own_copy(r).wait()
        out_copy(r).wait_send()
        arrived(out_h.at[:, 1 - half, :, out_cols(r)], out_sem.at[r])
    for build in sent.values():
        build().wait_send()


def hand_over(att_h, cache_h, att_out, cache_out, att, cache, sem):
    pieces = [(cache_h, cache, cache_out)]
    for k in range(4):
        rows = pl.ds(64 * k, 64)
        pieces.append((att_h.at[rows], att.at[rows], att_out.at[rows]))
    into = [pltpu.make_async_copy(p[0], p[1], sem.at[0, k]) for k, p in enumerate(pieces)]
    out = [pltpu.make_async_copy(p[1], p[2], sem.at[1, k]) for k, p in enumerate(pieces)]
    for copy in into:
        copy.start()
    for first, second in zip(into, out):
        first.wait()
        second.start()
    for copy in out:
        copy.wait()


def per_device(tokens, w_down_q, w_down_kv, q_gain, kv_gain, w_up_q, w_absorb, w_value, slot_block):
    bf16, f32 = jnp.bfloat16, jnp.float32
    table = jnp.asarray(rotary_tables())
    hbm = pl.BlockSpec(memory_space=pl.ANY)
    dma = pltpu.SemaphoreType.DMA
    attended, cache = pl.pallas_call(
        kernel,
        out_shape=(
            jax.ShapeDtypeStruct((8, 2, 16, HEADS * VH), bf16),
            jax.ShapeDtypeStruct((2, 16, KV), bf16),
        ),
        in_specs=[hbm] * 8 + [pl.BlockSpec(memory_space=pltpu.SMEM), hbm],
        out_specs=(hbm, pl.BlockSpec(memory_space=pltpu.VMEM)),
        scratch_shapes=[
            pltpu.VMEM((256, 896), bf16),
            pltpu.VMEM((896, QL), bf16),
            pltpu.VMEM((KV, 896), bf16),
            pltpu.VMEM((QL // 128, 128), f32),
            pltpu.VMEM((LAT // 128, 128), f32),
            pltpu.VMEM((QL, HEADS * (NOPE + ROPE)), bf16),
            pltpu.VMEM((HEADS, NOPE, LAT), bf16),
            pltpu.VMEM((HEADS, LAT, VH), bf16),
            pltpu.VMEM((2, 16, 2 * ROPE), f32),
            pltpu.VMEM((2, 8, 16, 2 * ROPE), f32),
            pltpu.VMEM((128, KV), f32),
            pltpu.VMEM((128, KV), f32),
            pltpu.VMEM((128, KV), f32),
            pltpu.VMEM((128, QL), f32),
            pltpu.VMEM((128, QL), f32),
            pltpu.VMEM((128, QL), f32),
            pltpu.VMEM((6, 16, KV), bf16),
            pltpu.VMEM((6, 16, KV), bf16),
            pltpu.VMEM((6, 16, QL), f32),
            pltpu.VMEM((6, 16, QL), f32),
            pltpu.VMEM((2, 16, QL), bf16),
            pltpu.VMEM((2, 8, 16, QL), bf16),
            pltpu.VMEM((32, 128, KEYW), bf16),
            pltpu.VMEM((2, HEADS * 128, KEYW), bf16),
            pltpu.VMEM((512, 512), f32),
            pltpu.VMEM((512, 512), f32),
            pltpu.VMEM((2, HEADS * 128, LAT), f32),
            pltpu.VMEM((2, HEADS * 128, 128), f32),
            pltpu.VMEM((2, HEADS * 128, 128), f32),
            pltpu.VMEM((2, 8, 16, HEADS * VH), bf16),
            dma((11,)),
            dma((N_SEND,)),
            dma((2,)),
            dma((6,)),
            dma((6,)),
            dma((2, 8)),
            dma((4,)),
            dma((16, 2)),
            dma((16,)),
            dma((2,)),
            dma((2,)),
            dma((2,)),
        ],
        compiler_params=pltpu.CompilerParams(
            collective_id=0, has_side_effects=True, vmem_limit_bytes=56 * 2**20
        ),
    )(
        tokens, w_down_q, w_down_kv.T, q_gain.reshape(-1, 128), kv_gain.reshape(-1, 128),
        w_up_q, w_absorb, w_value, slot_block, table,
    )
    attended = attended.reshape(256, HEADS * VH)
    return pl.pallas_call(
        hand_over,
        out_shape=(
            jax.ShapeDtypeStruct(attended.shape, bf16),
            jax.ShapeDtypeStruct(cache.shape, bf16),
        ),
        in_specs=[hbm, hbm],
        out_specs=(hbm, hbm),
        scratch_shapes=[
            pltpu.VMEM(attended.shape, bf16),
            pltpu.VMEM(cache.shape, bf16),
            dma((2, 5)),
        ],
        compiler_params=pltpu.CompilerParams(vmem_limit_bytes=60 * 2**20),
    )(attended, cache)


def solution(mesh):
    placed = (
        P("chain", "tp"),
        P("tp", None),
        P("tp", None),
        P(),
        P(),
        P(None, "tp"),
        P("tp", None, None),
        P("tp", None, None),
        P("chain"),
    )
    return jax.shard_map(
        per_device,
        mesh=mesh,
        in_specs=placed,
        out_specs=(P("chain", "tp"), P("chain", "tp", None)),
        check_vma=False,
    )
```

```python
import functools
import math

import jax
import jax.numpy as jnp
import numpy as np
from jax import lax
from jax.experimental import pallas as pl
from jax.experimental.pallas import tpu as pltpu
from jax.sharding import PartitionSpec as P

MESH = pl.DeviceIdType.MESH
ROPE_BASE = 50000.0
FLOOR_SCORE = -1e30
QL, LAT, ROPE, NOPE, VH, HEADS = 1536, 512, 64, 128, 128, 8
KEYW = 640
KV = LAT + ROPE
SCALE2 = (NOPE + ROPE) ** -0.5 * math.log2(math.e)
NT = (((1,), (1,)), ((), ()))
N_SEND = 80
RINGS = (
    (0, 0), (3, 0), (1, 0), (0, 3), (0, 1), (2, 0), (0, 2), (3, 3), (3, 1), (1, 3), (1, 1),
    (2, 3), (2, 1), (3, 2), (1, 2), (2, 2),
)


def rotary_tables():
    inverse = ROPE_BASE ** (-2.0 * np.arange(ROPE // 2) / ROPE)
    angles = np.arange(4096)[:, None] * inverse[None, :]
    cosine = np.concatenate([np.cos(angles), np.cos(angles)], 1)
    sine = np.concatenate([-np.sin(angles), np.sin(angles)], 1)
    both = np.concatenate([cosine, sine], 1).astype(np.float32)
    return both.reshape(16, 8, 2, 16, 2 * ROPE)


def rotate(values, table):
    half = ROPE // 2
    swapped = jnp.concatenate([values[:, half:], values[:, :half]], 1)
    return values * table[:, :ROPE] + swapped * table[:, ROPE:]


def normalize(values, gain):
    return values * lax.rsqrt(jnp.mean(values * values, -1, keepdims=True) + 1e-06) * gain


def kernel(
    tok_h, wq_h, wkv_h, qg_h, kvg_h, wu_h, wa_h, wv_h, slot_ref, tab_h,
    out_h, cache_ref,
    tok, wq, wkv, qg, kvg, wu, wa, wv, tabk, tabq,
    psk, pok, prk, psq, poq, prq, rks, rkr, rqs, rqr, cs, cq, kb, qb, first, second, acc, mx, tot, ob,
    load_sem, send_sem, sib_sem, rk_sem, rq_sem, cq_sem, ky_sem, kp_sem, ks_sem, out_sem, outs_sem, own_sem,
):
    chain = lax.axis_index("chain")
    tp = lax.axis_index("tp")
    z, x = chain // 4, chain % 4
    y, core = tp // 2, tp % 2
    other = 1 - core
    mirror = 15 - chain
    half = chain // 8
    piece = core * 4 + y
    yp, ym, yf = (y + 1) % 4, (y + 3) % 4, (y + 2) % 4
    sibling = {"chain": chain, "tp": 2 * y + other}
    up = {"chain": chain, "tp": 2 * yp + core}
    down = {"chain": chain, "tp": 2 * ym + core}
    pair = {"chain": mirror, "tp": tp}
    a = x + core * (z - x)
    b = z + core * (x - z)
    stride_a, stride_b = 1 + 3 * core, 4 - 3 * core

    def at(da, db):
        return ((a + da) % 4) * stride_a + ((b + db) % 4) * stride_b

    ap = {"chain": at(1, 0), "tp": tp}
    am = {"chain": at(3, 0), "tp": tp}
    bp = {"chain": at(0, 1), "tp": tp}
    bm = {"chain": at(0, 3), "tp": tp}

    loads = {}
    for k, (name, src, dst) in enumerate(
        [
            ("tok", tok_h, tok), ("wkv", wkv_h, wkv), ("wq", wq_h, wq), ("kvg", kvg_h, kvg),
            ("qg", qg_h, qg), ("tabk", tab_h.at[chain, piece], tabk), ("wa", wa_h, wa),
            ("wu", wu_h, wu), ("wv", wv_h, wv), ("tab0", tab_h.at[chain, :, half], tabq.at[0]),
            ("tab1", tab_h.at[mirror, :, half], tabq.at[1]),
        ]
    ):
        loads[name] = pltpu.make_async_copy(src, dst, load_sem.at[k])
        if k < 6:
            loads[name].start()

    def loaded(*names):
        for name in names:
            loads[name].wait()

    barrier = pltpu.get_barrier_semaphore()
    partners = (sibling, up, down, pair, ap, am, bp, bm)
    for device in partners:
        pl.semaphore_signal(barrier, inc=1, device_id=device, device_id_type=MESH)
    pl.semaphore_wait(barrier, len(partners))

    sent = {}

    def send(src, dst, recv, device, key=None):
        if key is None or key not in sent:
            slot = len(sent)

            def build():
                return pltpu.make_async_remote_copy(
                    src_ref=src(), dst_ref=dst(), send_sem=send_sem.at[slot], recv_sem=recv(),
                    device_id=device, device_id_type=MESH,
                )

            key = slot if key is None else key
            sent[key] = build
        sent[key]().start()

    def arrived(dst, recv):
        pltpu.make_async_remote_copy(
            src_ref=dst, dst_ref=dst, send_sem=send_sem.at[0], recv_sem=recv,
            device_id=sibling, device_id_type=MESH,
        ).wait_recv()

    def rows_of(c):
        return tok[pl.ds(pl.multiple_of(c * 128, 128), 128), :]

    def project_keys(c, dst):
        dst[...] = lax.dot_general(rows_of(c), wkv[...], NT, preferred_element_type=jnp.float32)

    def project_queries(c, dst):
        left = rows_of(c)

        def tile(i, _):
            cols = pl.ds(pl.multiple_of(i * 512, 512), 512)
            dst[:, cols] = jnp.dot(left, wq[:, cols], preferred_element_type=jnp.float32)
            return 0

        lax.fori_loop(0, 3, tile, 0)

    def ring_of(own, got, out, came, sems):
        def part(yy, h):
            rows = pl.ds(pl.multiple_of(yy * 32 + h * 16, 16), 16)
            return own[rows, :] + got[rows, :]

        def push(k, value, device):
            out[k] = value.astype(out.dtype)
            send(lambda: out.at[k], lambda: came.at[k], lambda: sems.at[k], device)

        def start():
            push(0, part(yf, 0), up)
            push(1, part(yf, 1), down)
            push(2, part(yp, 1), up)
            push(3, part(ym, 0), down)

        def middle():
            arrived(came.at[0], sems.at[0])
            push(4, part(yp, 0) + came[0].astype(jnp.float32), up)
            arrived(came.at[1], sems.at[1])
            push(5, part(ym, 1) + came[1].astype(jnp.float32), down)

        def end():
            for k in (2, 3, 4, 5):
                arrived(came.at[k], sems.at[k])
            totals = []
            for h, first, second in ((0, 4, 3), (1, 2, 5)):
                total = part(y, h) + came[first].astype(jnp.float32)
                totals.append(total + came[second].astype(jnp.float32))
            return totals

        return start, middle, end

    keys_start, keys_middle, keys_end = ring_of(pok, prk, rks, rkr, rk_sem)
    queries_start, queries_middle, queries_end = ring_of(poq, prq, rqs, rqr, rq_sem)

    loaded("tok", "wkv")
    project_keys(other, psk)
    send(lambda: psk, lambda: prk, lambda: sib_sem.at[0], sibling)
    project_keys(core, pok)
    loaded("wq")
    for name in ("wa", "wu", "wv", "tab0", "tab1"):
        loads[name].start()
    arrived(prk, sib_sem.at[0])
    keys_start()
    project_queries(other, psq)
    send(lambda: psq, lambda: prq, lambda: sib_sem.at[1], sibling)
    keys_middle()
    project_queries(core, poq)

    slot_own = 2 * chain + core

    def keys_y(yy, h, n):
        return kb.at[slot_own, pl.ds(pl.multiple_of(yy * 32 + h * 16, 16), n)]

    loaded("kvg", "tabk")
    gain_kv = jnp.concatenate([kvg[k : k + 1, :] for k in range(LAT // 128)], 1)
    for h, total in enumerate(keys_end()):
        latent = normalize(total[:, :LAT], gain_kv)
        turned = rotate(total[:, LAT:], tabk[h])
        rows = pl.ds(pl.multiple_of(y * 32 + h * 16, 16), 16)
        kb[slot_own, rows, :LAT] = latent.astype(jnp.bfloat16)
        kb[slot_own, rows, LAT:] = jnp.concatenate(
            [turned, jnp.zeros_like(turned)], 1
        ).astype(jnp.bfloat16)
    def send_y(yy, h, n, k, device):
        send(lambda: keys_y(yy, h, n), lambda: keys_y(yy, h, n), lambda: ky_sem.at[k], device)

    send_y(y, 0, 32, 0, up)
    send_y(y, 0, 32, 1, down)
    arrived(prq, sib_sem.at[1])
    queries_start()
    arrived(keys_y(ym, 0, 32), ky_sem.at[0])
    send_y(ym, 0, 16, 2, up)
    arrived(keys_y(yp, 0, 32), ky_sem.at[1])
    send_y(yp, 1, 16, 3, down)

    def block(n, p=None):
        if p is None:
            return kb.at[2 * n + core]
        return kb.at[2 * n + core, pl.ds(64 * p, 64)]

    def pass_on(step, n, *devices):
        for k, device in enumerate(devices):
            send(lambda: block(n), lambda: block(n), lambda: kp_sem.at[n, 0], device, (step, k))
        send(lambda: block(n), lambda: block(n), lambda: ks_sem.at[n], sibling, (step, 4))

    def pass_part(step, n, p, device):
        send(lambda: block(n, p), lambda: block(n, p), lambda: kp_sem.at[n, p], device, (step, 5))

    places_of = {step: at(*step) for step in RINGS}

    def whole(n):
        arrived(block(n), kp_sem.at[n, 0])

    def halves(n):
        for p in range(2):
            arrived(block(n, p), kp_sem.at[n, p])

    def relay(u, v):
        n = places_of[u, v]
        if v == 2 or (u, v) == (2, 0):
            halves(n)
        else:
            whole(n)
        if v == 0:
            if u != 2:
                pass_part((u, v), n, 0 if u == 3 else 1, ap if u == 3 else am)
            pass_on((u, v), n, bp, bm)
        else:
            if v != 2:
                pass_part((u, v), n, 0 if v == 3 else 1, bp if v == 3 else bm)
            pass_on((u, v), n)

    arrived(keys_y(yf, 0, 16), ky_sem.at[2])
    arrived(keys_y(yf, 1, 16), ky_sem.at[3])
    pass_on((0, 0), places_of[0, 0], ap, am, bp, bm)
    queries_middle()
    acc[...] = jnp.zeros_like(acc)
    tot[...] = jnp.zeros_like(tot)
    mx[...] = jnp.full_like(mx, FLOOR_SCORE)

    loaded("qg")
    gain_q = jnp.concatenate([qg[k : k + 1, :] for k in range(QL // 128)], 1)
    for h, total in enumerate(queries_end()):
        cs[h] = normalize(total, gain_q).astype(jnp.bfloat16)

    def give(s, p, *devices):
        for device in devices:
            send(lambda: cq.at[s, p], lambda: cq.at[s, p], lambda: cq_sem.at[s, p], device)

    def take(s, p):
        arrived(cq.at[s, p], cq_sem.at[s, p])

    send(lambda: cs.at[1 - half], lambda: cq.at[1, piece], lambda: cq_sem.at[1, piece], pair)
    cq[0, piece] = cs[half]
    give(0, piece, up, down, sibling)
    pm, pp, pf = core * 4 + ym, core * 4 + yp, core * 4 + yf
    for u, v in RINGS[1:5]:
        relay(u, v)
    take(1, piece)
    give(1, piece, up, down, sibling)
    take(0, pm)
    give(0, pm, up, sibling)
    take(0, pp)
    give(0, pp, sibling)
    take(1, pp)
    give(1, pp, down, sibling)
    take(1, pm)
    give(1, pm, sibling)
    for u, v in RINGS[5:7]:
        relay(u, v)
    take(0, pf)
    give(0, pf, sibling)
    take(1, pf)
    give(1, pf, sibling)
    for s in range(2):
        for yy in range(4):
            take(s, other * 4 + yy)

    loaded("wa", "wu", "tab0", "tab1")

    def expand(i, _):
        cols = pl.ds(pl.multiple_of(i * 384, 384), 384)
        rows = cq[...].reshape(256, QL)
        projected = jnp.dot(rows, wu[:, cols], preferred_element_type=jnp.float32)
        table = tabq[...].reshape(256, 2 * ROPE)
        for j in range(2):
            head = 2 * i + j
            base = j * (NOPE + ROPE)
            nope = projected[:, base : base + NOPE].astype(jnp.bfloat16)
            turned = rotate(projected[:, base + NOPE : base + NOPE + ROPE], table)
            turned = jnp.concatenate([turned, jnp.zeros_like(turned)], 1).astype(jnp.bfloat16)
            absorbed = jnp.dot(nope, wa[head], preferred_element_type=jnp.float32)
            absorbed = absorbed.astype(jnp.bfloat16)
            places = pl.ds(pl.multiple_of(head * 128, 128), 128)
            for s in range(2):
                qb[s, places, :LAT] = absorbed[s * 128 : s * 128 + 128]
                qb[s, places, LAT:] = turned[s * 128 : s * 128 + 128]
        return 0

    lax.fori_loop(0, HEADS // 4, expand, 0)
    for u, v in RINGS[7:11]:
        relay(u, v)
    lax.fori_loop(HEADS // 4, HEADS // 2, expand, 0)

    def meet(c):
        for k in range(4):
            n = 4 * (c % 4) + k
            arrived(kb.at[2 * n + other], ks_sem.at[n])

    def second_rows():
        for u, v in RINGS[11:15]:
            relay(u, v)
        meet(z + 1)
        meet(z + 3)

    def last_row():
        relay(2, 2)
        meet(z + 2)

    def turn(n, side):
        cols = pl.ds(pl.multiple_of((n % 4) * 256 + side * 128, 128), 128)
        kt[n // 4, :LAT, cols] = kb[2 * n + side, :, :LAT].T

    def turn_own(steps):
        for u, v in steps:
            turn(at(u, v), core)

    def turn_other(steps):
        for u, v in steps:
            n = at(u, v)
            arrived(kb.at[2 * n + other], ks_sem.at[n])
            turn(n, other)

    def whole(n):
        arrived(block(n), kp_sem.at[n, 0])

    def halves(n):
        for p in range(2):
            arrived(block(n, p), kp_sem.at[n, p])

    token = lax.broadcasted_iota(jnp.int32, (512, 1), 0) & 127
    place = ((token >> 4) << 5) + (token & 15) + half * 16
    key_iota = lax.broadcasted_iota(jnp.int32, (1, 512), 1)
    n_own, n_far = chain // 2 + 1, mirror // 2 + 1
    first_z = (z == 0).astype(jnp.int32)
    segments = []
    for k, offset in enumerate((0, 1, 3, 2)):
        c = (z + offset) % 4
        segments.append((1, c, jnp.clip(n_far - 2 * c, 0, 2)))
        segments.append((0, c, jnp.clip(n_own - 2 * c, 0, 2) * (1 - first_z * (k == 0))))
    segments.append((0, z, jnp.clip(n_own - 2 * z, 0, 2) * first_z))
    starts, final = [jnp.int32(0)], [jnp.int32(0), jnp.int32(0)]
    for k, (s, _, chunks) in enumerate(segments):
        starts.append(starts[-1] + 2 * chunks)
        final[s] = jnp.where(chunks > 0, k, final[s])

    def plan(t):
        s, c, r, done = jnp.int32(0), jnp.int32(0), jnp.int32(0), jnp.int32(0)
        for k, (side, row, chunks) in enumerate(segments):
            inside = (t >= starts[k]) & (t < starts[k + 1])
            place_in = t - starts[k]
            pairs = chunks - 1
            s = jnp.where(inside, side, s)
            r = jnp.where(inside, jnp.where(chunks == 2, place_in // 2, place_in), r)
            c = jnp.where(inside, 2 * row + pairs * (place_in % 2), c)
            ended = (final[side] == k).astype(jnp.int32) * (1 - pairs * (1 - place_in % 2))
            done = jnp.where(inside, ended, done)
        chunks = n_own + s * (n_far - n_own)
        return s, r, c, c == chunks - 1, done == 1

    def rows_of_pass(r):
        return pl.ds(pl.multiple_of(r * 512, 512), 512)

    def score(t, dst):
        s, r, c, _, _ = plan(t)
        keys = kb[pl.ds(4 * c, 4)].reshape(512, KEYW)
        dst[...] = lax.dot_general(
            qb[s, rows_of_pass(r), :], keys, NT, preferred_element_type=jnp.float32
        )

    def hide(t, dst):
        s, _, c, last, _ = plan(t)

        @pl.when(last)
        def _():
            blk = chain + s * (mirror - chain)
            visible = key_iota + 512 * c <= place + 256 * blk
            dst[...] = jnp.where(visible, dst[...], FLOOR_SCORE)

    def out_cols(r):
        return pl.ds(pl.multiple_of(r * 512, 512), 512)

    def out_copy(r):
        return pltpu.make_async_remote_copy(
            src_ref=ob.at[1, :, :, out_cols(r)], dst_ref=out_h.at[:, half, :, out_cols(r)],
            send_sem=outs_sem.at[r], recv_sem=out_sem.at[r], device_id=pair, device_id_type=MESH,
        )

    def own_copy(r):
        return pltpu.make_async_copy(
            ob.at[0, :, :, out_cols(r)], out_h.at[:, half, :, out_cols(r)], own_sem.at[r]
        )

    def step(t, now, later):
        s, r, c, _, done = plan(t)
        rows = rows_of_pass(r)
        score(jnp.minimum(t + 1, 17), later)
        parts = [now[:, k : k + 128] * SCALE2 for k in range(0, 512, 128)]
        before = mx[s, rows, :]
        top = jnp.max(functools.reduce(jnp.maximum, parts), 1, keepdims=True)
        peak = jnp.maximum(before, top)
        shrink = jnp.exp2(before - peak)
        weights = [jnp.exp2(p - peak) for p in parts]
        mx[s, rows, :] = peak
        tot[s, rows, :] = tot[s, rows, :] * shrink + sum(weights[1:], weights[0])
        weights = jnp.concatenate([w.astype(jnp.bfloat16) for w in weights], 1)
        latent = kb[pl.ds(4 * c, 4), :, :LAT].reshape(512, LAT)
        mixed = jnp.dot(weights, latent, preferred_element_type=jnp.float32)
        shrink = jnp.concatenate([shrink] * (LAT // 128), 1)
        acc[s, rows, :] = acc[s, rows, :] * shrink + mixed
        hide(jnp.minimum(t + 1, 17), later)

        @pl.when(done)
        def _():
            for k in range(4):
                part = pl.ds(pl.multiple_of(r * 512 + k * 128, 128), 128)
                total = jnp.sum(tot[s, part, :], 1, keepdims=True)
                mixed = (acc[s, part, :] * (1.0 / total)).astype(jnp.bfloat16)
                value = jnp.dot(mixed, wv[4 * r + k], preferred_element_type=jnp.float32)
                ob[s, :, :, part] = value.astype(jnp.bfloat16).reshape(8, 16, VH)

            @pl.when(s == 1)
            def _():
                out_copy(r).start()

            @pl.when(s == 0)
            def _():
                own_copy(r).start()

    loaded("wv")
    meet(z)
    score(0, first)
    hide(0, first)

    def two_steps(i, _):
        for k, (now, later) in enumerate(((first, second), (second, first))):
            t = 2 * i + k

            @pl.when(t + 1 == starts[2])
            def _():
                second_rows()

            @pl.when(t + 1 == starts[6])
            def _():
                last_row()

            step(t, now, later)
        return 0

    lax.fori_loop(0, 9, two_steps, 0)
    for j in range(2):
        rows = pl.ds(pl.multiple_of(tp * 16, 16), 16)
        cache_ref[j] = kb[slot_ref[j], rows, :][:, :KV]
    for r in range(2):
        own_copy(r).wait()
        out_copy(r).wait_send()
        arrived(out_h.at[:, 1 - half, :, out_cols(r)], out_sem.at[r])
    for build in sent.values():
        build().wait_send()


def hand_over(att_h, cache_h, att_out, cache_out, att, cache, sem):
    pieces = [(cache_h, cache, cache_out)]
    for k in range(4):
        rows = pl.ds(64 * k, 64)
        pieces.append((att_h.at[rows], att.at[rows], att_out.at[rows]))
    into = [pltpu.make_async_copy(p[0], p[1], sem.at[0, k]) for k, p in enumerate(pieces)]
    out = [pltpu.make_async_copy(p[1], p[2], sem.at[1, k]) for k, p in enumerate(pieces)]
    for copy in into:
        copy.start()
    for first, second in zip(into, out):
        first.wait()
        second.start()
    for copy in out:
        copy.wait()


def per_device(tokens, w_down_q, w_down_kv, q_gain, kv_gain, w_up_q, w_absorb, w_value, slot_block):
    bf16, f32 = jnp.bfloat16, jnp.float32
    table = jnp.asarray(rotary_tables())
    hbm = pl.BlockSpec(memory_space=pl.ANY)
    dma = pltpu.SemaphoreType.DMA
    attended, cache = pl.pallas_call(
        kernel,
        out_shape=(
            jax.ShapeDtypeStruct((8, 2, 16, HEADS * VH), bf16),
            jax.ShapeDtypeStruct((2, 16, KV), bf16),
        ),
        in_specs=[hbm] * 8 + [pl.BlockSpec(memory_space=pltpu.SMEM), hbm],
        out_specs=(hbm, pl.BlockSpec(memory_space=pltpu.VMEM)),
        scratch_shapes=[
            pltpu.VMEM((256, 896), bf16),
            pltpu.VMEM((896, QL), bf16),
            pltpu.VMEM((KV, 896), bf16),
            pltpu.VMEM((QL // 128, 128), f32),
            pltpu.VMEM((LAT // 128, 128), f32),
            pltpu.VMEM((QL, HEADS * (NOPE + ROPE)), bf16),
            pltpu.VMEM((HEADS, NOPE, LAT), bf16),
            pltpu.VMEM((HEADS, LAT, VH), bf16),
            pltpu.VMEM((2, 16, 2 * ROPE), f32),
            pltpu.VMEM((2, 8, 16, 2 * ROPE), f32),
            pltpu.VMEM((128, KV), f32),
            pltpu.VMEM((128, KV), f32),
            pltpu.VMEM((128, KV), f32),
            pltpu.VMEM((128, QL), f32),
            pltpu.VMEM((128, QL), f32),
            pltpu.VMEM((128, QL), f32),
            pltpu.VMEM((6, 16, KV), bf16),
            pltpu.VMEM((6, 16, KV), bf16),
            pltpu.VMEM((6, 16, QL), f32),
            pltpu.VMEM((6, 16, QL), f32),
            pltpu.VMEM((2, 16, QL), bf16),
            pltpu.VMEM((2, 8, 16, QL), bf16),
            pltpu.VMEM((32, 128, KEYW), bf16),
            pltpu.VMEM((2, HEADS * 128, KEYW), bf16),
            pltpu.VMEM((512, 512), f32),
            pltpu.VMEM((512, 512), f32),
            pltpu.VMEM((2, HEADS * 128, LAT), f32),
            pltpu.VMEM((2, HEADS * 128, 128), f32),
            pltpu.VMEM((2, HEADS * 128, 128), f32),
            pltpu.VMEM((2, 8, 16, HEADS * VH), bf16),
            dma((11,)),
            dma((N_SEND,)),
            dma((2,)),
            dma((6,)),
            dma((6,)),
            dma((2, 8)),
            dma((4,)),
            dma((16, 2)),
            dma((16,)),
            dma((2,)),
            dma((2,)),
            dma((2,)),
        ],
        compiler_params=pltpu.CompilerParams(
            collective_id=0, has_side_effects=True, vmem_limit_bytes=56 * 2**20
        ),
    )(
        tokens, w_down_q, w_down_kv.T, q_gain.reshape(-1, 128), kv_gain.reshape(-1, 128),
        w_up_q, w_absorb, w_value, slot_block, table,
    )
    attended = attended.reshape(256, HEADS * VH)
    return pl.pallas_call(
        hand_over,
        out_shape=(
            jax.ShapeDtypeStruct(attended.shape, bf16),
            jax.ShapeDtypeStruct(cache.shape, bf16),
        ),
        in_specs=[hbm, hbm],
        out_specs=(hbm, hbm),
        scratch_shapes=[
            pltpu.VMEM(attended.shape, bf16),
            pltpu.VMEM(cache.shape, bf16),
            dma((2, 5)),
        ],
        compiler_params=pltpu.CompilerParams(vmem_limit_bytes=60 * 2**20),
    )(attended, cache)


def solution(mesh):
    placed = (
        P("chain", "tp"),
        P("tp", None),
        P("tp", None),
        P(),
        P(),
        P(None, "tp"),
        P("tp", None, None),
        P("tp", None, None),
        P("chain"),
    )
    return jax.shard_map(
        per_device,
        mesh=mesh,
        in_specs=placed,
        out_specs=(P("chain", "tp"), P("chain", "tp", None)),
        check_vma=False,
    )
```

```python
import functools
import math

import jax
import jax.numpy as jnp
import numpy as np
from jax import lax
from jax.experimental import pallas as pl
from jax.experimental.pallas import tpu as pltpu
from jax.sharding import PartitionSpec as P

MESH = pl.DeviceIdType.MESH
ROPE_BASE = 50000.0
FLOOR_SCORE = -1e30
QL, LAT, ROPE, NOPE, VH, HEADS = 1536, 512, 64, 128, 128, 8
KEYW = 640
KV = LAT + ROPE
SCALE2 = (NOPE + ROPE) ** -0.5 * math.log2(math.e)
NT = (((1,), (1,)), ((), ()))
N_SEND = 80
RINGS = (
    (0, 0), (3, 0), (1, 0), (0, 3), (0, 1), (2, 0), (0, 2), (3, 3), (3, 1), (1, 3), (1, 1),
    (2, 3), (2, 1), (3, 2), (1, 2), (2, 2),
)


def rotary_tables():
    inverse = ROPE_BASE ** (-2.0 * np.arange(ROPE // 2) / ROPE)
    angles = np.arange(4096)[:, None] * inverse[None, :]
    cosine = np.concatenate([np.cos(angles), np.cos(angles)], 1)
    sine = np.concatenate([-np.sin(angles), np.sin(angles)], 1)
    both = np.concatenate([cosine, sine], 1).astype(np.float32)
    return both.reshape(16, 8, 2, 16, 2 * ROPE)


def rotate(values, table):
    half = ROPE // 2
    swapped = jnp.concatenate([values[:, half:], values[:, :half]], 1)
    return values * table[:, :ROPE] + swapped * table[:, ROPE:]


def normalize(values, gain):
    return values * lax.rsqrt(jnp.mean(values * values, -1, keepdims=True) + 1e-06) * gain


def kernel(
    tok_h, wq_h, wkv_h, qg_h, kvg_h, wu_h, wa_h, wv_h, slot_ref, tab_h,
    out_h, cache_ref,
    tok, wq, wkv, qg, kvg, wu, wa, wv, tabk, tabq,
    psk, pok, prk, psq, poq, prq, rks, rkr, rqs, rqr, cs, cq, kb, qb, first, second, acc, mx, tot, ob,
    load_sem, send_sem, sib_sem, rk_sem, rq_sem, cq_sem, ky_sem, kp_sem, ks_sem, out_sem, outs_sem, own_sem,
):
    chain = lax.axis_index("chain")
    tp = lax.axis_index("tp")
    z, x = chain // 4, chain % 4
    y, core = tp // 2, tp % 2
    other = 1 - core
    mirror = 15 - chain
    half = chain // 8
    piece = core * 4 + y
    yp, ym, yf = (y + 1) % 4, (y + 3) % 4, (y + 2) % 4
    sibling = {"chain": chain, "tp": 2 * y + other}
    up = {"chain": chain, "tp": 2 * yp + core}
    down = {"chain": chain, "tp": 2 * ym + core}
    pair = {"chain": mirror, "tp": tp}
    a = x + core * (z - x)
    b = z + core * (x - z)
    stride_a, stride_b = 1 + 3 * core, 4 - 3 * core

    def at(da, db):
        return ((a + da) % 4) * stride_a + ((b + db) % 4) * stride_b

    ap = {"chain": at(1, 0), "tp": tp}
    am = {"chain": at(3, 0), "tp": tp}
    bp = {"chain": at(0, 1), "tp": tp}
    bm = {"chain": at(0, 3), "tp": tp}

    loads = {}
    for k, (name, src, dst) in enumerate(
        [
            ("tok", tok_h, tok), ("wkv", wkv_h, wkv), ("wq", wq_h, wq), ("kvg", kvg_h, kvg),
            ("qg", qg_h, qg), ("tabk", tab_h.at[chain, piece], tabk), ("wa", wa_h, wa),
            ("wu", wu_h, wu), ("wv", wv_h, wv), ("tab0", tab_h.at[chain, :, half], tabq.at[0]),
            ("tab1", tab_h.at[mirror, :, half], tabq.at[1]),
        ]
    ):
        loads[name] = pltpu.make_async_copy(src, dst, load_sem.at[k])
        if k < 6:
            loads[name].start()

    def loaded(*names):
        for name in names:
            loads[name].wait()

    barrier = pltpu.get_barrier_semaphore()
    partners = (sibling, up, down, pair, ap, am, bp, bm)
    for device in partners:
        pl.semaphore_signal(barrier, inc=1, device_id=device, device_id_type=MESH)
    pl.semaphore_wait(barrier, len(partners))

    sent = {}

    def send(src, dst, recv, device, key=None):
        if key is None or key not in sent:
            slot = len(sent)

            def build():
                return pltpu.make_async_remote_copy(
                    src_ref=src(), dst_ref=dst(), send_sem=send_sem.at[slot], recv_sem=recv(),
                    device_id=device, device_id_type=MESH,
                )

            key = slot if key is None else key
            sent[key] = build
        sent[key]().start()

    def arrived(dst, recv):
        pltpu.make_async_remote_copy(
            src_ref=dst, dst_ref=dst, send_sem=send_sem.at[0], recv_sem=recv,
            device_id=sibling, device_id_type=MESH,
        ).wait_recv()

    def rows_of(c):
        return tok[pl.ds(pl.multiple_of(c * 128, 128), 128), :]

    def project_keys(c, dst):
        dst[...] = lax.dot_general(rows_of(c), wkv[...], NT, preferred_element_type=jnp.float32)

    def project_queries(c, dst):
        left = rows_of(c)

        def tile(i, _):
            cols = pl.ds(pl.multiple_of(i * 512, 512), 512)
            dst[:, cols] = jnp.dot(left, wq[:, cols], preferred_element_type=jnp.float32)
            return 0

        lax.fori_loop(0, 3, tile, 0)

    def ring_of(own, got, out, came, sems):
        def part(yy, h):
            rows = pl.ds(pl.multiple_of(yy * 32 + h * 16, 16), 16)
            return own[rows, :] + got[rows, :]

        def push(k, value, device):
            out[k] = value.astype(out.dtype)
            send(lambda: out.at[k], lambda: came.at[k], lambda: sems.at[k], device)

        def start():
            push(0, part(yf, 0), up)
            push(1, part(yf, 1), down)
            push(2, part(yp, 1), up)
            push(3, part(ym, 0), down)

        def middle():
            arrived(came.at[0], sems.at[0])
            push(4, part(yp, 0) + came[0].astype(jnp.float32), up)
            arrived(came.at[1], sems.at[1])
            push(5, part(ym, 1) + came[1].astype(jnp.float32), down)

        def end():
            for k in (2, 3, 4, 5):
                arrived(came.at[k], sems.at[k])
            totals = []
            for h, first, second in ((0, 4, 3), (1, 2, 5)):
                total = part(y, h) + came[first].astype(jnp.float32)
                totals.append(total + came[second].astype(jnp.float32))
            return totals

        return start, middle, end

    keys_start, keys_middle, keys_end = ring_of(pok, prk, rks, rkr, rk_sem)
    queries_start, queries_middle, queries_end = ring_of(poq, prq, rqs, rqr, rq_sem)

    loaded("tok", "wkv")
    project_keys(other, psk)
    send(lambda: psk, lambda: prk, lambda: sib_sem.at[0], sibling)
    project_keys(core, pok)
    loaded("wq")
    for name in ("wa", "wu", "wv", "tab0", "tab1"):
        loads[name].start()
    arrived(prk, sib_sem.at[0])
    keys_start()
    project_queries(other, psq)
    send(lambda: psq, lambda: prq, lambda: sib_sem.at[1], sibling)
    keys_middle()
    project_queries(core, poq)

    slot_own = 2 * chain + core

    def keys_y(yy, h, n):
        return kb.at[slot_own, pl.ds(pl.multiple_of(yy * 32 + h * 16, 16), n)]

    loaded("kvg", "tabk")
    gain_kv = jnp.concatenate([kvg[k : k + 1, :] for k in range(LAT // 128)], 1)
    for h, total in enumerate(keys_end()):
        latent = normalize(total[:, :LAT], gain_kv)
        turned = rotate(total[:, LAT:], tabk[h])
        rows = pl.ds(pl.multiple_of(y * 32 + h * 16, 16), 16)
        kb[slot_own, rows, :LAT] = latent.astype(jnp.bfloat16)
        kb[slot_own, rows, LAT:] = jnp.concatenate(
            [turned, jnp.zeros_like(turned)], 1
        ).astype(jnp.bfloat16)
    def send_y(yy, h, n, k, device):
        send(lambda: keys_y(yy, h, n), lambda: keys_y(yy, h, n), lambda: ky_sem.at[k], device)

    send_y(y, 0, 32, 0, up)
    send_y(y, 0, 32, 1, down)
    arrived(prq, sib_sem.at[1])
    queries_start()
    arrived(keys_y(ym, 0, 32), ky_sem.at[0])
    send_y(ym, 0, 16, 2, up)
    arrived(keys_y(yp, 0, 32), ky_sem.at[1])
    send_y(yp, 1, 16, 3, down)

    def block(n, p=None):
        if p is None:
            return kb.at[2 * n + core]
        return kb.at[2 * n + core, pl.ds(64 * p, 64)]

    def pass_on(step, n, *devices):
        for k, device in enumerate(devices):
            send(lambda: block(n), lambda: block(n), lambda: kp_sem.at[n, 0], device, (step, k))
        send(lambda: block(n), lambda: block(n), lambda: ks_sem.at[n], sibling, (step, 4))

    def pass_part(step, n, p, device):
        send(lambda: block(n, p), lambda: block(n, p), lambda: kp_sem.at[n, p], device, (step, 5))

    places_of = {step: at(*step) for step in RINGS}

    def whole(n):
        arrived(block(n), kp_sem.at[n, 0])

    def halves(n):
        for p in range(2):
            arrived(block(n, p), kp_sem.at[n, p])

    def relay(u, v):
        n = places_of[u, v]
        if v == 2 or (u, v) == (2, 0):
            halves(n)
        else:
            whole(n)
        if v == 0:
            if u != 2:
                pass_part((u, v), n, 0 if u == 3 else 1, ap if u == 3 else am)
            pass_on((u, v), n, bp, bm)
        else:
            if v != 2:
                pass_part((u, v), n, 0 if v == 3 else 1, bp if v == 3 else bm)
            pass_on((u, v), n)

    arrived(keys_y(yf, 0, 16), ky_sem.at[2])
    arrived(keys_y(yf, 1, 16), ky_sem.at[3])
    pass_on((0, 0), places_of[0, 0], ap, am, bp, bm)
    queries_middle()
    acc[...] = jnp.zeros_like(acc)
    tot[...] = jnp.zeros_like(tot)
    mx[...] = jnp.full_like(mx, FLOOR_SCORE)

    loaded("qg")
    gain_q = jnp.concatenate([qg[k : k + 1, :] for k in range(QL // 128)], 1)
    for h, total in enumerate(queries_end()):
        cs[h] = normalize(total, gain_q).astype(jnp.bfloat16)

    def give(s, p, *devices):
        for device in devices:
            send(lambda: cq.at[s, p], lambda: cq.at[s, p], lambda: cq_sem.at[s, p], device)

    def take(s, p):
        arrived(cq.at[s, p], cq_sem.at[s, p])

    send(lambda: cs.at[1 - half], lambda: cq.at[1, piece], lambda: cq_sem.at[1, piece], pair)
    cq[0, piece] = cs[half]
    give(0, piece, up, down, sibling)
    pm, pp, pf = core * 4 + ym, core * 4 + yp, core * 4 + yf
    for u, v in RINGS[1:5]:
        relay(u, v)
    take(1, piece)
    give(1, piece, up, down, sibling)
    take(0, pm)
    give(0, pm, up, sibling)
    take(0, pp)
    give(0, pp, sibling)
    take(1, pp)
    give(1, pp, down, sibling)
    take(1, pm)
    give(1, pm, sibling)
    for u, v in RINGS[5:7]:
        relay(u, v)
    take(0, pf)
    give(0, pf, sibling)
    take(1, pf)
    give(1, pf, sibling)
    for s in range(2):
        for yy in range(4):
            take(s, other * 4 + yy)

    loaded("wa", "wu", "tab0", "tab1")

    def expand(i, _):
        cols = pl.ds(pl.multiple_of(i * 384, 384), 384)
        rows = cq[...].reshape(256, QL)
        projected = jnp.dot(rows, wu[:, cols], preferred_element_type=jnp.float32)
        table = tabq[...].reshape(256, 2 * ROPE)
        for j in range(2):
            head = 2 * i + j
            base = j * (NOPE + ROPE)
            nope = projected[:, base : base + NOPE].astype(jnp.bfloat16)
            turned = rotate(projected[:, base + NOPE : base + NOPE + ROPE], table)
            turned = jnp.concatenate([turned, jnp.zeros_like(turned)], 1).astype(jnp.bfloat16)
            absorbed = jnp.dot(nope, wa[head], preferred_element_type=jnp.float32)
            absorbed = absorbed.astype(jnp.bfloat16)
            places = pl.ds(pl.multiple_of(head * 128, 128), 128)
            for s in range(2):
                qb[s, places, :LAT] = absorbed[s * 128 : s * 128 + 128]
                qb[s, places, LAT:] = turned[s * 128 : s * 128 + 128]
        return 0

    lax.fori_loop(0, HEADS // 4, expand, 0)
    for u, v in RINGS[7:11]:
        relay(u, v)
    lax.fori_loop(HEADS // 4, HEADS // 2, expand, 0)

    def meet(c):
        for k in range(4):
            n = 4 * (c % 4) + k
            arrived(kb.at[2 * n + other], ks_sem.at[n])

    def second_rows():
        for u, v in RINGS[11:15]:
            relay(u, v)
        meet(z + 1)
        meet(z + 3)

    def last_row():
        relay(2, 2)
        meet(z + 2)

    def turn(n, side):
        cols = pl.ds(pl.multiple_of((n % 4) * 256 + side * 128, 128), 128)
        kt[n // 4, :LAT, cols] = kb[2 * n + side, :, :LAT].T

    def turn_own(steps):
        for u, v in steps:
            turn(at(u, v), core)

    def turn_other(steps):
        for u, v in steps:
            n = at(u, v)
            arrived(kb.at[2 * n + other], ks_sem.at[n])
            turn(n, other)

    def whole(n):
        arrived(block(n), kp_sem.at[n, 0])

    def halves(n):
        for p in range(2):
            arrived(block(n, p), kp_sem.at[n, p])

    token = lax.broadcasted_iota(jnp.int32, (1024, 1), 0) & 127
    place = ((token >> 4) << 5) + (token & 15) + half * 16
    key_iota = lax.broadcasted_iota(jnp.int32, (1, 512), 1)
    n_own, n_far = chain // 2 + 1, mirror // 2 + 1
    first_z = (z == 0).astype(jnp.int32)
    segments = []
    for k, offset in enumerate((0, 1, 3, 2)):
        c = (z + offset) % 4
        segments.append((1, c, jnp.clip(n_far - 2 * c, 0, 2)))
        segments.append((0, c, jnp.clip(n_own - 2 * c, 0, 2) * (1 - first_z * (k == 0))))
    segments.append((0, z, jnp.clip(n_own - 2 * z, 0, 2) * first_z))
    starts, final = [jnp.int32(0)], [jnp.int32(0), jnp.int32(0)]
    for k, (s, _, chunks) in enumerate(segments):
        starts.append(starts[-1] + chunks)
        final[s] = jnp.where(chunks > 0, k, final[s])

    def plan(t):
        s, c, done = jnp.int32(0), jnp.int32(0), jnp.int32(0)
        for k, (side, row, chunks) in enumerate(segments):
            inside = (t >= starts[k]) & (t < starts[k + 1])
            s = jnp.where(inside, side, s)
            c = jnp.where(inside, 2 * row + t - starts[k], c)
            ended = (final[side] == k) & (t + 1 == starts[k + 1])
            done = jnp.where(inside, ended.astype(jnp.int32), done)
        chunks = n_own + s * (n_far - n_own)
        return s, c, c == chunks - 1, done == 1

    def score(t, dst):
        s, c, _, _ = plan(t)
        keys = kb[pl.ds(4 * c, 4)].reshape(512, KEYW)
        dst[...] = lax.dot_general(qb[s], keys, NT, preferred_element_type=jnp.float32)

    def hide(t, dst):
        s, c, last, _ = plan(t)

        @pl.when(last)
        def _():
            blk = chain + s * (mirror - chain)
            visible = key_iota + 512 * c <= place + 256 * blk
            dst[...] = jnp.where(visible, dst[...], FLOOR_SCORE)

    def out_cols(r):
        return pl.ds(pl.multiple_of(r * 512, 512), 512)

    def out_copy(r):
        return pltpu.make_async_remote_copy(
            src_ref=ob.at[1, :, :, out_cols(r)], dst_ref=out_h.at[:, half, :, out_cols(r)],
            send_sem=outs_sem.at[r], recv_sem=out_sem.at[r], device_id=pair, device_id_type=MESH,
        )

    def own_copy(r):
        return pltpu.make_async_copy(
            ob.at[0, :, :, out_cols(r)], out_h.at[:, half, :, out_cols(r)], own_sem.at[r]
        )

    def step(t, now, later):
        s, c, _, done = plan(t)
        score(jnp.minimum(t + 1, 8), later)
        parts = [now[:, k : k + 128] * SCALE2 for k in range(0, 512, 128)]
        before = mx[s]
        top = jnp.max(functools.reduce(jnp.maximum, parts), 1, keepdims=True)
        peak = jnp.maximum(before, top)
        shrink = jnp.exp2(before - peak)
        weights = [jnp.exp2(p - peak) for p in parts]
        mx[s] = peak
        tot[s] = tot[s] * shrink + sum(weights[1:], weights[0])
        weights = jnp.concatenate([w.astype(jnp.bfloat16) for w in weights], 1)
        latent = kb[pl.ds(4 * c, 4), :, :LAT].reshape(512, LAT)
        mixed = jnp.dot(weights, latent, preferred_element_type=jnp.float32)
        shrink = jnp.concatenate([shrink] * (LAT // 128), 1)
        acc[s] = acc[s] * shrink + mixed
        hide(jnp.minimum(t + 1, 8), later)

        @pl.when(done)
        def _():
            def group(r, _):
                for k in range(4):
                    part = pl.ds(pl.multiple_of(r * 512 + k * 128, 128), 128)
                    total = jnp.sum(tot[s, part, :], 1, keepdims=True)
                    mixed = (acc[s, part, :] * (1.0 / total)).astype(jnp.bfloat16)
                    value = jnp.dot(mixed, wv[4 * r + k], preferred_element_type=jnp.float32)
                    ob[s, :, :, part] = value.astype(jnp.bfloat16).reshape(8, 16, VH)

                @pl.when(s == 1)
                def _():
                    out_copy(r).start()

                @pl.when(s == 0)
                def _():
                    own_copy(r).start()

                return 0

            lax.fori_loop(0, 2, group, 0)

    loaded("wv")
    meet(z)
    score(0, first)
    hide(0, first)

    def serve(t):
        @pl.when(t + 1 == starts[2])
        def _():
            second_rows()

        @pl.when(t + 1 == starts[6])
        def _():
            last_row()

    def two_steps(i, _):
        serve(2 * i)
        step(2 * i, first, second)

        @pl.when(i < 4)
        def _():
            serve(2 * i + 1)
            step(2 * i + 1, second, first)

        return 0

    lax.fori_loop(0, 5, two_steps, 0)
    for j in range(2):
        rows = pl.ds(pl.multiple_of(tp * 16, 16), 16)
        cache_ref[j] = kb[slot_ref[j], rows, :][:, :KV]
    for r in range(2):
        own_copy(r).wait()
        out_copy(r).wait_send()
        arrived(out_h.at[:, 1 - half, :, out_cols(r)], out_sem.at[r])
    for build in sent.values():
        build().wait_send()


def hand_over(att_h, cache_h, att_out, cache_out, att, cache, sem):
    pieces = [(cache_h, cache, cache_out)]
    for k in range(4):
        rows = pl.ds(64 * k, 64)
        pieces.append((att_h.at[rows], att.at[rows], att_out.at[rows]))
    into = [pltpu.make_async_copy(p[0], p[1], sem.at[0, k]) for k, p in enumerate(pieces)]
    out = [pltpu.make_async_copy(p[1], p[2], sem.at[1, k]) for k, p in enumerate(pieces)]
    for copy in into:
        copy.start()
    for first, second in zip(into, out):
        first.wait()
        second.start()
    for copy in out:
        copy.wait()


def per_device(tokens, w_down_q, w_down_kv, q_gain, kv_gain, w_up_q, w_absorb, w_value, slot_block):
    bf16, f32 = jnp.bfloat16, jnp.float32
    table = jnp.asarray(rotary_tables())
    hbm = pl.BlockSpec(memory_space=pl.ANY)
    dma = pltpu.SemaphoreType.DMA
    attended, cache = pl.pallas_call(
        kernel,
        out_shape=(
            jax.ShapeDtypeStruct((8, 2, 16, HEADS * VH), bf16),
            jax.ShapeDtypeStruct((2, 16, KV), bf16),
        ),
        in_specs=[hbm] * 8 + [pl.BlockSpec(memory_space=pltpu.SMEM), hbm],
        out_specs=(hbm, pl.BlockSpec(memory_space=pltpu.VMEM)),
        scratch_shapes=[
            pltpu.VMEM((256, 896), bf16),
            pltpu.VMEM((896, QL), bf16),
            pltpu.VMEM((KV, 896), bf16),
            pltpu.VMEM((QL // 128, 128), f32),
            pltpu.VMEM((LAT // 128, 128), f32),
            pltpu.VMEM((QL, HEADS * (NOPE + ROPE)), bf16),
            pltpu.VMEM((HEADS, NOPE, LAT), bf16),
            pltpu.VMEM((HEADS, LAT, VH), bf16),
            pltpu.VMEM((2, 16, 2 * ROPE), f32),
            pltpu.VMEM((2, 8, 16, 2 * ROPE), f32),
            pltpu.VMEM((128, KV), f32),
            pltpu.VMEM((128, KV), f32),
            pltpu.VMEM((128, KV), f32),
            pltpu.VMEM((128, QL), f32),
            pltpu.VMEM((128, QL), f32),
            pltpu.VMEM((128, QL), f32),
            pltpu.VMEM((6, 16, KV), bf16),
            pltpu.VMEM((6, 16, KV), bf16),
            pltpu.VMEM((6, 16, QL), f32),
            pltpu.VMEM((6, 16, QL), f32),
            pltpu.VMEM((2, 16, QL), bf16),
            pltpu.VMEM((2, 8, 16, QL), bf16),
            pltpu.VMEM((32, 128, KEYW), bf16),
            pltpu.VMEM((2, HEADS * 128, KEYW), bf16),
            pltpu.VMEM((1024, 512), f32),
            pltpu.VMEM((1024, 512), f32),
            pltpu.VMEM((2, HEADS * 128, LAT), f32),
            pltpu.VMEM((2, HEADS * 128, 128), f32),
            pltpu.VMEM((2, HEADS * 128, 128), f32),
            pltpu.VMEM((2, 8, 16, HEADS * VH), bf16),
            dma((11,)),
            dma((N_SEND,)),
            dma((2,)),
            dma((6,)),
            dma((6,)),
            dma((2, 8)),
            dma((4,)),
            dma((16, 2)),
            dma((16,)),
            dma((2,)),
            dma((2,)),
            dma((2,)),
        ],
        compiler_params=pltpu.CompilerParams(
            collective_id=0, has_side_effects=True, vmem_limit_bytes=56 * 2**20
        ),
    )(
        tokens, w_down_q, w_down_kv.T, q_gain.reshape(-1, 128), kv_gain.reshape(-1, 128),
        w_up_q, w_absorb, w_value, slot_block, table,
    )
    attended = attended.reshape(256, HEADS * VH)
    return pl.pallas_call(
        hand_over,
        out_shape=(
            jax.ShapeDtypeStruct(attended.shape, bf16),
            jax.ShapeDtypeStruct(cache.shape, bf16),
        ),
        in_specs=[hbm, hbm],
        out_specs=(hbm, hbm),
        scratch_shapes=[
            pltpu.VMEM(attended.shape, bf16),
            pltpu.VMEM(cache.shape, bf16),
            dma((2, 5)),
        ],
        compiler_params=pltpu.CompilerParams(vmem_limit_bytes=60 * 2**20),
    )(attended, cache)


def solution(mesh):
    placed = (
        P("chain", "tp"),
        P("tp", None),
        P("tp", None),
        P(),
        P(),
        P(None, "tp"),
        P("tp", None, None),
        P("tp", None, None),
        P("chain"),
    )
    return jax.shard_map(
        per_device,
        mesh=mesh,
        in_specs=placed,
        out_specs=(P("chain", "tp"), P("chain", "tp", None)),
        check_vma=False,
    )
```

```python
import functools
import math

import jax
import jax.numpy as jnp
import numpy as np
from jax import lax
from jax.experimental import pallas as pl
from jax.experimental.pallas import tpu as pltpu
from jax.sharding import PartitionSpec as P

MESH = pl.DeviceIdType.MESH
ROPE_BASE = 50000.0
FLOOR_SCORE = -1e30
QL, LAT, ROPE, NOPE, VH, HEADS = 1536, 512, 64, 128, 128, 8
KEYW = 640
KV = LAT + ROPE
SCALE2 = (NOPE + ROPE) ** -0.5 * math.log2(math.e)
NT = (((1,), (1,)), ((), ()))
N_SEND = 80
RINGS = (
    (0, 0), (3, 0), (1, 0), (0, 3), (0, 1), (2, 0), (0, 2), (3, 3), (3, 1), (1, 3), (1, 1),
    (2, 3), (2, 1), (3, 2), (1, 2), (2, 2),
)


def rotary_tables():
    inverse = ROPE_BASE ** (-2.0 * np.arange(ROPE // 2) / ROPE)
    angles = np.arange(4096)[:, None] * inverse[None, :]
    cosine = np.concatenate([np.cos(angles), np.cos(angles)], 1)
    sine = np.concatenate([-np.sin(angles), np.sin(angles)], 1)
    both = np.concatenate([cosine, sine], 1).astype(np.float32)
    return both.reshape(16, 8, 2, 16, 2 * ROPE)


def rotate(values, table):
    half = ROPE // 2
    swapped = jnp.concatenate([values[:, half:], values[:, :half]], 1)
    return values * table[:, :ROPE] + swapped * table[:, ROPE:]


def normalize(values, gain):
    return values * lax.rsqrt(jnp.mean(values * values, -1, keepdims=True) + 1e-06) * gain


def kernel(
    tok_h, wq_h, wkv_h, qg_h, kvg_h, wu_h, wa_h, wv_h, slot_ref, tab_h,
    out_h, cache_ref,
    tok, wq, wkv, qg, kvg, wu, wa, wv, tabk, tabq,
    psk, pok, prk, psq, poq, prq, rks, rkr, rqs, rqr, cs, cq, kb, qb, first, second, acc, mx, tot, ob,
    load_sem, send_sem, sib_sem, rk_sem, rq_sem, cq_sem, ky_sem, kp_sem, ks_sem, out_sem, outs_sem, own_sem,
):
    chain = lax.axis_index("chain")
    tp = lax.axis_index("tp")
    z, x = chain // 4, chain % 4
    y, core = tp // 2, tp % 2
    other = 1 - core
    mirror = 15 - chain
    half = chain // 8
    piece = core * 4 + y
    yp, ym, yf = (y + 1) % 4, (y + 3) % 4, (y + 2) % 4
    sibling = {"chain": chain, "tp": 2 * y + other}
    up = {"chain": chain, "tp": 2 * yp + core}
    down = {"chain": chain, "tp": 2 * ym + core}
    pair = {"chain": mirror, "tp": tp}
    a = x + core * (z - x)
    b = z + core * (x - z)
    stride_a, stride_b = 1 + 3 * core, 4 - 3 * core

    def at(da, db):
        return ((a + da) % 4) * stride_a + ((b + db) % 4) * stride_b

    ap = {"chain": at(1, 0), "tp": tp}
    am = {"chain": at(3, 0), "tp": tp}
    bp = {"chain": at(0, 1), "tp": tp}
    bm = {"chain": at(0, 3), "tp": tp}

    loads = {}
    for k, (name, src, dst) in enumerate(
        [
            ("tok", tok_h, tok), ("wkv", wkv_h, wkv), ("wq", wq_h, wq), ("kvg", kvg_h, kvg),
            ("qg", qg_h, qg), ("tabk", tab_h.at[chain, piece], tabk), ("wa", wa_h, wa),
            ("wu", wu_h, wu), ("wv", wv_h, wv), ("tab0", tab_h.at[chain, :, half], tabq.at[0]),
            ("tab1", tab_h.at[mirror, :, half], tabq.at[1]),
        ]
    ):
        loads[name] = pltpu.make_async_copy(src, dst, load_sem.at[k])
        if k < 6:
            loads[name].start()

    def loaded(*names):
        for name in names:
            loads[name].wait()

    barrier = pltpu.get_barrier_semaphore()
    partners = (sibling, up, down, pair, ap, am, bp, bm)
    for device in partners:
        pl.semaphore_signal(barrier, inc=1, device_id=device, device_id_type=MESH)
    pl.semaphore_wait(barrier, len(partners))

    sent = {}

    def send(src, dst, recv, device, key=None):
        if key is None or key not in sent:
            slot = len(sent)

            def build():
                return pltpu.make_async_remote_copy(
                    src_ref=src(), dst_ref=dst(), send_sem=send_sem.at[slot], recv_sem=recv(),
                    device_id=device, device_id_type=MESH,
                )

            key = slot if key is None else key
            sent[key] = build
        sent[key]().start()

    def arrived(dst, recv):
        pltpu.make_async_remote_copy(
            src_ref=dst, dst_ref=dst, send_sem=send_sem.at[0], recv_sem=recv,
            device_id=sibling, device_id_type=MESH,
        ).wait_recv()

    def rows_of(c):
        return tok[pl.ds(pl.multiple_of(c * 128, 128), 128), :]

    def project_keys(c, dst):
        dst[...] = lax.dot_general(rows_of(c), wkv[...], NT, preferred_element_type=jnp.float32)

    def project_queries(c, dst):
        left = rows_of(c)

        def tile(i, _):
            cols = pl.ds(pl.multiple_of(i * 512, 512), 512)
            dst[:, cols] = jnp.dot(left, wq[:, cols], preferred_element_type=jnp.float32)
            return 0

        lax.fori_loop(0, 3, tile, 0)

    def ring_of(own, got, out, came, sems):
        def part(yy, h):
            rows = pl.ds(pl.multiple_of(yy * 32 + h * 16, 16), 16)
            return own[rows, :] + got[rows, :]

        def push(k, value, device):
            out[k] = value.astype(out.dtype)
            send(lambda: out.at[k], lambda: came.at[k], lambda: sems.at[k], device)

        def start():
            push(0, part(yf, 0), up)
            push(1, part(yf, 1), down)
            push(2, part(yp, 1), up)
            push(3, part(ym, 0), down)

        def middle():
            arrived(came.at[0], sems.at[0])
            push(4, part(yp, 0) + came[0].astype(jnp.float32), up)
            arrived(came.at[1], sems.at[1])
            push(5, part(ym, 1) + came[1].astype(jnp.float32), down)

        def end():
            for k in (2, 3, 4, 5):
                arrived(came.at[k], sems.at[k])
            totals = []
            for h, first, second in ((0, 4, 3), (1, 2, 5)):
                total = part(y, h) + came[first].astype(jnp.float32)
                totals.append(total + came[second].astype(jnp.float32))
            return totals

        return start, middle, end

    keys_start, keys_middle, keys_end = ring_of(pok, prk, rks, rkr, rk_sem)
    queries_start, queries_middle, queries_end = ring_of(poq, prq, rqs, rqr, rq_sem)

    loaded("tok", "wkv")
    project_keys(other, psk)
    send(lambda: psk, lambda: prk, lambda: sib_sem.at[0], sibling)
    project_keys(core, pok)
    loaded("wq")
    for name in ("wa", "wu", "wv", "tab0", "tab1"):
        loads[name].start()
    arrived(prk, sib_sem.at[0])
    keys_start()
    project_queries(other, psq)
    send(lambda: psq, lambda: prq, lambda: sib_sem.at[1], sibling)
    keys_middle()
    project_queries(core, poq)

    slot_own = 2 * chain + core

    def keys_y(yy, h, n):
        return kb.at[slot_own, pl.ds(pl.multiple_of(yy * 32 + h * 16, 16), n)]

    loaded("kvg", "tabk")
    gain_kv = jnp.concatenate([kvg[k : k + 1, :] for k in range(LAT // 128)], 1)
    for h, total in enumerate(keys_end()):
        latent = normalize(total[:, :LAT], gain_kv)
        turned = rotate(total[:, LAT:], tabk[h])
        rows = pl.ds(pl.multiple_of(y * 32 + h * 16, 16), 16)
        kb[slot_own, rows, :LAT] = latent.astype(jnp.bfloat16)
        kb[slot_own, rows, LAT:] = jnp.concatenate(
            [turned, jnp.zeros_like(turned)], 1
        ).astype(jnp.bfloat16)
    def send_y(yy, h, n, k, device):
        send(lambda: keys_y(yy, h, n), lambda: keys_y(yy, h, n), lambda: ky_sem.at[k], device)

    send_y(y, 0, 32, 0, up)
    send_y(y, 0, 32, 1, down)
    arrived(prq, sib_sem.at[1])
    queries_start()
    arrived(keys_y(ym, 0, 32), ky_sem.at[0])
    send_y(ym, 0, 16, 2, up)
    arrived(keys_y(yp, 0, 32), ky_sem.at[1])
    send_y(yp, 1, 16, 3, down)

    def block(n, p=None):
        if p is None:
            return kb.at[2 * n + core]
        return kb.at[2 * n + core, pl.ds(64 * p, 64)]

    def pass_on(step, n, *devices):
        for k, device in enumerate(devices):
            send(lambda: block(n), lambda: block(n), lambda: kp_sem.at[n, 0], device, (step, k))
        send(lambda: block(n), lambda: block(n), lambda: ks_sem.at[n], sibling, (step, 4))

    def pass_part(step, n, p, device):
        send(lambda: block(n, p), lambda: block(n, p), lambda: kp_sem.at[n, p], device, (step, 5))

    places_of = {step: at(*step) for step in RINGS}

    def whole(n):
        arrived(block(n), kp_sem.at[n, 0])

    def halves(n):
        for p in range(2):
            arrived(block(n, p), kp_sem.at[n, p])

    def relay(u, v):
        n = places_of[u, v]
        if v == 2 or (u, v) == (2, 0):
            halves(n)
        else:
            whole(n)
        if v == 0:
            if u != 2:
                pass_part((u, v), n, 0 if u == 3 else 1, ap if u == 3 else am)
            pass_on((u, v), n, bp, bm)
        else:
            if v != 2:
                pass_part((u, v), n, 0 if v == 3 else 1, bp if v == 3 else bm)
            pass_on((u, v), n)

    arrived(keys_y(yf, 0, 16), ky_sem.at[2])
    arrived(keys_y(yf, 1, 16), ky_sem.at[3])
    pass_on((0, 0), places_of[0, 0], ap, am, bp, bm)
    queries_middle()
    acc[...] = jnp.zeros_like(acc)
    tot[...] = jnp.zeros_like(tot)
    mx[...] = jnp.full_like(mx, FLOOR_SCORE)

    loaded("qg")
    gain_q = jnp.concatenate([qg[k : k + 1, :] for k in range(QL // 128)], 1)
    for h, total in enumerate(queries_end()):
        cs[h] = normalize(total, gain_q).astype(jnp.bfloat16)

    def give(s, p, *devices):
        for device in devices:
            send(lambda: cq.at[s, p], lambda: cq.at[s, p], lambda: cq_sem.at[s, p], device)

    def take(s, p):
        arrived(cq.at[s, p], cq_sem.at[s, p])

    send(lambda: cs.at[1 - half], lambda: cq.at[1, piece], lambda: cq_sem.at[1, piece], pair)
    cq[0, piece] = cs[half]
    give(0, piece, up, down, sibling)
    pm, pp, pf = core * 4 + ym, core * 4 + yp, core * 4 + yf
    for u, v in RINGS[1:5]:
        relay(u, v)
    take(1, piece)
    give(1, piece, up, down, sibling)
    take(0, pm)
    give(0, pm, up, sibling)
    take(0, pp)
    give(0, pp, sibling)
    take(1, pp)
    give(1, pp, down, sibling)
    take(1, pm)
    give(1, pm, sibling)
    for u, v in RINGS[5:7]:
        relay(u, v)
    take(0, pf)
    give(0, pf, sibling)
    take(1, pf)
    give(1, pf, sibling)
    for s in range(2):
        for yy in range(4):
            take(s, other * 4 + yy)

    loaded("wa", "wu", "tab0", "tab1")

    def expand(i, _):
        cols = pl.ds(pl.multiple_of(i * 384, 384), 384)
        rows = cq[...].reshape(256, QL)
        projected = jnp.dot(rows, wu[:, cols], preferred_element_type=jnp.float32)
        table = tabq[...].reshape(256, 2 * ROPE)
        for j in range(2):
            head = 2 * i + j
            base = j * (NOPE + ROPE)
            nope = projected[:, base : base + NOPE].astype(jnp.bfloat16)
            turned = rotate(projected[:, base + NOPE : base + NOPE + ROPE], table)
            turned = jnp.concatenate([turned, jnp.zeros_like(turned)], 1).astype(jnp.bfloat16)
            absorbed = jnp.dot(nope, wa[head], preferred_element_type=jnp.float32)
            absorbed = absorbed.astype(jnp.bfloat16)
            places = pl.ds(pl.multiple_of(head * 128, 128), 128)
            for s in range(2):
                qb[s, places, :LAT] = absorbed[s * 128 : s * 128 + 128]
                qb[s, places, LAT:] = turned[s * 128 : s * 128 + 128]
        return 0

    lax.fori_loop(0, HEADS // 4, expand, 0)
    for u, v in RINGS[7:11]:
        relay(u, v)
    lax.fori_loop(HEADS // 4, HEADS // 2, expand, 0)
    for u, v in RINGS[11:15]:
        relay(u, v)

    def meet(c):
        for k in range(4):
            n = 4 * (c % 4) + k
            arrived(kb.at[2 * n + other], ks_sem.at[n])

    def second_rows():
        relay(2, 2)
        meet(z + 1)
        meet(z + 3)

    def last_row():
        meet(z + 2)

    def turn(n, side):
        cols = pl.ds(pl.multiple_of((n % 4) * 256 + side * 128, 128), 128)
        kt[n // 4, :LAT, cols] = kb[2 * n + side, :, :LAT].T

    def turn_own(steps):
        for u, v in steps:
            turn(at(u, v), core)

    def turn_other(steps):
        for u, v in steps:
            n = at(u, v)
            arrived(kb.at[2 * n + other], ks_sem.at[n])
            turn(n, other)

    def whole(n):
        arrived(block(n), kp_sem.at[n, 0])

    def halves(n):
        for p in range(2):
            arrived(block(n, p), kp_sem.at[n, p])

    token = lax.broadcasted_iota(jnp.int32, (1024, 1), 0) & 127
    place = ((token >> 4) << 5) + (token & 15) + half * 16
    key_iota = lax.broadcasted_iota(jnp.int32, (1, 512), 1)
    n_own, n_far = chain // 2 + 1, mirror // 2 + 1
    first_z = (z == 0).astype(jnp.int32)
    segments = []
    for k, offset in enumerate((0, 1, 3, 2)):
        c = (z + offset) % 4
        segments.append((1, c, jnp.clip(n_far - 2 * c, 0, 2)))
        segments.append((0, c, jnp.clip(n_own - 2 * c, 0, 2) * (1 - first_z * (k == 0))))
    segments.append((0, z, jnp.clip(n_own - 2 * z, 0, 2) * first_z))
    starts, final = [jnp.int32(0)], [jnp.int32(0), jnp.int32(0)]
    for k, (s, _, chunks) in enumerate(segments):
        starts.append(starts[-1] + chunks)
        final[s] = jnp.where(chunks > 0, k, final[s])

    def plan(t):
        s, c, done = jnp.int32(0), jnp.int32(0), jnp.int32(0)
        for k, (side, row, chunks) in enumerate(segments):
            inside = (t >= starts[k]) & (t < starts[k + 1])
            s = jnp.where(inside, side, s)
            c = jnp.where(inside, 2 * row + t - starts[k], c)
            ended = (final[side] == k) & (t + 1 == starts[k + 1])
            done = jnp.where(inside, ended.astype(jnp.int32), done)
        chunks = n_own + s * (n_far - n_own)
        return s, c, c == chunks - 1, done == 1

    def score(t, dst):
        s, c, _, _ = plan(t)
        keys = kb[pl.ds(4 * c, 4)].reshape(512, KEYW)
        dst[...] = lax.dot_general(qb[s], keys, NT, preferred_element_type=jnp.float32)

    def hide(t, dst):
        s, c, last, _ = plan(t)

        @pl.when(last)
        def _():
            blk = chain + s * (mirror - chain)
            visible = key_iota + 512 * c <= place + 256 * blk
            dst[...] = jnp.where(visible, dst[...], FLOOR_SCORE)

    def out_cols(r):
        return pl.ds(pl.multiple_of(r * 512, 512), 512)

    def out_copy(r):
        return pltpu.make_async_remote_copy(
            src_ref=ob.at[1, :, :, out_cols(r)], dst_ref=out_h.at[:, half, :, out_cols(r)],
            send_sem=outs_sem.at[r], recv_sem=out_sem.at[r], device_id=pair, device_id_type=MESH,
        )

    def own_copy(r):
        return pltpu.make_async_copy(
            ob.at[0, :, :, out_cols(r)], out_h.at[:, half, :, out_cols(r)], own_sem.at[r]
        )

    def step(t, now, later):
        s, c, _, done = plan(t)
        score(jnp.minimum(t + 1, 8), later)
        parts = [now[:, k : k + 128] * SCALE2 for k in range(0, 512, 128)]
        before = mx[s]
        top = jnp.max(functools.reduce(jnp.maximum, parts), 1, keepdims=True)
        peak = jnp.maximum(before, top)
        shrink = jnp.exp2(before - peak)
        weights = [jnp.exp2(p - peak) for p in parts]
        mx[s] = peak
        tot[s] = tot[s] * shrink + sum(weights[1:], weights[0])
        weights = jnp.concatenate([w.astype(jnp.bfloat16) for w in weights], 1)
        latent = kb[pl.ds(4 * c, 4), :, :LAT].reshape(512, LAT)
        mixed = jnp.dot(weights, latent, preferred_element_type=jnp.float32)
        shrink = jnp.concatenate([shrink] * (LAT // 128), 1)
        acc[s] = acc[s] * shrink + mixed
        hide(jnp.minimum(t + 1, 8), later)

        @pl.when(done)
        def _():
            def group(r, _):
                for k in range(4):
                    part = pl.ds(pl.multiple_of(r * 512 + k * 128, 128), 128)
                    total = jnp.sum(tot[s, part, :], 1, keepdims=True)
                    mixed = (acc[s, part, :] * (1.0 / total)).astype(jnp.bfloat16)
                    value = jnp.dot(mixed, wv[4 * r + k], preferred_element_type=jnp.float32)
                    ob[s, :, :, part] = value.astype(jnp.bfloat16).reshape(8, 16, VH)

                @pl.when(s == 1)
                def _():
                    out_copy(r).start()

                @pl.when(s == 0)
                def _():
                    own_copy(r).start()

                return 0

            lax.fori_loop(0, 2, group, 0)

    loaded("wv")
    meet(z)
    score(0, first)
    hide(0, first)

    def serve(t):
        @pl.when(t + 1 == starts[2])
        def _():
            second_rows()

        @pl.when(t + 1 == starts[6])
        def _():
            last_row()

    def two_steps(i, _):
        serve(2 * i)
        step(2 * i, first, second)

        @pl.when(i < 4)
        def _():
            serve(2 * i + 1)
            step(2 * i + 1, second, first)

        return 0

    lax.fori_loop(0, 5, two_steps, 0)
    for j in range(2):
        rows = pl.ds(pl.multiple_of(tp * 16, 16), 16)
        cache_ref[j] = kb[slot_ref[j], rows, :][:, :KV]
    for r in range(2):
        own_copy(r).wait()
        out_copy(r).wait_send()
        arrived(out_h.at[:, 1 - half, :, out_cols(r)], out_sem.at[r])
    for build in sent.values():
        build().wait_send()


def hand_over(att_h, cache_h, att_out, cache_out, att, cache, sem):
    pieces = [(cache_h, cache, cache_out)]
    for k in range(4):
        rows = pl.ds(64 * k, 64)
        pieces.append((att_h.at[rows], att.at[rows], att_out.at[rows]))
    into = [pltpu.make_async_copy(p[0], p[1], sem.at[0, k]) for k, p in enumerate(pieces)]
    out = [pltpu.make_async_copy(p[1], p[2], sem.at[1, k]) for k, p in enumerate(pieces)]
    for copy in into:
        copy.start()
    for first, second in zip(into, out):
        first.wait()
        second.start()
    for copy in out:
        copy.wait()


def per_device(tokens, w_down_q, w_down_kv, q_gain, kv_gain, w_up_q, w_absorb, w_value, slot_block):
    bf16, f32 = jnp.bfloat16, jnp.float32
    table = jnp.asarray(rotary_tables())
    hbm = pl.BlockSpec(memory_space=pl.ANY)
    dma = pltpu.SemaphoreType.DMA
    attended, cache = pl.pallas_call(
        kernel,
        out_shape=(
            jax.ShapeDtypeStruct((8, 2, 16, HEADS * VH), bf16),
            jax.ShapeDtypeStruct((2, 16, KV), bf16),
        ),
        in_specs=[hbm] * 8 + [pl.BlockSpec(memory_space=pltpu.SMEM), hbm],
        out_specs=(hbm, pl.BlockSpec(memory_space=pltpu.VMEM)),
        scratch_shapes=[
            pltpu.VMEM((256, 896), bf16),
            pltpu.VMEM((896, QL), bf16),
            pltpu.VMEM((KV, 896), bf16),
            pltpu.VMEM((QL // 128, 128), f32),
            pltpu.VMEM((LAT // 128, 128), f32),
            pltpu.VMEM((QL, HEADS * (NOPE + ROPE)), bf16),
            pltpu.VMEM((HEADS, NOPE, LAT), bf16),
            pltpu.VMEM((HEADS, LAT, VH), bf16),
            pltpu.VMEM((2, 16, 2 * ROPE), f32),
            pltpu.VMEM((2, 8, 16, 2 * ROPE), f32),
            pltpu.VMEM((128, KV), f32),
            pltpu.VMEM((128, KV), f32),
            pltpu.VMEM((128, KV), f32),
            pltpu.VMEM((128, QL), f32),
            pltpu.VMEM((128, QL), f32),
            pltpu.VMEM((128, QL), f32),
            pltpu.VMEM((6, 16, KV), bf16),
            pltpu.VMEM((6, 16, KV), bf16),
            pltpu.VMEM((6, 16, QL), f32),
            pltpu.VMEM((6, 16, QL), f32),
            pltpu.VMEM((2, 16, QL), bf16),
            pltpu.VMEM((2, 8, 16, QL), bf16),
            pltpu.VMEM((32, 128, KEYW), bf16),
            pltpu.VMEM((2, HEADS * 128, KEYW), bf16),
            pltpu.VMEM((1024, 512), f32),
            pltpu.VMEM((1024, 512), f32),
            pltpu.VMEM((2, HEADS * 128, LAT), f32),
            pltpu.VMEM((2, HEADS * 128, 128), f32),
            pltpu.VMEM((2, HEADS * 128, 128), f32),
            pltpu.VMEM((2, 8, 16, HEADS * VH), bf16),
            dma((11,)),
            dma((N_SEND,)),
            dma((2,)),
            dma((6,)),
            dma((6,)),
            dma((2, 8)),
            dma((4,)),
            dma((16, 2)),
            dma((16,)),
            dma((2,)),
            dma((2,)),
            dma((2,)),
        ],
        compiler_params=pltpu.CompilerParams(
            collective_id=0, has_side_effects=True, vmem_limit_bytes=56 * 2**20
        ),
    )(
        tokens, w_down_q, w_down_kv.T, q_gain.reshape(-1, 128), kv_gain.reshape(-1, 128),
        w_up_q, w_absorb, w_value, slot_block, table,
    )
    attended = attended.reshape(256, HEADS * VH)
    return pl.pallas_call(
        hand_over,
        out_shape=(
            jax.ShapeDtypeStruct(attended.shape, bf16),
            jax.ShapeDtypeStruct(cache.shape, bf16),
        ),
        in_specs=[hbm, hbm],
        out_specs=(hbm, hbm),
        scratch_shapes=[
            pltpu.VMEM(attended.shape, bf16),
            pltpu.VMEM(cache.shape, bf16),
            dma((2, 5)),
        ],
        compiler_params=pltpu.CompilerParams(vmem_limit_bytes=60 * 2**20),
    )(attended, cache)


def solution(mesh):
    placed = (
        P("chain", "tp"),
        P("tp", None),
        P("tp", None),
        P(),
        P(),
        P(None, "tp"),
        P("tp", None, None),
        P("tp", None, None),
        P("chain"),
    )
    return jax.shard_map(
        per_device,
        mesh=mesh,
        in_specs=placed,
        out_specs=(P("chain", "tp"), P("chain", "tp", None)),
        check_vma=False,
    )
```

```python
import functools
import math

import jax
import jax.numpy as jnp
import numpy as np
from jax import lax
from jax.experimental import pallas as pl
from jax.experimental.pallas import tpu as pltpu
from jax.sharding import PartitionSpec as P

MESH = pl.DeviceIdType.MESH
ROPE_BASE = 50000.0
FLOOR_SCORE = -1e30
QL, LAT, ROPE, NOPE, VH, HEADS = 1536, 512, 64, 128, 128, 8
KEYW = 640
KV = LAT + ROPE
SCALE2 = (NOPE + ROPE) ** -0.5 * math.log2(math.e)
NT = (((1,), (1,)), ((), ()))
N_SEND = 80
RINGS = (
    (0, 0), (3, 0), (1, 0), (0, 3), (0, 1), (2, 0), (0, 2), (3, 3), (3, 1), (1, 3), (1, 1),
    (2, 3), (2, 1), (3, 2), (1, 2), (2, 2),
)


def rotary_tables():
    inverse = ROPE_BASE ** (-2.0 * np.arange(ROPE // 2) / ROPE)
    angles = np.arange(4096)[:, None] * inverse[None, :]
    cosine = np.concatenate([np.cos(angles), np.cos(angles)], 1)
    sine = np.concatenate([-np.sin(angles), np.sin(angles)], 1)
    both = np.concatenate([cosine, sine], 1).astype(np.float32)
    return both.reshape(16, 8, 2, 16, 2 * ROPE)


def rotate(values, table):
    half = ROPE // 2
    swapped = jnp.concatenate([values[:, half:], values[:, :half]], 1)
    return values * table[:, :ROPE] + swapped * table[:, ROPE:]


def normalize(values, gain):
    return values * lax.rsqrt(jnp.mean(values * values, -1, keepdims=True) + 1e-06) * gain


def kernel(
    tok_h, wq_h, wkv_h, qg_h, kvg_h, wu_h, wa_h, wv_h, slot_ref, tab_h,
    out_h, cache_ref,
    tok, wq, wkv, qg, kvg, wu, wa, wv, tabk, tabq,
    psk, pok, prk, psq, poq, prq, rks, rkr, rqs, rqr, cs, cq, kb, qb, first, second, acc, mx, tot, ob,
    load_sem, send_sem, sib_sem, rk_sem, rq_sem, cq_sem, ky_sem, kp_sem, ks_sem, out_sem, outs_sem, own_sem,
):
    chain = lax.axis_index("chain")
    tp = lax.axis_index("tp")
    z, x = chain // 4, chain % 4
    y, core = tp // 2, tp % 2
    other = 1 - core
    mirror = 15 - chain
    half = chain // 8
    piece = core * 4 + y
    yp, ym, yf = (y + 1) % 4, (y + 3) % 4, (y + 2) % 4
    sibling = {"chain": chain, "tp": 2 * y + other}
    up = {"chain": chain, "tp": 2 * yp + core}
    down = {"chain": chain, "tp": 2 * ym + core}
    pair = {"chain": mirror, "tp": tp}
    pair_up = {"chain": mirror, "tp": 2 * yp + core}
    pair_down = {"chain": mirror, "tp": 2 * ym + core}
    a = x + core * (z - x)
    b = z + core * (x - z)
    stride_a, stride_b = 1 + 3 * core, 4 - 3 * core

    def at(da, db):
        return ((a + da) % 4) * stride_a + ((b + db) % 4) * stride_b

    ap = {"chain": at(1, 0), "tp": tp}
    am = {"chain": at(3, 0), "tp": tp}
    bp = {"chain": at(0, 1), "tp": tp}
    bm = {"chain": at(0, 3), "tp": tp}

    loads = {}
    for k, (name, src, dst) in enumerate(
        [
            ("tok", tok_h, tok), ("wq", wq_h, wq), ("wkv", wkv_h, wkv), ("kvg", kvg_h, kvg),
            ("qg", qg_h, qg), ("tabk", tab_h.at[chain, piece], tabk), ("wa", wa_h, wa),
            ("wu", wu_h, wu), ("wv", wv_h, wv), ("tab0", tab_h.at[chain, :, half], tabq.at[0]),
            ("tab1", tab_h.at[mirror, :, half], tabq.at[1]),
        ]
    ):
        loads[name] = pltpu.make_async_copy(src, dst, load_sem.at[k])
        if k < 6:
            loads[name].start()

    def loaded(*names):
        for name in names:
            loads[name].wait()

    barrier = pltpu.get_barrier_semaphore()
    partners = (sibling, up, down, pair, pair_up, pair_down, ap, am, bp, bm)
    for device in partners:
        pl.semaphore_signal(barrier, inc=1, device_id=device, device_id_type=MESH)

    sent = {}

    def send(src, dst, recv, device, key=None):
        if key is None or key not in sent:
            slot = len(sent)

            def build():
                return pltpu.make_async_remote_copy(
                    src_ref=src(), dst_ref=dst(), send_sem=send_sem.at[slot], recv_sem=recv(),
                    device_id=device, device_id_type=MESH,
                )

            key = slot if key is None else key
            sent[key] = build
        sent[key]().start()

    def arrived(dst, recv):
        pltpu.make_async_remote_copy(
            src_ref=dst, dst_ref=dst, send_sem=send_sem.at[0], recv_sem=recv,
            device_id=sibling, device_id_type=MESH,
        ).wait_recv()

    def rows_of(c):
        return tok[pl.ds(pl.multiple_of(c * 128, 128), 128), :]

    def project_keys(c, dst):
        dst[...] = lax.dot_general(rows_of(c), wkv[...], NT, preferred_element_type=jnp.float32)

    def project_queries(c, dst):
        left = rows_of(c)

        def tile(i, _):
            cols = pl.ds(pl.multiple_of(i * 512, 512), 512)
            dst[:, cols] = jnp.dot(left, wq[:, cols], preferred_element_type=jnp.float32)
            return 0

        lax.fori_loop(0, 3, tile, 0)

    def ring_of(own, got, out, came, sems):
        def part(yy, h):
            rows = pl.ds(pl.multiple_of(yy * 32 + h * 16, 16), 16)
            return own[rows, :] + got[rows, :]

        def push(k, value, device):
            out[k] = value.astype(out.dtype)
            send(lambda: out.at[k], lambda: came.at[k], lambda: sems.at[k], device)

        def start():
            push(0, part(yf, 0), up)
            push(1, part(yf, 1), down)
            push(2, part(yp, 1), up)
            push(3, part(ym, 0), down)

        def middle():
            arrived(came.at[0], sems.at[0])
            push(4, part(yp, 0) + came[0].astype(jnp.float32), up)
            arrived(came.at[1], sems.at[1])
            push(5, part(ym, 1) + came[1].astype(jnp.float32), down)

        def end():
            for k in (2, 3, 4, 5):
                arrived(came.at[k], sems.at[k])
            totals = []
            for h, first, second in ((0, 4, 3), (1, 2, 5)):
                total = part(y, h) + came[first].astype(jnp.float32)
                totals.append(total + came[second].astype(jnp.float32))
            return totals

        return start, middle, end

    keys_start, keys_middle, keys_end = ring_of(pok, prk, rks, rkr, rk_sem)
    queries_start, queries_middle, queries_end = ring_of(poq, prq, rqs, rqr, rq_sem)

    loaded("tok", "wq")
    project_queries(other, psq)
    pl.semaphore_wait(barrier, len(partners))
    send(lambda: psq, lambda: prq, lambda: sib_sem.at[1], sibling)
    loaded("wkv")
    for name in ("wa", "wu", "wv", "tab0", "tab1"):
        loads[name].start()
    project_keys(other, psk)
    send(lambda: psk, lambda: prk, lambda: sib_sem.at[0], sibling)
    project_keys(core, pok)
    project_queries(core, poq)
    arrived(prq, sib_sem.at[1])
    queries_start()
    arrived(prk, sib_sem.at[0])
    keys_start()
    acc[...] = jnp.zeros_like(acc)
    tot[...] = jnp.zeros_like(tot)
    mx[...] = jnp.full_like(mx, FLOOR_SCORE)
    keys_middle()

    slot_own = 2 * chain + core

    def keys_y(yy, h, n):
        return kb.at[slot_own, pl.ds(pl.multiple_of(yy * 32 + h * 16, 16), n)]

    loaded("kvg", "tabk")
    gain_kv = jnp.concatenate([kvg[k : k + 1, :] for k in range(LAT // 128)], 1)
    for h, total in enumerate(keys_end()):
        latent = normalize(total[:, :LAT], gain_kv)
        turned = rotate(total[:, LAT:], tabk[h])
        rows = pl.ds(pl.multiple_of(y * 32 + h * 16, 16), 16)
        kb[slot_own, rows, :LAT] = latent.astype(jnp.bfloat16)
        kb[slot_own, rows, LAT:] = jnp.concatenate(
            [turned, jnp.zeros_like(turned)], 1
        ).astype(jnp.bfloat16)
    def send_y(yy, h, n, k, device):
        send(lambda: keys_y(yy, h, n), lambda: keys_y(yy, h, n), lambda: ky_sem.at[k], device)

    send_y(y, 0, 32, 0, up)
    send_y(y, 0, 32, 1, down)
    queries_middle()
    arrived(keys_y(ym, 0, 32), ky_sem.at[0])
    send_y(ym, 0, 16, 2, up)
    arrived(keys_y(yp, 0, 32), ky_sem.at[1])
    send_y(yp, 1, 16, 3, down)

    def block(n, p=None):
        if p is None:
            return kb.at[2 * n + core]
        return kb.at[2 * n + core, pl.ds(64 * p, 64)]

    def pass_on(step, n, *devices):
        for k, device in enumerate(devices):
            send(lambda: block(n), lambda: block(n), lambda: kp_sem.at[n, 0], device, (step, k))
        send(lambda: block(n), lambda: block(n), lambda: ks_sem.at[n], sibling, (step, 4))

    def pass_part(step, n, p, device):
        send(lambda: block(n, p), lambda: block(n, p), lambda: kp_sem.at[n, p], device, (step, 5))

    places_of = {step: at(*step) for step in RINGS}

    def whole(n):
        arrived(block(n), kp_sem.at[n, 0])

    def halves(n):
        for p in range(2):
            arrived(block(n, p), kp_sem.at[n, p])

    def relay(u, v):
        n = places_of[u, v]
        if v == 2 or (u, v) == (2, 0):
            halves(n)
        else:
            whole(n)
        if v == 0:
            if u != 2:
                pass_part((u, v), n, 0 if u == 3 else 1, ap if u == 3 else am)
            pass_on((u, v), n, bp, bm)
        else:
            if v != 2:
                pass_part((u, v), n, 0 if v == 3 else 1, bp if v == 3 else bm)
            pass_on((u, v), n)

    arrived(keys_y(yf, 0, 16), ky_sem.at[2])
    arrived(keys_y(yf, 1, 16), ky_sem.at[3])
    pass_on((0, 0), places_of[0, 0], ap, am, bp, bm)

    loaded("qg")
    gain_q = jnp.concatenate([qg[k : k + 1, :] for k in range(QL // 128)], 1)
    for h, total in enumerate(queries_end()):
        cs[h] = normalize(total, gain_q).astype(jnp.bfloat16)

    def give(s, p, *devices):
        for device in devices:
            send(lambda: cq.at[s, p], lambda: cq.at[s, p], lambda: cq_sem.at[s, p], device)

    def take(s, p):
        arrived(cq.at[s, p], cq_sem.at[s, p])

    for device in (pair, pair_up, pair_down):
        send(lambda: cs.at[1 - half], lambda: cq.at[1, piece], lambda: cq_sem.at[1, piece], device)
    cq[0, piece] = cs[half]
    give(0, piece, up, down, sibling)
    pm, pp, pf = core * 4 + ym, core * 4 + yp, core * 4 + yf
    take(0, pm)
    give(0, pm, up, sibling)
    take(1, pp)
    give(1, pp, down, sibling)
    for u, v in RINGS[1:5]:
        relay(u, v)
    take(0, pp)
    give(0, pp, sibling)
    take(1, piece)
    give(1, piece, sibling)
    take(1, pm)
    give(1, pm, sibling)
    for u, v in RINGS[5:7]:
        relay(u, v)
    take(0, pf)
    give(0, pf, sibling)
    take(1, pf)
    give(1, pf, sibling)
    for s in range(2):
        for yy in range(4):
            take(s, other * 4 + yy)

    loaded("wa", "wu", "tab0", "tab1")

    def expand(i, _):
        cols = pl.ds(pl.multiple_of(i * 384, 384), 384)
        rows = cq[...].reshape(256, QL)
        projected = jnp.dot(rows, wu[:, cols], preferred_element_type=jnp.float32)
        table = tabq[...].reshape(256, 2 * ROPE)
        for j in range(2):
            head = 2 * i + j
            base = j * (NOPE + ROPE)
            nope = projected[:, base : base + NOPE].astype(jnp.bfloat16)
            turned = rotate(projected[:, base + NOPE : base + NOPE + ROPE], table)
            turned = jnp.concatenate([turned, jnp.zeros_like(turned)], 1).astype(jnp.bfloat16)
            absorbed = jnp.dot(nope, wa[head], preferred_element_type=jnp.float32)
            absorbed = absorbed.astype(jnp.bfloat16)
            places = pl.ds(pl.multiple_of(head * 128, 128), 128)
            for s in range(2):
                qb[s, places, :LAT] = absorbed[s * 128 : s * 128 + 128]
                qb[s, places, LAT:] = turned[s * 128 : s * 128 + 128]
        return 0

    lax.fori_loop(0, HEADS // 4, expand, 0)
    for u, v in RINGS[7:11]:
        relay(u, v)
    lax.fori_loop(HEADS // 4, HEADS // 2, expand, 0)
    for u, v in RINGS[11:15]:
        relay(u, v)

    def meet(c):
        for k in range(4):
            n = 4 * (c % 4) + k
            arrived(kb.at[2 * n + other], ks_sem.at[n])

    def second_rows():
        relay(2, 2)
        meet(z + 1)
        meet(z + 3)

    def last_row():
        meet(z + 2)

    token = lax.broadcasted_iota(jnp.int32, (1024, 1), 0) & 127
    place = ((token >> 4) << 5) + (token & 15) + half * 16
    key_iota = lax.broadcasted_iota(jnp.int32, (1, 512), 1)
    n_own, n_far = chain // 2 + 1, mirror // 2 + 1
    first_z = (z == 0).astype(jnp.int32)
    segments = []
    for k, offset in enumerate((0, 1, 3, 2)):
        c = (z + offset) % 4
        segments.append((1, c, jnp.clip(n_far - 2 * c, 0, 2)))
        segments.append((0, c, jnp.clip(n_own - 2 * c, 0, 2) * (1 - first_z * (k == 0))))
    segments.append((0, z, jnp.clip(n_own - 2 * z, 0, 2) * first_z))
    starts, final = [jnp.int32(0)], [jnp.int32(0), jnp.int32(0)]
    for k, (s, _, chunks) in enumerate(segments):
        starts.append(starts[-1] + chunks)
        final[s] = jnp.where(chunks > 0, k, final[s])

    def plan(t):
        s, c, done = jnp.int32(0), jnp.int32(0), jnp.int32(0)
        for k, (side, row, chunks) in enumerate(segments):
            inside = (t >= starts[k]) & (t < starts[k + 1])
            s = jnp.where(inside, side, s)
            c = jnp.where(inside, 2 * row + t - starts[k], c)
            ended = (final[side] == k) & (t + 1 == starts[k + 1])
            done = jnp.where(inside, ended.astype(jnp.int32), done)
        chunks = n_own + s * (n_far - n_own)
        return s, c, c == chunks - 1, done == 1

    def score(t, dst):
        s, c, _, _ = plan(t)
        keys = kb[pl.ds(4 * c, 4)].reshape(512, KEYW)
        dst[...] = lax.dot_general(qb[s], keys, NT, preferred_element_type=jnp.float32)

    def hide(t, dst):
        s, c, last, _ = plan(t)

        @pl.when(last)
        def _():
            blk = chain + s * (mirror - chain)
            visible = key_iota + 512 * c <= place + 256 * blk
            dst[...] = jnp.where(visible, dst[...], FLOOR_SCORE)

    def out_cols(r):
        return pl.ds(pl.multiple_of(r * 512, 512), 512)

    def out_copy(r):
        return pltpu.make_async_remote_copy(
            src_ref=ob.at[1, :, :, out_cols(r)], dst_ref=out_h.at[:, half, :, out_cols(r)],
            send_sem=outs_sem.at[r], recv_sem=out_sem.at[r], device_id=pair, device_id_type=MESH,
        )

    def own_copy(r):
        return pltpu.make_async_copy(
            ob.at[0, :, :, out_cols(r)], out_h.at[:, half, :, out_cols(r)], own_sem.at[r]
        )

    def step(t, now, later):
        s, c, _, done = plan(t)
        if later is not None:
            score(t + 1, later)
        parts = [now[:, k : k + 128] * SCALE2 for k in range(0, 512, 128)]
        before = mx[s]
        top = jnp.max(functools.reduce(jnp.maximum, parts), 1, keepdims=True)
        peak = jnp.maximum(before, top)
        shrink = jnp.exp2(before - peak)
        weights = [jnp.exp2(p - peak) for p in parts]
        mx[s] = peak
        tot[s] = tot[s] * shrink + sum(weights[1:], weights[0])
        weights = jnp.concatenate([w.astype(jnp.bfloat16) for w in weights], 1)
        latent = kb[pl.ds(4 * c, 4), :, :LAT].reshape(512, LAT)
        mixed = jnp.dot(weights, latent, preferred_element_type=jnp.float32)
        shrink = jnp.concatenate([shrink] * (LAT // 128), 1)
        acc[s] = acc[s] * shrink + mixed
        if later is not None:
            hide(t + 1, later)

        @pl.when(done)
        def _():
            def group(r, _):
                for k in range(4):
                    part = pl.ds(pl.multiple_of(r * 512 + k * 128, 128), 128)
                    total = jnp.sum(tot[s, part, :], 1, keepdims=True)
                    mixed = (acc[s, part, :] * (1.0 / total)).astype(jnp.bfloat16)
                    value = jnp.dot(mixed, wv[4 * r + k], preferred_element_type=jnp.float32)
                    ob[s, :, :, part] = value.astype(jnp.bfloat16).reshape(8, 16, VH)

                @pl.when(s == 1)
                def _():
                    out_copy(r).start()

                @pl.when(s == 0)
                def _():
                    own_copy(r).start()

                return 0

            lax.fori_loop(0, 2, group, 0)

    loaded("wv")
    meet(z)
    score(0, first)
    hide(0, first)

    def serve(t):
        @pl.when(t + 1 == starts[2])
        def _():
            second_rows()

        @pl.when(t + 1 == starts[6])
        def _():
            last_row()

    def two_steps(i, _):
        serve(2 * i)
        step(2 * i, first, second)
        serve(2 * i + 1)
        step(2 * i + 1, second, first)
        return 0

    lax.fori_loop(0, 4, two_steps, 0)
    serve(8)
    step(8, first, None)
    for j in range(2):
        rows = pl.ds(pl.multiple_of(tp * 16, 16), 16)
        cache_ref[j] = kb[slot_ref[j], rows, :][:, :KV]
    for r in range(2):
        own_copy(r).wait()
        out_copy(r).wait_send()
        arrived(out_h.at[:, 1 - half, :, out_cols(r)], out_sem.at[r])
    for build in sent.values():
        build().wait_send()


def hand_over(att_h, cache_h, att_out, cache_out, att, cache, sem):
    pieces = [(cache_h, cache, cache_out)]
    for k in range(4):
        rows = pl.ds(64 * k, 64)
        pieces.append((att_h.at[rows], att.at[rows], att_out.at[rows]))
    into = [pltpu.make_async_copy(p[0], p[1], sem.at[0, k]) for k, p in enumerate(pieces)]
    out = [pltpu.make_async_copy(p[1], p[2], sem.at[1, k]) for k, p in enumerate(pieces)]
    for copy in into:
        copy.start()
    for first, second in zip(into, out):
        first.wait()
        second.start()
    for copy in out:
        copy.wait()


def per_device(tokens, w_down_q, w_down_kv, q_gain, kv_gain, w_up_q, w_absorb, w_value, slot_block):
    bf16, f32 = jnp.bfloat16, jnp.float32
    table = jnp.asarray(rotary_tables())
    hbm = pl.BlockSpec(memory_space=pl.ANY)
    dma = pltpu.SemaphoreType.DMA
    attended, cache = pl.pallas_call(
        kernel,
        out_shape=(
            jax.ShapeDtypeStruct((8, 2, 16, HEADS * VH), bf16),
            jax.ShapeDtypeStruct((2, 16, KV), bf16),
        ),
        in_specs=[hbm] * 8 + [pl.BlockSpec(memory_space=pltpu.SMEM), hbm],
        out_specs=(hbm, pl.BlockSpec(memory_space=pltpu.VMEM)),
        scratch_shapes=[
            pltpu.VMEM((256, 896), bf16),
            pltpu.VMEM((896, QL), bf16),
            pltpu.VMEM((KV, 896), bf16),
            pltpu.VMEM((QL // 128, 128), f32),
            pltpu.VMEM((LAT // 128, 128), f32),
            pltpu.VMEM((QL, HEADS * (NOPE + ROPE)), bf16),
            pltpu.VMEM((HEADS, NOPE, LAT), bf16),
            pltpu.VMEM((HEADS, LAT, VH), bf16),
            pltpu.VMEM((2, 16, 2 * ROPE), f32),
            pltpu.VMEM((2, 8, 16, 2 * ROPE), f32),
            pltpu.VMEM((128, KV), f32),
            pltpu.VMEM((128, KV), f32),
            pltpu.VMEM((128, KV), f32),
            pltpu.VMEM((128, QL), f32),
            pltpu.VMEM((128, QL), f32),
            pltpu.VMEM((128, QL), f32),
            pltpu.VMEM((6, 16, KV), bf16),
            pltpu.VMEM((6, 16, KV), bf16),
            pltpu.VMEM((6, 16, QL), f32),
            pltpu.VMEM((6, 16, QL), f32),
            pltpu.VMEM((2, 16, QL), bf16),
            pltpu.VMEM((2, 8, 16, QL), bf16),
            pltpu.VMEM((32, 128, KEYW), bf16),
            pltpu.VMEM((2, HEADS * 128, KEYW), bf16),
            pltpu.VMEM((1024, 512), f32),
            pltpu.VMEM((1024, 512), f32),
            pltpu.VMEM((2, HEADS * 128, LAT), f32),
            pltpu.VMEM((2, HEADS * 128, 128), f32),
            pltpu.VMEM((2, HEADS * 128, 128), f32),
            pltpu.VMEM((2, 8, 16, HEADS * VH), bf16),
            dma((11,)),
            dma((N_SEND,)),
            dma((2,)),
            dma((6,)),
            dma((6,)),
            dma((2, 8)),
            dma((4,)),
            dma((16, 2)),
            dma((16,)),
            dma((2,)),
            dma((2,)),
            dma((2,)),
        ],
        compiler_params=pltpu.CompilerParams(
            collective_id=0, has_side_effects=True, vmem_limit_bytes=56 * 2**20
        ),
    )(
        tokens, w_down_q, w_down_kv.T, q_gain.reshape(-1, 128), kv_gain.reshape(-1, 128),
        w_up_q, w_absorb, w_value, slot_block, table,
    )
    attended = attended.reshape(256, HEADS * VH)
    return pl.pallas_call(
        hand_over,
        out_shape=(
            jax.ShapeDtypeStruct(attended.shape, bf16),
            jax.ShapeDtypeStruct(cache.shape, bf16),
        ),
        in_specs=[hbm, hbm],
        out_specs=(hbm, hbm),
        scratch_shapes=[
            pltpu.VMEM(attended.shape, bf16),
            pltpu.VMEM(cache.shape, bf16),
            dma((2, 5)),
        ],
        compiler_params=pltpu.CompilerParams(vmem_limit_bytes=60 * 2**20),
    )(attended, cache)


def solution(mesh):
    placed = (
        P("chain", "tp"),
        P("tp", None),
        P("tp", None),
        P(),
        P(),
        P(None, "tp"),
        P("tp", None, None),
        P("tp", None, None),
        P("chain"),
    )
    return jax.shard_map(
        per_device,
        mesh=mesh,
        in_specs=placed,
        out_specs=(P("chain", "tp"), P("chain", "tp", None)),
        check_vma=False,
    )
```

```python
import functools
import math

import jax
import jax.numpy as jnp
import numpy as np
from jax import lax
from jax.experimental import pallas as pl
from jax.experimental.pallas import tpu as pltpu
from jax.sharding import PartitionSpec as P

MESH = pl.DeviceIdType.MESH
ROPE_BASE = 50000.0
FLOOR_SCORE = -1e30
QL, LAT, ROPE, NOPE, VH, HEADS = 1536, 512, 64, 128, 128, 8
KEYW = 640
KV = LAT + ROPE
SCALE2 = (NOPE + ROPE) ** -0.5 * math.log2(math.e)
NT = (((1,), (1,)), ((), ()))
N_SEND = 80
RINGS = (
    (0, 0), (3, 0), (1, 0), (0, 3), (0, 1), (2, 0), (0, 2), (3, 3), (3, 1), (1, 3), (1, 1),
    (2, 3), (2, 1), (3, 2), (1, 2), (2, 2),
)


def rotary_tables():
    inverse = ROPE_BASE ** (-2.0 * np.arange(ROPE // 2) / ROPE)
    angles = np.arange(4096)[:, None] * inverse[None, :]
    cosine = np.concatenate([np.cos(angles), np.cos(angles)], 1)
    sine = np.concatenate([-np.sin(angles), np.sin(angles)], 1)
    both = np.concatenate([cosine, sine], 1).astype(np.float32)
    return both.reshape(16, 8, 2, 16, 2 * ROPE)


def rotate(values, table):
    half = ROPE // 2
    swapped = jnp.concatenate([values[:, half:], values[:, :half]], 1)
    return values * table[:, :ROPE] + swapped * table[:, ROPE:]


def normalize(values, gain):
    return values * lax.rsqrt(jnp.mean(values * values, -1, keepdims=True) + 1e-06) * gain


def kernel(
    tok_h, wq_h, wkv_h, qg_h, kvg_h, wu_h, wa_h, wv_h, slot_ref, tab_h,
    out_h, cache_ref,
    tok, wq, wkv, qg, kvg, wu, wa, wv, tabk, tabq,
    psk, pok, prk, psq, poq, prq, rks, rkr, rqs, rqr, cs, cq, kb, qb, first, acc, mx, tot, ob,
    load_sem, send_sem, sib_sem, rk_sem, rq_sem, cq_sem, ky_sem, kp_sem, ks_sem, out_sem, outs_sem, own_sem,
):
    chain = lax.axis_index("chain")
    tp = lax.axis_index("tp")
    z, x = chain // 4, chain % 4
    y, core = tp // 2, tp % 2
    other = 1 - core
    mirror = 15 - chain
    half = chain // 8
    piece = core * 4 + y
    yp, ym, yf = (y + 1) % 4, (y + 3) % 4, (y + 2) % 4
    sibling = {"chain": chain, "tp": 2 * y + other}
    up = {"chain": chain, "tp": 2 * yp + core}
    down = {"chain": chain, "tp": 2 * ym + core}
    pair = {"chain": mirror, "tp": tp}
    a = x + core * (z - x)
    b = z + core * (x - z)
    stride_a, stride_b = 1 + 3 * core, 4 - 3 * core

    def at(da, db):
        return ((a + da) % 4) * stride_a + ((b + db) % 4) * stride_b

    ap = {"chain": at(1, 0), "tp": tp}
    am = {"chain": at(3, 0), "tp": tp}
    bp = {"chain": at(0, 1), "tp": tp}
    bm = {"chain": at(0, 3), "tp": tp}

    loads = {}
    for k, (name, src, dst) in enumerate(
        [
            ("tok", tok_h, tok), ("wkv", wkv_h, wkv), ("wq", wq_h, wq), ("kvg", kvg_h, kvg),
            ("qg", qg_h, qg), ("tabk", tab_h.at[chain, piece], tabk), ("wa", wa_h, wa),
            ("wu", wu_h, wu), ("wv", wv_h, wv), ("tab0", tab_h.at[chain, :, half], tabq.at[0]),
            ("tab1", tab_h.at[mirror, :, half], tabq.at[1]),
        ]
    ):
        loads[name] = pltpu.make_async_copy(src, dst, load_sem.at[k])
        if name in ("tok", "wkv", "kvg", "tabk"):
            loads[name].start()

    def loaded(*names):
        for name in names:
            loads[name].wait()

    barrier = pltpu.get_barrier_semaphore()
    partners = (sibling, up, down, pair, ap, am, bp, bm)
    for device in partners:
        pl.semaphore_signal(barrier, inc=1, device_id=device, device_id_type=MESH)
    for name in ("wq", "qg"):
        loads[name].start()

    sent = []

    def send(src, dst, recv, device):
        copy = pltpu.make_async_remote_copy(
            src_ref=src, dst_ref=dst, send_sem=send_sem.at[len(sent)], recv_sem=recv,
            device_id=device, device_id_type=MESH,
        )
        copy.start()
        sent.append(copy)

    def arrived(dst, recv):
        pltpu.make_async_remote_copy(
            src_ref=dst, dst_ref=dst, send_sem=send_sem.at[0], recv_sem=recv,
            device_id=sibling, device_id_type=MESH,
        ).wait_recv()

    def rows_of(c):
        return tok[pl.ds(pl.multiple_of(c * 128, 128), 128), :]

    def project_keys(c, dst):
        dst[...] = lax.dot_general(rows_of(c), wkv[...], NT, preferred_element_type=jnp.float32)

    def project_queries(c, dst):
        left = rows_of(c)

        def tile(i, _):
            cols = pl.ds(pl.multiple_of(i * 512, 512), 512)
            dst[:, cols] = jnp.dot(left, wq[:, cols], preferred_element_type=jnp.float32)
            return 0

        lax.fori_loop(0, 3, tile, 0)

    def ring_of(own, got, out, came, sems):
        def part(yy, h):
            rows = pl.ds(pl.multiple_of(yy * 32 + h * 16, 16), 16)
            return own[rows, :] + got[rows, :]

        def push(k, value, device):
            out[k] = value.astype(out.dtype)
            send(out.at[k], came.at[k], sems.at[k], device)

        def start():
            push(0, part(yf, 0), up)
            push(1, part(yf, 1), down)
            push(2, part(yp, 1), up)
            push(3, part(ym, 0), down)

        def middle():
            arrived(came.at[0], sems.at[0])
            push(4, part(yp, 0) + came[0].astype(jnp.float32), up)
            arrived(came.at[1], sems.at[1])
            push(5, part(ym, 1) + came[1].astype(jnp.float32), down)

        def end():
            for k in (2, 3, 4, 5):
                arrived(came.at[k], sems.at[k])
            totals = []
            for h, first, second in ((0, 4, 3), (1, 2, 5)):
                total = part(y, h) + came[first].astype(jnp.float32)
                totals.append(total + came[second].astype(jnp.float32))
            return totals

        return start, middle, end

    keys_start, keys_middle, keys_end = ring_of(pok, prk, rks, rkr, rk_sem)
    queries_start, queries_middle, queries_end = ring_of(poq, prq, rqs, rqr, rq_sem)

    loaded("tok", "wkv")
    project_keys(other, psk)
    pl.semaphore_wait(barrier, len(partners))
    send(psk, prk, sib_sem.at[0], sibling)
    project_keys(core, pok)
    arrived(prk, sib_sem.at[0])
    keys_start()
    loaded("wq")
    for name in ("wa", "wu", "wv", "tab0", "tab1"):
        loads[name].start()
    project_queries(other, psq)
    send(psq, prq, sib_sem.at[1], sibling)
    keys_middle()
    project_queries(core, poq)

    slot_own = 2 * chain + core

    def keys_y(yy, h, n):
        return kb.at[slot_own, pl.ds(pl.multiple_of(yy * 32 + h * 16, 16), n)]

    loaded("kvg", "tabk")
    gain_kv = jnp.concatenate([kvg[k : k + 1, :] for k in range(LAT // 128)], 1)
    for h, total in enumerate(keys_end()):
        latent = normalize(total[:, :LAT], gain_kv)
        turned = rotate(total[:, LAT:], tabk[h])
        rows = pl.ds(pl.multiple_of(y * 32 + h * 16, 16), 16)
        kb[slot_own, rows, :LAT] = latent.astype(jnp.bfloat16)
        kb[slot_own, rows, LAT:] = jnp.concatenate(
            [turned, jnp.zeros_like(turned)], 1
        ).astype(jnp.bfloat16)
    for k, device in enumerate((up, down)):
        send(keys_y(y, 0, 32), keys_y(y, 0, 32), ky_sem.at[k], device)
    arrived(prq, sib_sem.at[1])
    queries_start()
    arrived(keys_y(ym, 0, 32), ky_sem.at[0])
    send(keys_y(ym, 0, 16), keys_y(ym, 0, 16), ky_sem.at[2], up)
    arrived(keys_y(yp, 0, 32), ky_sem.at[1])
    send(keys_y(yp, 1, 16), keys_y(yp, 1, 16), ky_sem.at[3], down)

    def block(n, p=None):
        if p is None:
            return kb.at[2 * n + core]
        return kb.at[2 * n + core, pl.ds(64 * p, 64)]

    def pass_on(n, *devices):
        for device in devices:
            send(block(n), block(n), kp_sem.at[n, 0], device)
        send(block(n), block(n), ks_sem.at[n], sibling)

    def pass_part(n, p, device):
        send(block(n, p), block(n, p), kp_sem.at[n, p], device)

    def whole(n):
        arrived(block(n), kp_sem.at[n, 0])

    def halves(n):
        for p in range(2):
            arrived(block(n, p), kp_sem.at[n, p])

    def relay(u, v):
        n = at(u, v)
        if v == 2 or (u, v) == (2, 0):
            halves(n)
        else:
            whole(n)
        if v == 0:
            if u != 2:
                pass_part(n, 0 if u == 3 else 1, ap if u == 3 else am)
            pass_on(n, bp, bm)
        else:
            if v != 2:
                pass_part(n, 0 if v == 3 else 1, bp if v == 3 else bm)
            pass_on(n)

    arrived(keys_y(yf, 0, 16), ky_sem.at[2])
    arrived(keys_y(yf, 1, 16), ky_sem.at[3])
    pass_on(at(0, 0), ap, am, bp, bm)
    acc[...] = jnp.zeros_like(acc)
    tot[...] = jnp.zeros_like(tot)
    mx[...] = jnp.full_like(mx, FLOOR_SCORE)
    queries_middle()
    for u, v in RINGS[1:5]:
        relay(u, v)

    loaded("qg")
    gain_q = jnp.concatenate([qg[k : k + 1, :] for k in range(QL // 128)], 1)
    for h, total in enumerate(queries_end()):
        cs[h] = normalize(total, gain_q).astype(jnp.bfloat16)

    def give(s, p, *devices):
        for device in devices:
            send(cq.at[s, p], cq.at[s, p], cq_sem.at[s, p], device)

    def take(s, p):
        arrived(cq.at[s, p], cq_sem.at[s, p])

    send(cs.at[1 - half], cq.at[1, piece], cq_sem.at[1, piece], pair)
    cq[0, piece] = cs[half]
    give(0, piece, up, down, sibling)
    pm, pp, pf = core * 4 + ym, core * 4 + yp, core * 4 + yf
    for u, v in RINGS[5:7]:
        relay(u, v)
    take(1, piece)
    give(1, piece, up, down, sibling)
    take(0, pm)
    give(0, pm, up, sibling)
    take(0, pp)
    give(0, pp, sibling)
    for u, v in RINGS[7:11]:
        relay(u, v)
    take(1, pp)
    give(1, pp, down, sibling)
    take(1, pm)
    give(1, pm, sibling)
    take(0, pf)
    give(0, pf, sibling)
    for u, v in RINGS[11:15]:
        relay(u, v)
    take(1, pf)
    give(1, pf, sibling)
    for s in range(2):
        for yy in range(4):
            take(s, other * 4 + yy)

    loaded("wa", "wu", "tab0", "tab1")

    def expand(i, _):
        cols = pl.ds(pl.multiple_of(i * 384, 384), 384)
        rows = cq[...].reshape(256, QL)
        projected = jnp.dot(rows, wu[:, cols], preferred_element_type=jnp.float32)
        table = tabq[...].reshape(256, 2 * ROPE)
        for j in range(2):
            head = 2 * i + j
            base = j * (NOPE + ROPE)
            nope = projected[:, base : base + NOPE].astype(jnp.bfloat16)
            turned = rotate(projected[:, base + NOPE : base + NOPE + ROPE], table)
            turned = jnp.concatenate([turned, jnp.zeros_like(turned)], 1).astype(jnp.bfloat16)
            absorbed = jnp.dot(nope, wa[head], preferred_element_type=jnp.float32)
            absorbed = absorbed.astype(jnp.bfloat16)
            places = pl.ds(pl.multiple_of(head * 128, 128), 128)
            for s in range(2):
                qb[s, places, :LAT] = absorbed[s * 128 : s * 128 + 128]
                qb[s, places, LAT:] = turned[s * 128 : s * 128 + 128]
        return 0

    lax.fori_loop(0, HEADS // 2, expand, 0)
    relay(2, 2)
    for n in range(16):
        arrived(kb.at[2 * n + other], ks_sem.at[n])

    token = lax.broadcasted_iota(jnp.int32, (512, 1), 0) & 127
    place = ((token >> 4) << 5) + (token & 15) + half * 16
    key_iota = lax.broadcasted_iota(jnp.int32, (1, 1024), 1)

    def score(s, c, r, size):
        keys = kb[pl.ds(8 * c, size // 128)].reshape(size, KEYW)
        queries = qb[s, 512 * r : 512 * r + 512, :]
        return lax.dot_general(queries, keys, NT, preferred_element_type=jnp.float32)

    def chunk(s, c, blk, size, last):
        ahead = first[:, :size]
        for r in range(2):
            rows = slice(512 * r, 512 * r + 512)
            scores = ahead * SCALE2
            if r < 1:
                ahead = score(s, c, r + 1, size)
            elif not last:
                first[...] = score(s, c + 1, 0, size)
            if last:
                visible = key_iota[:, :size] + 1024 * c <= place + 256 * blk
                scores = jnp.where(visible, scores, FLOOR_SCORE)
            parts = [scores[:, k : k + 128] for k in range(0, size, 128)]
            before = mx[s, rows, :]
            top = jnp.max(functools.reduce(jnp.maximum, parts), 1, keepdims=True)
            peak = jnp.maximum(before, top)
            shrink = jnp.exp2(before - peak)
            weights = [jnp.exp2(p - peak) for p in parts]
            mx[s, rows, :] = peak
            tot[s, rows, :] = tot[s, rows, :] * shrink + sum(weights[1:], weights[0])
            weights = jnp.concatenate([w.astype(jnp.bfloat16) for w in weights], 1)
            latent = kb[pl.ds(8 * c, size // 128), :, :LAT].reshape(size, LAT)
            mixed = jnp.dot(weights, latent, preferred_element_type=jnp.float32)
            shrink = jnp.concatenate([shrink] * (LAT // 128), 1)
            acc[s, rows, :] = acc[s, rows, :] * shrink + mixed

    def attend(s, blk):
        first[...] = score(s, 0, 0, 1024)

        def step(c, _):
            chunk(s, c, blk, 1024, False)
            return 0

        lax.fori_loop(0, blk // 4, step, 0)

        @pl.when(blk % 4 >= 2)
        def _():
            chunk(s, blk // 4, blk, 1024, True)

        @pl.when(blk % 4 < 2)
        def _():
            chunk(s, blk // 4, blk, 512, True)

    def out_cols(r):
        return pl.ds(pl.multiple_of(r * 512, 512), 512)

    def out_copy(r):
        return pltpu.make_async_remote_copy(
            src_ref=ob.at[1, :, :, out_cols(r)], dst_ref=out_h.at[:, half, :, out_cols(r)],
            send_sem=outs_sem.at[r], recv_sem=out_sem.at[r], device_id=pair, device_id_type=MESH,
        )

    def own_copy(r):
        return pltpu.make_async_copy(
            ob.at[0, :, :, out_cols(r)], out_h.at[:, half, :, out_cols(r)], own_sem.at[r]
        )

    def finish(s):
        def group(r, _):
            for k in range(4):
                part = pl.ds(pl.multiple_of(r * 512 + k * 128, 128), 128)
                total = jnp.sum(tot[s, part, :], 1, keepdims=True)
                mixed = (acc[s, part, :] * (1.0 / total)).astype(jnp.bfloat16)
                value = jnp.dot(mixed, wv[4 * r + k], preferred_element_type=jnp.float32)
                ob[s, :, :, part] = value.astype(jnp.bfloat16).reshape(8, 16, VH)
            (own_copy, out_copy)[s](r).start()
            return 0

        lax.fori_loop(0, 2, group, 0)

    loaded("wv")
    attend(1, mirror)
    finish(1)
    attend(0, chain)
    finish(0)
    for j in range(2):
        rows = pl.ds(pl.multiple_of(tp * 16, 16), 16)
        cache_ref[j] = kb[slot_ref[j], rows, :][:, :KV]
    for r in range(2):
        own_copy(r).wait()
        out_copy(r).wait_send()
        arrived(out_h.at[:, 1 - half, :, out_cols(r)], out_sem.at[r])
    for copy in sent:
        copy.wait_send()


def hand_over(att_h, cache_h, att_out, cache_out, att, cache, sem):
    pieces = [(cache_h, cache, cache_out)]
    for k in range(4):
        rows = pl.ds(64 * k, 64)
        pieces.append((att_h.at[rows], att.at[rows], att_out.at[rows]))
    into = [pltpu.make_async_copy(p[0], p[1], sem.at[0, k]) for k, p in enumerate(pieces)]
    out = [pltpu.make_async_copy(p[1], p[2], sem.at[1, k]) for k, p in enumerate(pieces)]
    for copy in into:
        copy.start()
    for first, second in zip(into, out):
        first.wait()
        second.start()
    for copy in out:
        copy.wait()


def per_device(tokens, w_down_q, w_down_kv, q_gain, kv_gain, w_up_q, w_absorb, w_value, slot_block):
    bf16, f32 = jnp.bfloat16, jnp.float32
    table = jnp.asarray(rotary_tables())
    hbm = pl.BlockSpec(memory_space=pl.ANY)
    dma = pltpu.SemaphoreType.DMA
    attended, cache = pl.pallas_call(
        kernel,
        out_shape=(
            jax.ShapeDtypeStruct((8, 2, 16, HEADS * VH), bf16),
            jax.ShapeDtypeStruct((2, 16, KV), bf16),
        ),
        in_specs=[hbm] * 8 + [pl.BlockSpec(memory_space=pltpu.SMEM), hbm],
        out_specs=(hbm, pl.BlockSpec(memory_space=pltpu.VMEM)),
        scratch_shapes=[
            pltpu.VMEM((256, 896), bf16),
            pltpu.VMEM((896, QL), bf16),
            pltpu.VMEM((KV, 896), bf16),
            pltpu.VMEM((QL // 128, 128), f32),
            pltpu.VMEM((LAT // 128, 128), f32),
            pltpu.VMEM((QL, HEADS * (NOPE + ROPE)), bf16),
            pltpu.VMEM((HEADS, NOPE, LAT), bf16),
            pltpu.VMEM((HEADS, LAT, VH), bf16),
            pltpu.VMEM((2, 16, 2 * ROPE), f32),
            pltpu.VMEM((2, 8, 16, 2 * ROPE), f32),
            pltpu.VMEM((128, KV), f32),
            pltpu.VMEM((128, KV), f32),
            pltpu.VMEM((128, KV), f32),
            pltpu.VMEM((128, QL), f32),
            pltpu.VMEM((128, QL), f32),
            pltpu.VMEM((128, QL), f32),
            pltpu.VMEM((6, 16, KV), bf16),
            pltpu.VMEM((6, 16, KV), bf16),
            pltpu.VMEM((6, 16, QL), f32),
            pltpu.VMEM((6, 16, QL), f32),
            pltpu.VMEM((2, 16, QL), bf16),
            pltpu.VMEM((2, 8, 16, QL), bf16),
            pltpu.VMEM((32, 128, KEYW), bf16),
            pltpu.VMEM((2, HEADS * 128, KEYW), bf16),
            pltpu.VMEM((512, 1024), f32),
            pltpu.VMEM((2, HEADS * 128, LAT), f32),
            pltpu.VMEM((2, HEADS * 128, 128), f32),
            pltpu.VMEM((2, HEADS * 128, 128), f32),
            pltpu.VMEM((2, 8, 16, HEADS * VH), bf16),
            dma((11,)),
            dma((N_SEND,)),
            dma((2,)),
            dma((6,)),
            dma((6,)),
            dma((2, 8)),
            dma((4,)),
            dma((16, 2)),
            dma((16,)),
            dma((2,)),
            dma((2,)),
            dma((2,)),
        ],
        compiler_params=pltpu.CompilerParams(
            collective_id=0, has_side_effects=True, vmem_limit_bytes=56 * 2**20
        ),
    )(
        tokens, w_down_q, w_down_kv.T, q_gain.reshape(-1, 128), kv_gain.reshape(-1, 128),
        w_up_q, w_absorb, w_value, slot_block, table,
    )
    attended = attended.reshape(256, HEADS * VH)
    return pl.pallas_call(
        hand_over,
        out_shape=(
            jax.ShapeDtypeStruct(attended.shape, bf16),
            jax.ShapeDtypeStruct(cache.shape, bf16),
        ),
        in_specs=[hbm, hbm],
        out_specs=(hbm, hbm),
        scratch_shapes=[
            pltpu.VMEM(attended.shape, bf16),
            pltpu.VMEM(cache.shape, bf16),
            dma((2, 5)),
        ],
        compiler_params=pltpu.CompilerParams(vmem_limit_bytes=60 * 2**20),
    )(attended, cache)


def solution(mesh):
    placed = (
        P("chain", "tp"),
        P("tp", None),
        P("tp", None),
        P(),
        P(),
        P(None, "tp"),
        P("tp", None, None),
        P("tp", None, None),
        P("chain"),
    )
    return jax.shard_map(
        per_device,
        mesh=mesh,
        in_specs=placed,
        out_specs=(P("chain", "tp"), P("chain", "tp", None)),
        check_vma=False,
    )
```

```python
import functools
import math

import jax
import jax.numpy as jnp
import numpy as np
from jax import lax
from jax.experimental import pallas as pl
from jax.experimental.pallas import tpu as pltpu
from jax.sharding import PartitionSpec as P

MESH = pl.DeviceIdType.MESH
ROPE_BASE = 50000.0
FLOOR_SCORE = -1e30
QL, LAT, ROPE, NOPE, VH, HEADS = 1536, 512, 64, 128, 128, 8
KEYW = 640
KV = LAT + ROPE
SCALE2 = (NOPE + ROPE) ** -0.5 * math.log2(math.e)
NT = (((1,), (1,)), ((), ()))
N_SEND = 80
RINGS = (
    (0, 0), (3, 0), (1, 0), (0, 3), (0, 1), (2, 0), (0, 2), (3, 3), (3, 1), (1, 3), (1, 1),
    (2, 3), (2, 1), (3, 2), (1, 2), (2, 2),
)


def rotary_tables():
    inverse = ROPE_BASE ** (-2.0 * np.arange(ROPE // 2) / ROPE)
    angles = np.arange(4096)[:, None] * inverse[None, :]
    cosine = np.concatenate([np.cos(angles), np.cos(angles)], 1)
    sine = np.concatenate([-np.sin(angles), np.sin(angles)], 1)
    both = np.concatenate([cosine, sine], 1).astype(np.float32)
    return both.reshape(16, 8, 2, 16, 2 * ROPE)


def rotate(values, table):
    half = ROPE // 2
    swapped = jnp.concatenate([values[:, half:], values[:, :half]], 1)
    return values * table[:, :ROPE] + swapped * table[:, ROPE:]


def normalize(values, gain):
    return values * lax.rsqrt(jnp.mean(values * values, -1, keepdims=True) + 1e-06) * gain


def kernel(
    tok_h, wq_h, wkv_h, qg_h, kvg_h, wu_h, wa_h, wv_h, slot_ref, tab_h,
    out_h, cache_ref,
    tok, wq, wkv, qg, kvg, wu, wa, wv, tabk, tabq,
    psk, pok, prk, psq, poq, prq, rks, rkr, rqs, rqr, cs, cq, kb, qb, first, acc, mx, tot, ob,
    load_sem, send_sem, sib_sem, rk_sem, rq_sem, cq_sem, ky_sem, kp_sem, ks_sem, out_sem, outs_sem, own_sem,
):
    chain = lax.axis_index("chain")
    tp = lax.axis_index("tp")
    z, x = chain // 4, chain % 4
    y, core = tp // 2, tp % 2
    other = 1 - core
    mirror = 15 - chain
    half = chain // 8
    piece = core * 4 + y
    yp, ym, yf = (y + 1) % 4, (y + 3) % 4, (y + 2) % 4
    sibling = {"chain": chain, "tp": 2 * y + other}
    up = {"chain": chain, "tp": 2 * yp + core}
    down = {"chain": chain, "tp": 2 * ym + core}
    pair = {"chain": mirror, "tp": tp}
    a = x + core * (z - x)
    b = z + core * (x - z)
    stride_a, stride_b = 1 + 3 * core, 4 - 3 * core

    def at(da, db):
        return ((a + da) % 4) * stride_a + ((b + db) % 4) * stride_b

    ap = {"chain": at(1, 0), "tp": tp}
    am = {"chain": at(3, 0), "tp": tp}
    bp = {"chain": at(0, 1), "tp": tp}
    bm = {"chain": at(0, 3), "tp": tp}

    loads = {}
    for k, (name, src, dst) in enumerate(
        [
            ("tok", tok_h, tok), ("wkv", wkv_h, wkv), ("wq", wq_h, wq), ("kvg", kvg_h, kvg),
            ("qg", qg_h, qg), ("tabk", tab_h.at[chain, piece], tabk), ("wa", wa_h, wa),
            ("wu", wu_h, wu), ("wv", wv_h, wv), ("tab0", tab_h.at[chain, :, half], tabq.at[0]),
            ("tab1", tab_h.at[mirror, :, half], tabq.at[1]),
        ]
    ):
        loads[name] = pltpu.make_async_copy(src, dst, load_sem.at[k])
        if name in ("tok", "wkv", "kvg", "tabk"):
            loads[name].start()

    def loaded(*names):
        for name in names:
            loads[name].wait()

    barrier = pltpu.get_barrier_semaphore()
    partners = (sibling, up, down, pair, ap, am, bp, bm)
    for device in partners:
        pl.semaphore_signal(barrier, inc=1, device_id=device, device_id_type=MESH)
    for name in ("wq", "qg"):
        loads[name].start()

    sent = []

    def send(src, dst, recv, device):
        copy = pltpu.make_async_remote_copy(
            src_ref=src, dst_ref=dst, send_sem=send_sem.at[len(sent)], recv_sem=recv,
            device_id=device, device_id_type=MESH,
        )
        copy.start()
        sent.append(copy)

    def arrived(dst, recv):
        pltpu.make_async_remote_copy(
            src_ref=dst, dst_ref=dst, send_sem=send_sem.at[0], recv_sem=recv,
            device_id=sibling, device_id_type=MESH,
        ).wait_recv()

    def rows_of(c):
        return tok[pl.ds(pl.multiple_of(c * 128, 128), 128), :]

    def project_keys(c, dst):
        dst[...] = lax.dot_general(rows_of(c), wkv[...], NT, preferred_element_type=jnp.float32)

    def project_queries(c, dst):
        left = rows_of(c)

        def tile(i, _):
            cols = pl.ds(pl.multiple_of(i * 512, 512), 512)
            dst[:, cols] = jnp.dot(left, wq[:, cols], preferred_element_type=jnp.float32)
            return 0

        lax.fori_loop(0, 3, tile, 0)

    def ring_of(own, got, out, came, sems):
        def part(yy, h):
            rows = pl.ds(pl.multiple_of(yy * 32 + h * 16, 16), 16)
            return own[rows, :] + got[rows, :]

        def push(k, value, device):
            out[k] = value.astype(out.dtype)
            send(out.at[k], came.at[k], sems.at[k], device)

        def start():
            push(0, part(yf, 0), up)
            push(1, part(yf, 1), down)
            push(2, part(yp, 1), up)
            push(3, part(ym, 0), down)

        def middle():
            arrived(came.at[0], sems.at[0])
            push(4, part(yp, 0) + came[0].astype(jnp.float32), up)
            arrived(came.at[1], sems.at[1])
            push(5, part(ym, 1) + came[1].astype(jnp.float32), down)

        def end():
            for k in (2, 3, 4, 5):
                arrived(came.at[k], sems.at[k])
            totals = []
            for h, first, second in ((0, 4, 3), (1, 2, 5)):
                total = part(y, h) + came[first].astype(jnp.float32)
                totals.append(total + came[second].astype(jnp.float32))
            return totals

        return start, middle, end

    keys_start, keys_middle, keys_end = ring_of(pok, prk, rks, rkr, rk_sem)
    queries_start, queries_middle, queries_end = ring_of(poq, prq, rqs, rqr, rq_sem)

    loaded("tok", "wkv")
    project_keys(other, psk)
    pl.semaphore_wait(barrier, len(partners))
    send(psk, prk, sib_sem.at[0], sibling)
    project_keys(core, pok)
    arrived(prk, sib_sem.at[0])
    keys_start()
    loaded("wq")
    for name in ("wa", "wu", "wv", "tab0", "tab1"):
        loads[name].start()
    project_queries(other, psq)
    send(psq, prq, sib_sem.at[1], sibling)
    keys_middle()
    project_queries(core, poq)
    arrived(prq, sib_sem.at[1])
    queries_start()

    slot_own = 2 * chain + core

    def keys_y(yy, h, n):
        return kb.at[slot_own, pl.ds(pl.multiple_of(yy * 32 + h * 16, 16), n)]

    loaded("kvg", "tabk")
    gain_kv = jnp.concatenate([kvg[k : k + 1, :] for k in range(LAT // 128)], 1)
    for h, total in enumerate(keys_end()):
        latent = normalize(total[:, :LAT], gain_kv)
        turned = rotate(total[:, LAT:], tabk[h])
        rows = pl.ds(pl.multiple_of(y * 32 + h * 16, 16), 16)
        kb[slot_own, rows, :LAT] = latent.astype(jnp.bfloat16)
        kb[slot_own, rows, LAT:] = jnp.concatenate(
            [turned, jnp.zeros_like(turned)], 1
        ).astype(jnp.bfloat16)
    for k, device in enumerate((up, down)):
        send(keys_y(y, 0, 32), keys_y(y, 0, 32), ky_sem.at[k], device)
    arrived(keys_y(ym, 0, 32), ky_sem.at[0])
    send(keys_y(ym, 0, 16), keys_y(ym, 0, 16), ky_sem.at[2], up)
    arrived(keys_y(yp, 0, 32), ky_sem.at[1])
    send(keys_y(yp, 1, 16), keys_y(yp, 1, 16), ky_sem.at[3], down)

    def block(n, p=None):
        if p is None:
            return kb.at[2 * n + core]
        return kb.at[2 * n + core, pl.ds(64 * p, 64)]

    def pass_on(n, *devices):
        for device in devices:
            send(block(n), block(n), kp_sem.at[n, 0], device)
        send(block(n), block(n), ks_sem.at[n], sibling)

    def pass_part(n, p, device):
        send(block(n, p), block(n, p), kp_sem.at[n, p], device)

    def whole(n):
        arrived(block(n), kp_sem.at[n, 0])

    def halves(n):
        for p in range(2):
            arrived(block(n, p), kp_sem.at[n, p])

    def relay(u, v):
        n = at(u, v)
        if v == 2 or (u, v) == (2, 0):
            halves(n)
        else:
            whole(n)
        if v == 0:
            if u != 2:
                pass_part(n, 0 if u == 3 else 1, ap if u == 3 else am)
            pass_on(n, bp, bm)
        else:
            if v != 2:
                pass_part(n, 0 if v == 3 else 1, bp if v == 3 else bm)
            pass_on(n)

    arrived(keys_y(yf, 0, 16), ky_sem.at[2])
    arrived(keys_y(yf, 1, 16), ky_sem.at[3])
    pass_on(at(0, 0), ap, am, bp, bm)
    acc[...] = jnp.zeros_like(acc)
    tot[...] = jnp.zeros_like(tot)
    mx[...] = jnp.full_like(mx, FLOOR_SCORE)
    queries_middle()

    loaded("qg")
    gain_q = jnp.concatenate([qg[k : k + 1, :] for k in range(QL // 128)], 1)
    for h, total in enumerate(queries_end()):
        cs[h] = normalize(total, gain_q).astype(jnp.bfloat16)

    def give(s, p, *devices):
        for device in devices:
            send(cq.at[s, p], cq.at[s, p], cq_sem.at[s, p], device)

    def take(s, p):
        arrived(cq.at[s, p], cq_sem.at[s, p])

    send(cs.at[1 - half], cq.at[1, piece], cq_sem.at[1, piece], pair)
    cq[0, piece] = cs[half]
    give(0, piece, up, down, sibling)
    pm, pp, pf = core * 4 + ym, core * 4 + yp, core * 4 + yf
    for u, v in RINGS[1:7]:
        relay(u, v)
    take(1, piece)
    give(1, piece, up, down, sibling)
    take(0, pm)
    give(0, pm, up, sibling)
    take(0, pp)
    give(0, pp, sibling)
    for u, v in RINGS[7:11]:
        relay(u, v)
    take(1, pp)
    give(1, pp, down, sibling)
    take(1, pm)
    give(1, pm, sibling)
    take(0, pf)
    give(0, pf, sibling)
    for u, v in RINGS[11:15]:
        relay(u, v)
    take(1, pf)
    give(1, pf, sibling)
    for s in range(2):
        for yy in range(4):
            take(s, other * 4 + yy)

    loaded("wa", "wu", "tab0", "tab1")

    def expand(i, _):
        cols = pl.ds(pl.multiple_of(i * 384, 384), 384)
        rows = cq[...].reshape(256, QL)
        projected = jnp.dot(rows, wu[:, cols], preferred_element_type=jnp.float32)
        table = tabq[...].reshape(256, 2 * ROPE)
        for j in range(2):
            head = 2 * i + j
            base = j * (NOPE + ROPE)
            nope = projected[:, base : base + NOPE].astype(jnp.bfloat16)
            turned = rotate(projected[:, base + NOPE : base + NOPE + ROPE], table)
            turned = jnp.concatenate([turned, jnp.zeros_like(turned)], 1).astype(jnp.bfloat16)
            absorbed = jnp.dot(nope, wa[head], preferred_element_type=jnp.float32)
            absorbed = absorbed.astype(jnp.bfloat16)
            places = pl.ds(pl.multiple_of(head * 128, 128), 128)
            for s in range(2):
                qb[s, places, :LAT] = absorbed[s * 128 : s * 128 + 128]
                qb[s, places, LAT:] = turned[s * 128 : s * 128 + 128]
        return 0

    lax.fori_loop(0, HEADS // 2, expand, 0)
    relay(2, 2)

    def meet(c):
        for k in range(4):
            n = 4 * c + k
            arrived(kb.at[2 * n + other], ks_sem.at[n])

    meet(0)

    token = lax.broadcasted_iota(jnp.int32, (512, 1), 0) & 127
    place = ((token >> 4) << 5) + (token & 15) + half * 16
    key_iota = lax.broadcasted_iota(jnp.int32, (1, 1024), 1)

    def score(s, c, r, size):
        keys = kb[pl.ds(8 * c, size // 128)].reshape(size, KEYW)
        queries = qb[s, 512 * r : 512 * r + 512, :]
        return lax.dot_general(queries, keys, NT, preferred_element_type=jnp.float32)

    def chunk(s, c, blk, size, last):
        ahead = first[:, :size]
        for r in range(2):
            rows = slice(512 * r, 512 * r + 512)
            scores = ahead * SCALE2
            if r < 1:
                ahead = score(s, c, r + 1, size)
            elif not last:
                first[...] = score(s, c + 1, 0, size)
            elif s == 1:
                first[...] = score(0, 0, 0, 1024)
            if last:
                visible = key_iota[:, :size] + 1024 * c <= place + 256 * blk
                scores = jnp.where(visible, scores, FLOOR_SCORE)
            parts = [scores[:, k : k + 128] for k in range(0, size, 128)]
            before = mx[s, rows, :]
            top = jnp.max(functools.reduce(jnp.maximum, parts), 1, keepdims=True)
            peak = jnp.maximum(before, top)
            shrink = jnp.exp2(before - peak)
            weights = [jnp.exp2(p - peak) for p in parts]
            mx[s, rows, :] = peak
            tot[s, rows, :] = tot[s, rows, :] * shrink + sum(weights[1:], weights[0])
            weights = jnp.concatenate([w.astype(jnp.bfloat16) for w in weights], 1)
            latent = kb[pl.ds(8 * c, size // 128), :, :LAT].reshape(size, LAT)
            mixed = jnp.dot(weights, latent, preferred_element_type=jnp.float32)
            shrink = jnp.concatenate([shrink] * (LAT // 128), 1)
            acc[s, rows, :] = acc[s, rows, :] * shrink + mixed

    def attend(s, blk, met):
        def step(c, _):
            @pl.when(c + 1 > met)
            def _():
                meet(c + 1)

            chunk(s, c, blk, 1024, False)
            return 0

        lax.fori_loop(0, blk // 4, step, 0)
        for k in range(4):
            @pl.when(blk % 4 == k)
            def _():
                chunk(s, blk // 4, blk, 256 * k + 256, True)

    def out_cols(r):
        return pl.ds(pl.multiple_of(r * 512, 512), 512)

    def out_copy(r):
        return pltpu.make_async_remote_copy(
            src_ref=ob.at[1, :, :, out_cols(r)], dst_ref=out_h.at[:, half, :, out_cols(r)],
            send_sem=outs_sem.at[r], recv_sem=out_sem.at[r], device_id=pair, device_id_type=MESH,
        )

    def own_copy(r):
        return pltpu.make_async_copy(
            ob.at[0, :, :, out_cols(r)], out_h.at[:, half, :, out_cols(r)], own_sem.at[r]
        )

    def finish(s):
        def group(r, _):
            for k in range(4):
                part = pl.ds(pl.multiple_of(r * 512 + k * 128, 128), 128)
                total = jnp.sum(tot[s, part, :], 1, keepdims=True)
                mixed = (acc[s, part, :] * (1.0 / total)).astype(jnp.bfloat16)
                value = jnp.dot(mixed, wv[4 * r + k], preferred_element_type=jnp.float32)
                ob[s, :, :, part] = value.astype(jnp.bfloat16).reshape(8, 16, VH)
            (own_copy, out_copy)[s](r).start()
            return 0

        lax.fori_loop(0, 2, group, 0)

    loaded("wv")
    first[...] = score(1, 0, 0, 1024)
    attend(1, mirror, 0)
    finish(1)
    attend(0, chain, 3 - z)
    finish(0)

    def rest(c, _):
        meet(c)
        return 0

    lax.fori_loop(jnp.maximum(3 - z, z) + 1, 4, rest, 0)
    for j in range(2):
        rows = pl.ds(pl.multiple_of(tp * 16, 16), 16)
        cache_ref[j] = kb[slot_ref[j], rows, :][:, :KV]
    for r in range(2):
        own_copy(r).wait()
        out_copy(r).wait_send()
        arrived(out_h.at[:, 1 - half, :, out_cols(r)], out_sem.at[r])
    for copy in sent:
        copy.wait_send()


def hand_over(att_h, cache_h, att_out, cache_out, att, cache, sem):
    pieces = [(cache_h, cache, cache_out)]
    for k in range(4):
        rows = pl.ds(64 * k, 64)
        pieces.append((att_h.at[rows], att.at[rows], att_out.at[rows]))
    into = [pltpu.make_async_copy(p[0], p[1], sem.at[0, k]) for k, p in enumerate(pieces)]
    out = [pltpu.make_async_copy(p[1], p[2], sem.at[1, k]) for k, p in enumerate(pieces)]
    for copy in into:
        copy.start()
    for first, second in zip(into, out):
        first.wait()
        second.start()
    for copy in out:
        copy.wait()


def per_device(tokens, w_down_q, w_down_kv, q_gain, kv_gain, w_up_q, w_absorb, w_value, slot_block):
    bf16, f32 = jnp.bfloat16, jnp.float32
    table = jnp.asarray(rotary_tables())
    hbm = pl.BlockSpec(memory_space=pl.ANY)
    dma = pltpu.SemaphoreType.DMA
    attended, cache = pl.pallas_call(
        kernel,
        out_shape=(
            jax.ShapeDtypeStruct((8, 2, 16, HEADS * VH), bf16),
            jax.ShapeDtypeStruct((2, 16, KV), bf16),
        ),
        in_specs=[hbm] * 8 + [pl.BlockSpec(memory_space=pltpu.SMEM), hbm],
        out_specs=(hbm, pl.BlockSpec(memory_space=pltpu.VMEM)),
        scratch_shapes=[
            pltpu.VMEM((256, 896), bf16),
            pltpu.VMEM((896, QL), bf16),
            pltpu.VMEM((KV, 896), bf16),
            pltpu.VMEM((QL // 128, 128), f32),
            pltpu.VMEM((LAT // 128, 128), f32),
            pltpu.VMEM((QL, HEADS * (NOPE + ROPE)), bf16),
            pltpu.VMEM((HEADS, NOPE, LAT), bf16),
            pltpu.VMEM((HEADS, LAT, VH), bf16),
            pltpu.VMEM((2, 16, 2 * ROPE), f32),
            pltpu.VMEM((2, 8, 16, 2 * ROPE), f32),
            pltpu.VMEM((128, KV), f32),
            pltpu.VMEM((128, KV), f32),
            pltpu.VMEM((128, KV), f32),
            pltpu.VMEM((128, QL), f32),
            pltpu.VMEM((128, QL), f32),
            pltpu.VMEM((128, QL), f32),
            pltpu.VMEM((6, 16, KV), bf16),
            pltpu.VMEM((6, 16, KV), bf16),
            pltpu.VMEM((6, 16, QL), f32),
            pltpu.VMEM((6, 16, QL), f32),
            pltpu.VMEM((2, 16, QL), bf16),
            pltpu.VMEM((2, 8, 16, QL), bf16),
            pltpu.VMEM((32, 128, KEYW), bf16),
            pltpu.VMEM((2, HEADS * 128, KEYW), bf16),
            pltpu.VMEM((512, 1024), f32),
            pltpu.VMEM((2, HEADS * 128, LAT), f32),
            pltpu.VMEM((2, HEADS * 128, 128), f32),
            pltpu.VMEM((2, HEADS * 128, 128), f32),
            pltpu.VMEM((2, 8, 16, HEADS * VH), bf16),
            dma((11,)),
            dma((N_SEND,)),
            dma((2,)),
            dma((6,)),
            dma((6,)),
            dma((2, 8)),
            dma((4,)),
            dma((16, 2)),
            dma((16,)),
            dma((2,)),
            dma((2,)),
            dma((2,)),
        ],
        compiler_params=pltpu.CompilerParams(
            collective_id=0, has_side_effects=True, vmem_limit_bytes=56 * 2**20
        ),
    )(
        tokens, w_down_q, w_down_kv.T, q_gain.reshape(-1, 128), kv_gain.reshape(-1, 128),
        w_up_q, w_absorb, w_value, slot_block, table,
    )
    attended = attended.reshape(256, HEADS * VH)
    return pl.pallas_call(
        hand_over,
        out_shape=(
            jax.ShapeDtypeStruct(attended.shape, bf16),
            jax.ShapeDtypeStruct(cache.shape, bf16),
        ),
        in_specs=[hbm, hbm],
        out_specs=(hbm, hbm),
        scratch_shapes=[
            pltpu.VMEM(attended.shape, bf16),
            pltpu.VMEM(cache.shape, bf16),
            dma((2, 5)),
        ],
        compiler_params=pltpu.CompilerParams(vmem_limit_bytes=60 * 2**20),
    )(attended, cache)


def solution(mesh):
    placed = (
        P("chain", "tp"),
        P("tp", None),
        P("tp", None),
        P(),
        P(),
        P(None, "tp"),
        P("tp", None, None),
        P("tp", None, None),
        P("chain"),
    )
    return jax.shard_map(
        per_device,
        mesh=mesh,
        in_specs=placed,
        out_specs=(P("chain", "tp"), P("chain", "tp", None)),
        check_vma=False,
    )
```

```python
import functools
import math

import jax
import jax.numpy as jnp
import numpy as np
from jax import lax
from jax.experimental import pallas as pl
from jax.experimental.pallas import tpu as pltpu
from jax.sharding import PartitionSpec as P

MESH = pl.DeviceIdType.MESH
ROPE_BASE = 50000.0
FLOOR_SCORE = -1e30
QL, LAT, ROPE, NOPE, VH, HEADS = 1536, 512, 64, 128, 128, 8
KEYW = 640
KV = LAT + ROPE
SCALE2 = (NOPE + ROPE) ** -0.5 * math.log2(math.e)
NT = (((1,), (1,)), ((), ()))
N_SEND = 80
RINGS = (
    (0, 0), (3, 0), (1, 0), (0, 3), (0, 1), (2, 0), (0, 2), (3, 3), (3, 1), (1, 3), (1, 1),
    (2, 3), (2, 1), (3, 2), (1, 2), (2, 2),
)


def rotary_tables():
    inverse = ROPE_BASE ** (-2.0 * np.arange(ROPE // 2) / ROPE)
    angles = np.arange(4096)[:, None] * inverse[None, :]
    cosine = np.concatenate([np.cos(angles), np.cos(angles)], 1)
    sine = np.concatenate([-np.sin(angles), np.sin(angles)], 1)
    both = np.concatenate([cosine, sine], 1).astype(np.float32)
    return both.reshape(16, 8, 2, 16, 2 * ROPE)


def rotate(values, table):
    half = ROPE // 2
    swapped = jnp.concatenate([values[:, half:], values[:, :half]], 1)
    return values * table[:, :ROPE] + swapped * table[:, ROPE:]


def normalize(values, gain):
    return values * lax.rsqrt(jnp.mean(values * values, -1, keepdims=True) + 1e-06) * gain


def kernel(
    tok_h, wq_h, wkv_h, qg_h, kvg_h, wu_h, wa_h, wv_h, slot_ref, tab_h,
    out_h, cache_ref,
    tok, wq, wkv, qg, kvg, wu, wa, wv, tabk, tabq,
    psk, pok, prk, psq, poq, prq, rks, rkr, rqs, rqr, cs, cq, kb, qb, first, acc, mx, tot, ob,
    load_sem, send_sem, sib_sem, rk_sem, rq_sem, cq_sem, ky_sem, kp_sem, ks_sem, out_sem, outs_sem, own_sem,
):
    chain = lax.axis_index("chain")
    tp = lax.axis_index("tp")
    z, x = chain // 4, chain % 4
    y, core = tp // 2, tp % 2
    other = 1 - core
    mirror = 15 - chain
    half = chain // 8
    piece = core * 4 + y
    yp, ym, yf = (y + 1) % 4, (y + 3) % 4, (y + 2) % 4
    sibling = {"chain": chain, "tp": 2 * y + other}
    up = {"chain": chain, "tp": 2 * yp + core}
    down = {"chain": chain, "tp": 2 * ym + core}
    pair = {"chain": mirror, "tp": tp}
    a = x + core * (z - x)
    b = z + core * (x - z)
    stride_a, stride_b = 1 + 3 * core, 4 - 3 * core

    def at(da, db):
        return ((a + da) % 4) * stride_a + ((b + db) % 4) * stride_b

    ap = {"chain": at(1, 0), "tp": tp}
    am = {"chain": at(3, 0), "tp": tp}
    bp = {"chain": at(0, 1), "tp": tp}
    bm = {"chain": at(0, 3), "tp": tp}

    loads = {}
    for k, (name, src, dst) in enumerate(
        [
            ("tok", tok_h, tok), ("wkv", wkv_h, wkv), ("wq", wq_h, wq), ("kvg", kvg_h, kvg),
            ("qg", qg_h, qg), ("tabk", tab_h.at[chain, piece], tabk), ("wa", wa_h, wa),
            ("wu", wu_h, wu), ("wv", wv_h, wv), ("tab0", tab_h.at[chain, :, half], tabq.at[0]),
            ("tab1", tab_h.at[mirror, :, half], tabq.at[1]),
        ]
    ):
        loads[name] = pltpu.make_async_copy(src, dst, load_sem.at[k])
        if name in ("tok", "wkv", "kvg", "tabk"):
            loads[name].start()

    def loaded(*names):
        for name in names:
            loads[name].wait()

    barrier = pltpu.get_barrier_semaphore()
    partners = (sibling, up, down, pair, ap, am, bp, bm)
    for device in partners:
        pl.semaphore_signal(barrier, inc=1, device_id=device, device_id_type=MESH)
    for name in ("wq", "qg"):
        loads[name].start()

    sent = []

    def send(src, dst, recv, device):
        copy = pltpu.make_async_remote_copy(
            src_ref=src, dst_ref=dst, send_sem=send_sem.at[len(sent)], recv_sem=recv,
            device_id=device, device_id_type=MESH,
        )
        copy.start()
        sent.append(copy)

    def arrived(dst, recv):
        pltpu.make_async_remote_copy(
            src_ref=dst, dst_ref=dst, send_sem=send_sem.at[0], recv_sem=recv,
            device_id=sibling, device_id_type=MESH,
        ).wait_recv()

    def rows_of(c):
        return tok[pl.ds(pl.multiple_of(c * 128, 128), 128), :]

    def project_keys(c, dst):
        dst[...] = lax.dot_general(rows_of(c), wkv[...], NT, preferred_element_type=jnp.float32)

    def project_queries(c, dst):
        left = rows_of(c)

        def tile(i, _):
            cols = pl.ds(pl.multiple_of(i * 512, 512), 512)
            dst[:, cols] = jnp.dot(left, wq[:, cols], preferred_element_type=jnp.float32)
            return 0

        lax.fori_loop(0, 3, tile, 0)

    def ring_of(own, got, out, came, sems):
        def part(yy, h):
            rows = pl.ds(pl.multiple_of(yy * 32 + h * 16, 16), 16)
            return own[rows, :] + got[rows, :]

        def push(k, value, device):
            out[k] = value.astype(out.dtype)
            send(out.at[k], came.at[k], sems.at[k], device)

        def start():
            push(0, part(yf, 0), up)
            push(1, part(yf, 1), down)
            push(2, part(yp, 1), up)
            push(3, part(ym, 0), down)

        def middle():
            arrived(came.at[0], sems.at[0])
            push(4, part(yp, 0) + came[0].astype(jnp.float32), up)
            arrived(came.at[1], sems.at[1])
            push(5, part(ym, 1) + came[1].astype(jnp.float32), down)

        def end():
            for k in (2, 3, 4, 5):
                arrived(came.at[k], sems.at[k])
            totals = []
            for h, first, second in ((0, 4, 3), (1, 2, 5)):
                total = part(y, h) + came[first].astype(jnp.float32)
                totals.append(total + came[second].astype(jnp.float32))
            return totals

        return start, middle, end

    keys_start, keys_middle, keys_end = ring_of(pok, prk, rks, rkr, rk_sem)
    queries_start, queries_middle, queries_end = ring_of(poq, prq, rqs, rqr, rq_sem)

    loaded("tok", "wkv")
    project_keys(other, psk)
    pl.semaphore_wait(barrier, len(partners))
    send(psk, prk, sib_sem.at[0], sibling)
    project_keys(core, pok)
    arrived(prk, sib_sem.at[0])
    keys_start()
    loaded("wq")
    for name in ("wa", "wu", "wv", "tab0", "tab1"):
        loads[name].start()
    project_queries(other, psq)
    send(psq, prq, sib_sem.at[1], sibling)
    keys_middle()
    project_queries(core, poq)
    arrived(prq, sib_sem.at[1])
    queries_start()

    slot_own = 2 * chain + core

    def keys_y(yy, h, n):
        return kb.at[slot_own, pl.ds(pl.multiple_of(yy * 32 + h * 16, 16), n)]

    loaded("kvg", "tabk")
    gain_kv = jnp.concatenate([kvg[k : k + 1, :] for k in range(LAT // 128)], 1)
    for h, total in enumerate(keys_end()):
        latent = normalize(total[:, :LAT], gain_kv)
        turned = rotate(total[:, LAT:], tabk[h])
        rows = pl.ds(pl.multiple_of(y * 32 + h * 16, 16), 16)
        kb[slot_own, rows, :LAT] = latent.astype(jnp.bfloat16)
        kb[slot_own, rows, LAT:] = jnp.concatenate(
            [turned, jnp.zeros_like(turned)], 1
        ).astype(jnp.bfloat16)
    for k, device in enumerate((up, down)):
        send(keys_y(y, 0, 32), keys_y(y, 0, 32), ky_sem.at[k], device)
    arrived(keys_y(ym, 0, 32), ky_sem.at[0])
    send(keys_y(ym, 0, 16), keys_y(ym, 0, 16), ky_sem.at[2], up)
    arrived(keys_y(yp, 0, 32), ky_sem.at[1])
    send(keys_y(yp, 1, 16), keys_y(yp, 1, 16), ky_sem.at[3], down)

    def block(n, p=None):
        if p is None:
            return kb.at[2 * n + core]
        return kb.at[2 * n + core, pl.ds(64 * p, 64)]

    def pass_on(n, *devices):
        for device in devices:
            send(block(n), block(n), kp_sem.at[n, 0], device)
        send(block(n), block(n), ks_sem.at[n], sibling)

    def pass_part(n, p, device):
        send(block(n, p), block(n, p), kp_sem.at[n, p], device)

    def whole(n):
        arrived(block(n), kp_sem.at[n, 0])

    def halves(n):
        for p in range(2):
            arrived(block(n, p), kp_sem.at[n, p])

    def relay(u, v):
        n = at(u, v)
        if v == 2 or (u, v) == (2, 0):
            halves(n)
        else:
            whole(n)
        if v == 0:
            if u != 2:
                pass_part(n, 0 if u == 3 else 1, ap if u == 3 else am)
            pass_on(n, bp, bm)
        else:
            if v != 2:
                pass_part(n, 0 if v == 3 else 1, bp if v == 3 else bm)
            pass_on(n)

    arrived(keys_y(yf, 0, 16), ky_sem.at[2])
    arrived(keys_y(yf, 1, 16), ky_sem.at[3])
    pass_on(at(0, 0), ap, am, bp, bm)
    acc[...] = jnp.zeros_like(acc)
    tot[...] = jnp.zeros_like(tot)
    mx[...] = jnp.full_like(mx, FLOOR_SCORE)
    queries_middle()

    loaded("qg")
    gain_q = jnp.concatenate([qg[k : k + 1, :] for k in range(QL // 128)], 1)
    for h, total in enumerate(queries_end()):
        cs[h] = normalize(total, gain_q).astype(jnp.bfloat16)

    def give(s, p, *devices):
        for device in devices:
            send(cq.at[s, p], cq.at[s, p], cq_sem.at[s, p], device)

    def take(s, p):
        arrived(cq.at[s, p], cq_sem.at[s, p])

    send(cs.at[1 - half], cq.at[1, piece], cq_sem.at[1, piece], pair)
    cq[0, piece] = cs[half]
    give(0, piece, up, down, sibling)
    pm, pp, pf = core * 4 + ym, core * 4 + yp, core * 4 + yf
    for u, v in RINGS[1:7]:
        relay(u, v)
    take(1, piece)
    give(1, piece, up, down, sibling)
    take(0, pm)
    give(0, pm, up, sibling)
    take(0, pp)
    give(0, pp, sibling)
    for u, v in RINGS[7:11]:
        relay(u, v)
    take(1, pp)
    give(1, pp, down, sibling)
    take(1, pm)
    give(1, pm, sibling)
    take(0, pf)
    give(0, pf, sibling)
    for u, v in RINGS[11:15]:
        relay(u, v)
    take(1, pf)
    give(1, pf, sibling)
    for s in range(2):
        for yy in range(4):
            take(s, other * 4 + yy)

    loaded("wa", "wu", "tab0", "tab1")

    def expand(i, _):
        cols = pl.ds(pl.multiple_of(i * 384, 384), 384)
        rows = cq[...].reshape(256, QL)
        projected = jnp.dot(rows, wu[:, cols], preferred_element_type=jnp.float32)
        table = tabq[...].reshape(256, 2 * ROPE)
        for j in range(2):
            head = 2 * i + j
            base = j * (NOPE + ROPE)
            nope = projected[:, base : base + NOPE].astype(jnp.bfloat16)
            turned = rotate(projected[:, base + NOPE : base + NOPE + ROPE], table)
            turned = jnp.concatenate([turned, jnp.zeros_like(turned)], 1).astype(jnp.bfloat16)
            absorbed = jnp.dot(nope, wa[head], preferred_element_type=jnp.float32)
            absorbed = absorbed.astype(jnp.bfloat16)
            places = pl.ds(pl.multiple_of(head * 128, 128), 128)
            for s in range(2):
                qb[s, places, :LAT] = absorbed[s * 128 : s * 128 + 128]
                qb[s, places, LAT:] = turned[s * 128 : s * 128 + 128]
        return 0

    lax.fori_loop(0, HEADS // 2, expand, 0)
    relay(2, 2)

    def meet(c):
        for k in range(4):
            n = 4 * c + k
            arrived(kb.at[2 * n + other], ks_sem.at[n])

    meet(0)

    token = lax.broadcasted_iota(jnp.int32, (512, 1), 0) & 127
    place = ((token >> 4) << 5) + (token & 15) + half * 16
    key_iota = lax.broadcasted_iota(jnp.int32, (1, 1024), 1)

    def score(s, c, r):
        keys = kb[pl.ds(8 * c, 8)].reshape(1024, KEYW)
        queries = qb[s, pl.ds(pl.multiple_of(r * 512, 512), 512), :]
        return lax.dot_general(queries, keys, NT, preferred_element_type=jnp.float32)

    def tile(s, r, c, blk, size, last, following):
        rows = pl.ds(pl.multiple_of(r * 512, 512), 512)
        scores = first[:, :size] * SCALE2
        if following is not None:
            first[...] = score(*following)
        if last:
            visible = key_iota[:, :size] + 1024 * c <= place + 256 * blk
            scores = jnp.where(visible, scores, FLOOR_SCORE)
        parts = [scores[:, k : k + 128] for k in range(0, size, 128)]
        before = mx[s, rows, :]
        top = jnp.max(functools.reduce(jnp.maximum, parts), 1, keepdims=True)
        peak = jnp.maximum(before, top)
        shrink = jnp.exp2(before - peak)
        weights = [jnp.exp2(p - peak) for p in parts]
        mx[s, rows, :] = peak
        tot[s, rows, :] = tot[s, rows, :] * shrink + sum(weights[1:], weights[0])
        weights = jnp.concatenate([w.astype(jnp.bfloat16) for w in weights], 1)
        latent = kb[pl.ds(8 * c, size // 128), :, :LAT].reshape(size, LAT)
        mixed = jnp.dot(weights, latent, preferred_element_type=jnp.float32)
        shrink = jnp.concatenate([shrink] * (LAT // 128), 1)
        acc[s, rows, :] = acc[s, rows, :] * shrink + mixed

    def attend(s, r, blk, met, after):
        def step(c, _):
            @pl.when(c + 1 > met)
            def _():
                meet(c + 1)

            tile(s, r, c, blk, 1024, False, (s, c + 1, r))
            return 0

        lax.fori_loop(0, blk // 4, step, 0)
        for k in range(4):
            @pl.when(blk % 4 == k)
            def _():
                tile(s, r, blk // 4, blk, 256 * k + 256, True, after)

        finish(s, r)

    def out_cols(r):
        return pl.ds(pl.multiple_of(r * 512, 512), 512)

    def out_copy(r):
        return pltpu.make_async_remote_copy(
            src_ref=ob.at[1, :, :, out_cols(r)], dst_ref=out_h.at[:, half, :, out_cols(r)],
            send_sem=outs_sem.at[r], recv_sem=out_sem.at[r], device_id=pair, device_id_type=MESH,
        )

    def own_copy(r):
        return pltpu.make_async_copy(
            ob.at[0, :, :, out_cols(r)], out_h.at[:, half, :, out_cols(r)], own_sem.at[r]
        )

    def finish(s, r):
        for k in range(4):
            part = pl.ds(pl.multiple_of(r * 512 + k * 128, 128), 128)
            total = jnp.sum(tot[s, part, :], 1, keepdims=True)
            mixed = (acc[s, part, :] * (1.0 / total)).astype(jnp.bfloat16)
            value = jnp.dot(mixed, wv[4 * r + k], preferred_element_type=jnp.float32)
            ob[s, :, :, part] = value.astype(jnp.bfloat16).reshape(8, 16, VH)
        (own_copy, out_copy)[s](r).start()

    loaded("wv")
    first[...] = score(1, 0, 0)

    def far_pass(r, _):
        attend(1, r, mirror, r * (3 - z), (1 - r, 0, 1 - r))
        return 0

    lax.fori_loop(0, 2, far_pass, 0)
    attend(0, 0, chain, 3 - z, (0, 0, 1))
    attend(0, 1, chain, 3, None)

    def rest(c, _):
        meet(c)
        return 0

    lax.fori_loop(jnp.maximum(3 - z, z) + 1, 4, rest, 0)
    for j in range(2):
        rows = pl.ds(pl.multiple_of(tp * 16, 16), 16)
        cache_ref[j] = kb[slot_ref[j], rows, :][:, :KV]
    for r in range(2):
        own_copy(r).wait()
        out_copy(r).wait_send()
        arrived(out_h.at[:, 1 - half, :, out_cols(r)], out_sem.at[r])
    for copy in sent:
        copy.wait_send()


def hand_over(att_h, cache_h, att_out, cache_out, att, cache, sem):
    pieces = [(cache_h, cache, cache_out)]
    for k in range(4):
        rows = pl.ds(64 * k, 64)
        pieces.append((att_h.at[rows], att.at[rows], att_out.at[rows]))
    into = [pltpu.make_async_copy(p[0], p[1], sem.at[0, k]) for k, p in enumerate(pieces)]
    out = [pltpu.make_async_copy(p[1], p[2], sem.at[1, k]) for k, p in enumerate(pieces)]
    for copy in into:
        copy.start()
    for first, second in zip(into, out):
        first.wait()
        second.start()
    for copy in out:
        copy.wait()


def per_device(tokens, w_down_q, w_down_kv, q_gain, kv_gain, w_up_q, w_absorb, w_value, slot_block):
    bf16, f32 = jnp.bfloat16, jnp.float32
    table = jnp.asarray(rotary_tables())
    hbm = pl.BlockSpec(memory_space=pl.ANY)
    dma = pltpu.SemaphoreType.DMA
    attended, cache = pl.pallas_call(
        kernel,
        out_shape=(
            jax.ShapeDtypeStruct((8, 2, 16, HEADS * VH), bf16),
            jax.ShapeDtypeStruct((2, 16, KV), bf16),
        ),
        in_specs=[hbm] * 8 + [pl.BlockSpec(memory_space=pltpu.SMEM), hbm],
        out_specs=(hbm, pl.BlockSpec(memory_space=pltpu.VMEM)),
        scratch_shapes=[
            pltpu.VMEM((256, 896), bf16),
            pltpu.VMEM((896, QL), bf16),
            pltpu.VMEM((KV, 896), bf16),
            pltpu.VMEM((QL // 128, 128), f32),
            pltpu.VMEM((LAT // 128, 128), f32),
            pltpu.VMEM((QL, HEADS * (NOPE + ROPE)), bf16),
            pltpu.VMEM((HEADS, NOPE, LAT), bf16),
            pltpu.VMEM((HEADS, LAT, VH), bf16),
            pltpu.VMEM((2, 16, 2 * ROPE), f32),
            pltpu.VMEM((2, 8, 16, 2 * ROPE), f32),
            pltpu.VMEM((128, KV), f32),
            pltpu.VMEM((128, KV), f32),
            pltpu.VMEM((128, KV), f32),
            pltpu.VMEM((128, QL), f32),
            pltpu.VMEM((128, QL), f32),
            pltpu.VMEM((128, QL), f32),
            pltpu.VMEM((6, 16, KV), bf16),
            pltpu.VMEM((6, 16, KV), bf16),
            pltpu.VMEM((6, 16, QL), f32),
            pltpu.VMEM((6, 16, QL), f32),
            pltpu.VMEM((2, 16, QL), bf16),
            pltpu.VMEM((2, 8, 16, QL), bf16),
            pltpu.VMEM((32, 128, KEYW), bf16),
            pltpu.VMEM((2, HEADS * 128, KEYW), bf16),
            pltpu.VMEM((512, 1024), f32),
            pltpu.VMEM((2, HEADS * 128, LAT), f32),
            pltpu.VMEM((2, HEADS * 128, 128), f32),
            pltpu.VMEM((2, HEADS * 128, 128), f32),
            pltpu.VMEM((2, 8, 16, HEADS * VH), bf16),
            dma((11,)),
            dma((N_SEND,)),
            dma((2,)),
            dma((6,)),
            dma((6,)),
            dma((2, 8)),
            dma((4,)),
            dma((16, 2)),
            dma((16,)),
            dma((2,)),
            dma((2,)),
            dma((2,)),
        ],
        compiler_params=pltpu.CompilerParams(
            collective_id=0, has_side_effects=True, vmem_limit_bytes=56 * 2**20
        ),
    )(
        tokens, w_down_q, w_down_kv.T, q_gain.reshape(-1, 128), kv_gain.reshape(-1, 128),
        w_up_q, w_absorb, w_value, slot_block, table,
    )
    attended = attended.reshape(256, HEADS * VH)
    return pl.pallas_call(
        hand_over,
        out_shape=(
            jax.ShapeDtypeStruct(attended.shape, bf16),
            jax.ShapeDtypeStruct(cache.shape, bf16),
        ),
        in_specs=[hbm, hbm],
        out_specs=(hbm, hbm),
        scratch_shapes=[
            pltpu.VMEM(attended.shape, bf16),
            pltpu.VMEM(cache.shape, bf16),
            dma((2, 5)),
        ],
        compiler_params=pltpu.CompilerParams(vmem_limit_bytes=60 * 2**20),
    )(attended, cache)


def solution(mesh):
    placed = (
        P("chain", "tp"),
        P("tp", None),
        P("tp", None),
        P(),
        P(),
        P(None, "tp"),
        P("tp", None, None),
        P("tp", None, None),
        P("chain"),
    )
    return jax.shard_map(
        per_device,
        mesh=mesh,
        in_specs=placed,
        out_specs=(P("chain", "tp"), P("chain", "tp", None)),
        check_vma=False,
    )
```

```python
import functools
import math

import jax
import jax.numpy as jnp
import numpy as np
from jax import lax
from jax.experimental import pallas as pl
from jax.experimental.pallas import tpu as pltpu
from jax.sharding import PartitionSpec as P

MESH = pl.DeviceIdType.MESH
ROPE_BASE = 50000.0
FLOOR_SCORE = -1e30
QL, LAT, ROPE, NOPE, VH, HEADS = 1536, 512, 64, 128, 128, 8
KEYW = 640
KV = LAT + ROPE
SCALE2 = (NOPE + ROPE) ** -0.5 * math.log2(math.e)
NT = (((1,), (1,)), ((), ()))
N_SEND = 80
RINGS = (
    (0, 0), (3, 0), (1, 0), (0, 3), (0, 1), (2, 0), (0, 2), (3, 3), (3, 1), (1, 3), (1, 1),
    (2, 3), (2, 1), (3, 2), (1, 2), (2, 2),
)


def rotary_tables():
    inverse = ROPE_BASE ** (-2.0 * np.arange(ROPE // 2) / ROPE)
    angles = np.arange(4096)[:, None] * inverse[None, :]
    cosine = np.concatenate([np.cos(angles), np.cos(angles)], 1)
    sine = np.concatenate([-np.sin(angles), np.sin(angles)], 1)
    both = np.concatenate([cosine, sine], 1).astype(np.float32)
    return both.reshape(16, 8, 2, 16, 2 * ROPE)


def rotate(values, table):
    half = ROPE // 2
    swapped = jnp.concatenate([values[:, half:], values[:, :half]], 1)
    return values * table[:, :ROPE] + swapped * table[:, ROPE:]


def normalize(values, gain):
    return values * lax.rsqrt(jnp.mean(values * values, -1, keepdims=True) + 1e-06) * gain


def kernel(
    tok_h, wq_h, wkv_h, qg_h, kvg_h, wu_h, wa_h, wv_h, slot_ref, tab_h,
    out_h, cache_ref,
    tok, wq, wkv, qg, kvg, wu, wa, wv, tabk, tabq,
    psk, pok, prk, psq, poq, prq, rks, rkr, rqs, rqr, cs, cq, kb, qb, first, acc, mx, tot, ob,
    load_sem, send_sem, sib_sem, rk_sem, rq_sem, cq_sem, ky_sem, kp_sem, ks_sem, out_sem, outs_sem, own_sem,
):
    chain = lax.axis_index("chain")
    tp = lax.axis_index("tp")
    z, x = chain // 4, chain % 4
    y, core = tp // 2, tp % 2
    other = 1 - core
    mirror = 15 - chain
    half = chain // 8
    piece = core * 4 + y
    yp, ym, yf = (y + 1) % 4, (y + 3) % 4, (y + 2) % 4
    sibling = {"chain": chain, "tp": 2 * y + other}
    up = {"chain": chain, "tp": 2 * yp + core}
    down = {"chain": chain, "tp": 2 * ym + core}
    pair = {"chain": mirror, "tp": tp}
    a = x + core * (z - x)
    b = z + core * (x - z)
    stride_a, stride_b = 1 + 3 * core, 4 - 3 * core

    def at(da, db):
        return ((a + da) % 4) * stride_a + ((b + db) % 4) * stride_b

    ap = {"chain": at(1, 0), "tp": tp}
    am = {"chain": at(3, 0), "tp": tp}
    bp = {"chain": at(0, 1), "tp": tp}
    bm = {"chain": at(0, 3), "tp": tp}

    loads = {}
    for k, (name, src, dst) in enumerate(
        [
            ("tok", tok_h, tok), ("wkv", wkv_h, wkv), ("wq", wq_h, wq), ("kvg", kvg_h, kvg),
            ("qg", qg_h, qg), ("tabk", tab_h.at[chain, piece], tabk), ("wa", wa_h, wa),
            ("wu", wu_h, wu), ("wv", wv_h, wv), ("tab0", tab_h.at[chain, :, half], tabq.at[0]),
            ("tab1", tab_h.at[mirror, :, half], tabq.at[1]),
        ]
    ):
        loads[name] = pltpu.make_async_copy(src, dst, load_sem.at[k])
        if name in ("tok", "wkv", "kvg", "tabk"):
            loads[name].start()

    def loaded(*names):
        for name in names:
            loads[name].wait()

    barrier = pltpu.get_barrier_semaphore()
    partners = (sibling, up, down, pair, ap, am, bp, bm)
    for device in partners:
        pl.semaphore_signal(barrier, inc=1, device_id=device, device_id_type=MESH)
    for name in ("wq", "qg"):
        loads[name].start()

    sent = []

    def send(src, dst, recv, device):
        copy = pltpu.make_async_remote_copy(
            src_ref=src, dst_ref=dst, send_sem=send_sem.at[len(sent)], recv_sem=recv,
            device_id=device, device_id_type=MESH,
        )
        copy.start()
        sent.append(copy)

    def arrived(dst, recv):
        pltpu.make_async_remote_copy(
            src_ref=dst, dst_ref=dst, send_sem=send_sem.at[0], recv_sem=recv,
            device_id=sibling, device_id_type=MESH,
        ).wait_recv()

    def rows_of(c):
        return tok[pl.ds(pl.multiple_of(c * 128, 128), 128), :]

    def project_keys(c, dst):
        dst[...] = lax.dot_general(rows_of(c), wkv[...], NT, preferred_element_type=jnp.float32)

    def project_queries(c, dst):
        left = rows_of(c)

        def tile(i, _):
            cols = pl.ds(pl.multiple_of(i * 512, 512), 512)
            dst[:, cols] = jnp.dot(left, wq[:, cols], preferred_element_type=jnp.float32)
            return 0

        lax.fori_loop(0, 3, tile, 0)

    def ring_of(own, got, out, came, sems):
        def part(yy, h):
            rows = pl.ds(pl.multiple_of(yy * 32 + h * 16, 16), 16)
            return own[rows, :] + got[rows, :]

        def push(k, value, device):
            out[k] = value.astype(out.dtype)
            send(out.at[k], came.at[k], sems.at[k], device)

        def start():
            push(0, part(yf, 0), up)
            push(1, part(yf, 1), down)
            push(2, part(yp, 1), up)
            push(3, part(ym, 0), down)

        def middle():
            arrived(came.at[0], sems.at[0])
            push(4, part(yp, 0) + came[0].astype(jnp.float32), up)
            arrived(came.at[1], sems.at[1])
            push(5, part(ym, 1) + came[1].astype(jnp.float32), down)

        def end():
            for k in (2, 3, 4, 5):
                arrived(came.at[k], sems.at[k])
            totals = []
            for h, first, second in ((0, 4, 3), (1, 2, 5)):
                total = part(y, h) + came[first].astype(jnp.float32)
                totals.append(total + came[second].astype(jnp.float32))
            return totals

        return start, middle, end

    keys_start, keys_middle, keys_end = ring_of(pok, prk, rks, rkr, rk_sem)
    queries_start, queries_middle, queries_end = ring_of(poq, prq, rqs, rqr, rq_sem)

    loaded("tok", "wkv")
    project_keys(other, psk)
    pl.semaphore_wait(barrier, len(partners))
    send(psk, prk, sib_sem.at[0], sibling)
    project_keys(core, pok)
    arrived(prk, sib_sem.at[0])
    keys_start()
    loaded("wq")
    for name in ("wa", "wu", "wv", "tab0", "tab1"):
        loads[name].start()
    project_queries(other, psq)
    send(psq, prq, sib_sem.at[1], sibling)
    keys_middle()
    project_queries(core, poq)
    arrived(prq, sib_sem.at[1])
    queries_start()

    slot_own = 2 * chain + core

    def keys_y(yy, h, n):
        return kb.at[slot_own, pl.ds(pl.multiple_of(yy * 32 + h * 16, 16), n)]

    loaded("kvg", "tabk")
    gain_kv = jnp.concatenate([kvg[k : k + 1, :] for k in range(LAT // 128)], 1)
    for h, total in enumerate(keys_end()):
        latent = normalize(total[:, :LAT], gain_kv)
        turned = rotate(total[:, LAT:], tabk[h])
        rows = pl.ds(pl.multiple_of(y * 32 + h * 16, 16), 16)
        kb[slot_own, rows, :LAT] = latent.astype(jnp.bfloat16)
        kb[slot_own, rows, LAT:] = jnp.concatenate(
            [turned, jnp.zeros_like(turned)], 1
        ).astype(jnp.bfloat16)
    for k, device in enumerate((up, down)):
        send(keys_y(y, 0, 32), keys_y(y, 0, 32), ky_sem.at[k], device)
    arrived(keys_y(ym, 0, 32), ky_sem.at[0])
    send(keys_y(ym, 0, 16), keys_y(ym, 0, 16), ky_sem.at[2], up)
    arrived(keys_y(yp, 0, 32), ky_sem.at[1])
    send(keys_y(yp, 1, 16), keys_y(yp, 1, 16), ky_sem.at[3], down)

    def block(n, p=None):
        if p is None:
            return kb.at[2 * n + core]
        return kb.at[2 * n + core, pl.ds(64 * p, 64)]

    def pass_on(n, *devices):
        for device in devices:
            send(block(n), block(n), kp_sem.at[n, 0], device)
        send(block(n), block(n), ks_sem.at[n], sibling)

    def pass_part(n, p, device):
        send(block(n, p), block(n, p), kp_sem.at[n, p], device)

    def whole(n):
        arrived(block(n), kp_sem.at[n, 0])

    def halves(n):
        for p in range(2):
            arrived(block(n, p), kp_sem.at[n, p])

    def relay(u, v):
        n = at(u, v)
        if v == 2 or (u, v) == (2, 0):
            halves(n)
        else:
            whole(n)
        if v == 0:
            if u != 2:
                pass_part(n, 0 if u == 3 else 1, ap if u == 3 else am)
            pass_on(n, bp, bm)
        else:
            if v != 2:
                pass_part(n, 0 if v == 3 else 1, bp if v == 3 else bm)
            pass_on(n)

    arrived(keys_y(yf, 0, 16), ky_sem.at[2])
    arrived(keys_y(yf, 1, 16), ky_sem.at[3])
    pass_on(at(0, 0), ap, am, bp, bm)
    acc[...] = jnp.zeros_like(acc)
    tot[...] = jnp.zeros_like(tot)
    mx[...] = jnp.full_like(mx, FLOOR_SCORE)
    queries_middle()

    loaded("qg")
    gain_q = jnp.concatenate([qg[k : k + 1, :] for k in range(QL // 128)], 1)
    for h, total in enumerate(queries_end()):
        cs[h] = normalize(total, gain_q).astype(jnp.bfloat16)

    def give(s, p, *devices):
        for device in devices:
            send(cq.at[s, p], cq.at[s, p], cq_sem.at[s, p], device)

    def take(s, p):
        arrived(cq.at[s, p], cq_sem.at[s, p])

    send(cs.at[1 - half], cq.at[1, piece], cq_sem.at[1, piece], pair)
    cq[0, piece] = cs[half]
    give(0, piece, up, down, sibling)
    pm, pp, pf = core * 4 + ym, core * 4 + yp, core * 4 + yf
    for u, v in RINGS[1:7]:
        relay(u, v)
    take(1, piece)
    give(1, piece, up, down, sibling)
    take(0, pm)
    give(0, pm, up, sibling)
    take(0, pp)
    give(0, pp, sibling)
    for u, v in RINGS[7:11]:
        relay(u, v)
    take(1, pp)
    give(1, pp, down, sibling)
    take(1, pm)
    give(1, pm, sibling)
    take(0, pf)
    give(0, pf, sibling)
    take(1, pf)
    give(1, pf, sibling)
    for s in range(2):
        for yy in range(4):
            take(s, other * 4 + yy)

    loaded("wa", "wu", "tab0", "tab1")

    def expand(i, _):
        cols = pl.ds(pl.multiple_of(i * 384, 384), 384)
        rows = cq[...].reshape(256, QL)
        projected = jnp.dot(rows, wu[:, cols], preferred_element_type=jnp.float32)
        table = tabq[...].reshape(256, 2 * ROPE)
        for j in range(2):
            head = 2 * i + j
            base = j * (NOPE + ROPE)
            nope = projected[:, base : base + NOPE].astype(jnp.bfloat16)
            turned = rotate(projected[:, base + NOPE : base + NOPE + ROPE], table)
            turned = jnp.concatenate([turned, jnp.zeros_like(turned)], 1).astype(jnp.bfloat16)
            absorbed = jnp.dot(nope, wa[head], preferred_element_type=jnp.float32)
            absorbed = absorbed.astype(jnp.bfloat16)
            places = pl.ds(pl.multiple_of(head * 128, 128), 128)
            for s in range(2):
                qb[s, places, :LAT] = absorbed[s * 128 : s * 128 + 128]
                qb[s, places, LAT:] = turned[s * 128 : s * 128 + 128]
        return 0

    lax.fori_loop(0, HEADS // 4, expand, 0)
    for u, v in RINGS[11:15]:
        relay(u, v)
    lax.fori_loop(HEADS // 4, HEADS // 2, expand, 0)
    relay(2, 2)

    def meet(c):
        for k in range(4):
            n = 4 * c + k
            arrived(kb.at[2 * n + other], ks_sem.at[n])

    meet(0)

    token = lax.broadcasted_iota(jnp.int32, (512, 1), 0) & 127
    place = ((token >> 4) << 5) + (token & 15) + half * 16
    key_iota = lax.broadcasted_iota(jnp.int32, (1, 1024), 1)

    def score(s, c, r):
        keys = kb[pl.ds(8 * c, 8)].reshape(1024, KEYW)
        queries = qb[s, pl.ds(pl.multiple_of(r * 512, 512), 512), :]
        return lax.dot_general(queries, keys, NT, preferred_element_type=jnp.float32)

    def tile(s, r, c, blk, size, last, following):
        rows = pl.ds(pl.multiple_of(r * 512, 512), 512)
        scores = first[:, :size] * SCALE2
        if following is not None:
            first[...] = score(*following)
        if last:
            visible = key_iota[:, :size] + 1024 * c <= place + 256 * blk
            scores = jnp.where(visible, scores, FLOOR_SCORE)
        parts = [scores[:, k : k + 128] for k in range(0, size, 128)]
        before = mx[s, rows, :]
        top = jnp.max(functools.reduce(jnp.maximum, parts), 1, keepdims=True)
        peak = jnp.maximum(before, top)
        shrink = jnp.exp2(before - peak)
        weights = [jnp.exp2(p - peak) for p in parts]
        mx[s, rows, :] = peak
        tot[s, rows, :] = tot[s, rows, :] * shrink + sum(weights[1:], weights[0])
        weights = jnp.concatenate([w.astype(jnp.bfloat16) for w in weights], 1)
        latent = kb[pl.ds(8 * c, size // 128), :, :LAT].reshape(size, LAT)
        mixed = jnp.dot(weights, latent, preferred_element_type=jnp.float32)
        shrink = jnp.concatenate([shrink] * (LAT // 128), 1)
        acc[s, rows, :] = acc[s, rows, :] * shrink + mixed

    def attend(s, r, blk, met, after):
        def step(c, _):
            @pl.when(c + 1 > met)
            def _():
                meet(c + 1)

            tile(s, r, c, blk, 1024, False, (s, c + 1, r))
            return 0

        lax.fori_loop(0, blk // 4, step, 0)
        for k in range(4):
            @pl.when(blk % 4 == k)
            def _():
                tile(s, r, blk // 4, blk, 256 * k + 256, True, after)

        finish(s, r)

    def out_cols(r):
        return pl.ds(pl.multiple_of(r * 512, 512), 512)

    def out_copy(r):
        return pltpu.make_async_remote_copy(
            src_ref=ob.at[1, :, :, out_cols(r)], dst_ref=out_h.at[:, half, :, out_cols(r)],
            send_sem=outs_sem.at[r], recv_sem=out_sem.at[r], device_id=pair, device_id_type=MESH,
        )

    def own_copy(r):
        return pltpu.make_async_copy(
            ob.at[0, :, :, out_cols(r)], out_h.at[:, half, :, out_cols(r)], own_sem.at[r]
        )

    def finish(s, r):
        for k in range(4):
            part = pl.ds(pl.multiple_of(r * 512 + k * 128, 128), 128)
            total = jnp.sum(tot[s, part, :], 1, keepdims=True)
            mixed = (acc[s, part, :] * (1.0 / total)).astype(jnp.bfloat16)
            value = jnp.dot(mixed, wv[4 * r + k], preferred_element_type=jnp.float32)
            ob[s, :, :, part] = value.astype(jnp.bfloat16).reshape(8, 16, VH)
        (own_copy, out_copy)[s](r).start()

    loaded("wv")
    first[...] = score(1, 0, 0)

    def far_pass(r, _):
        attend(1, r, mirror, r * (3 - z), (1 - r, 0, 1 - r))
        return 0

    lax.fori_loop(0, 2, far_pass, 0)
    attend(0, 0, chain, 3 - z, (0, 0, 1))
    attend(0, 1, chain, 3, None)

    def rest(c, _):
        meet(c)
        return 0

    lax.fori_loop(jnp.maximum(3 - z, z) + 1, 4, rest, 0)
    for j in range(2):
        rows = pl.ds(pl.multiple_of(tp * 16, 16), 16)
        cache_ref[j] = kb[slot_ref[j], rows, :][:, :KV]
    for r in range(2):
        own_copy(r).wait()
        out_copy(r).wait_send()
        arrived(out_h.at[:, 1 - half, :, out_cols(r)], out_sem.at[r])
    for copy in sent:
        copy.wait_send()


def hand_over(att_h, cache_h, att_out, cache_out, att, cache, sem):
    pieces = [(cache_h, cache, cache_out)]
    for k in range(4):
        rows = pl.ds(64 * k, 64)
        pieces.append((att_h.at[rows], att.at[rows], att_out.at[rows]))
    into = [pltpu.make_async_copy(p[0], p[1], sem.at[0, k]) for k, p in enumerate(pieces)]
    out = [pltpu.make_async_copy(p[1], p[2], sem.at[1, k]) for k, p in enumerate(pieces)]
    for copy in into:
        copy.start()
    for first, second in zip(into, out):
        first.wait()
        second.start()
    for copy in out:
        copy.wait()


def per_device(tokens, w_down_q, w_down_kv, q_gain, kv_gain, w_up_q, w_absorb, w_value, slot_block):
    bf16, f32 = jnp.bfloat16, jnp.float32
    table = jnp.asarray(rotary_tables())
    hbm = pl.BlockSpec(memory_space=pl.ANY)
    dma = pltpu.SemaphoreType.DMA
    attended, cache = pl.pallas_call(
        kernel,
        out_shape=(
            jax.ShapeDtypeStruct((8, 2, 16, HEADS * VH), bf16),
            jax.ShapeDtypeStruct((2, 16, KV), bf16),
        ),
        in_specs=[hbm] * 8 + [pl.BlockSpec(memory_space=pltpu.SMEM), hbm],
        out_specs=(hbm, pl.BlockSpec(memory_space=pltpu.VMEM)),
        scratch_shapes=[
            pltpu.VMEM((256, 896), bf16),
            pltpu.VMEM((896, QL), bf16),
            pltpu.VMEM((KV, 896), bf16),
            pltpu.VMEM((QL // 128, 128), f32),
            pltpu.VMEM((LAT // 128, 128), f32),
            pltpu.VMEM((QL, HEADS * (NOPE + ROPE)), bf16),
            pltpu.VMEM((HEADS, NOPE, LAT), bf16),
            pltpu.VMEM((HEADS, LAT, VH), bf16),
            pltpu.VMEM((2, 16, 2 * ROPE), f32),
            pltpu.VMEM((2, 8, 16, 2 * ROPE), f32),
            pltpu.VMEM((128, KV), f32),
            pltpu.VMEM((128, KV), f32),
            pltpu.VMEM((128, KV), f32),
            pltpu.VMEM((128, QL), f32),
            pltpu.VMEM((128, QL), f32),
            pltpu.VMEM((128, QL), f32),
            pltpu.VMEM((6, 16, KV), bf16),
            pltpu.VMEM((6, 16, KV), bf16),
            pltpu.VMEM((6, 16, QL), f32),
            pltpu.VMEM((6, 16, QL), f32),
            pltpu.VMEM((2, 16, QL), bf16),
            pltpu.VMEM((2, 8, 16, QL), bf16),
            pltpu.VMEM((32, 128, KEYW), bf16),
            pltpu.VMEM((2, HEADS * 128, KEYW), bf16),
            pltpu.VMEM((512, 1024), f32),
            pltpu.VMEM((2, HEADS * 128, LAT), f32),
            pltpu.VMEM((2, HEADS * 128, 128), f32),
            pltpu.VMEM((2, HEADS * 128, 128), f32),
            pltpu.VMEM((2, 8, 16, HEADS * VH), bf16),
            dma((11,)),
            dma((N_SEND,)),
            dma((2,)),
            dma((6,)),
            dma((6,)),
            dma((2, 8)),
            dma((4,)),
            dma((16, 2)),
            dma((16,)),
            dma((2,)),
            dma((2,)),
            dma((2,)),
        ],
        compiler_params=pltpu.CompilerParams(
            collective_id=0, has_side_effects=True, vmem_limit_bytes=56 * 2**20
        ),
    )(
        tokens, w_down_q, w_down_kv.T, q_gain.reshape(-1, 128), kv_gain.reshape(-1, 128),
        w_up_q, w_absorb, w_value, slot_block, table,
    )
    attended = attended.reshape(256, HEADS * VH)
    return pl.pallas_call(
        hand_over,
        out_shape=(
            jax.ShapeDtypeStruct(attended.shape, bf16),
            jax.ShapeDtypeStruct(cache.shape, bf16),
        ),
        in_specs=[hbm, hbm],
        out_specs=(hbm, hbm),
        scratch_shapes=[
            pltpu.VMEM(attended.shape, bf16),
            pltpu.VMEM(cache.shape, bf16),
            dma((2, 5)),
        ],
        compiler_params=pltpu.CompilerParams(vmem_limit_bytes=60 * 2**20),
    )(attended, cache)


def solution(mesh):
    placed = (
        P("chain", "tp"),
        P("tp", None),
        P("tp", None),
        P(),
        P(),
        P(None, "tp"),
        P("tp", None, None),
        P("tp", None, None),
        P("chain"),
    )
    return jax.shard_map(
        per_device,
        mesh=mesh,
        in_specs=placed,
        out_specs=(P("chain", "tp"), P("chain", "tp", None)),
        check_vma=False,
    )
```

```python
import functools
import math

import jax
import jax.numpy as jnp
import numpy as np
from jax import lax
from jax.experimental import pallas as pl
from jax.experimental.pallas import tpu as pltpu
from jax.sharding import PartitionSpec as P

MESH = pl.DeviceIdType.MESH
ROPE_BASE = 50000.0
FLOOR_SCORE = -1e30
QL, LAT, ROPE, NOPE, VH, HEADS = 1536, 512, 64, 128, 128, 8
KEYW = 640
KV = LAT + ROPE
SCALE2 = (NOPE + ROPE) ** -0.5 * math.log2(math.e)
NT = (((1,), (1,)), ((), ()))
N_SEND = 80
RINGS = (
    (0, 0), (3, 0), (1, 0), (0, 3), (0, 1), (2, 0), (0, 2), (3, 3), (3, 1), (1, 3), (1, 1),
    (2, 3), (2, 1), (3, 2), (1, 2), (2, 2),
)


def rotary_tables():
    inverse = ROPE_BASE ** (-2.0 * np.arange(ROPE // 2) / ROPE)
    angles = np.arange(4096)[:, None] * inverse[None, :]
    cosine = np.concatenate([np.cos(angles), np.cos(angles)], 1)
    sine = np.concatenate([-np.sin(angles), np.sin(angles)], 1)
    both = np.concatenate([cosine, sine], 1).astype(np.float32)
    return both.reshape(16, 8, 2, 16, 2 * ROPE)


def rotate(values, table):
    half = ROPE // 2
    swapped = jnp.concatenate([values[:, half:], values[:, :half]], 1)
    return values * table[:, :ROPE] + swapped * table[:, ROPE:]


def normalize(values, gain):
    return values * lax.rsqrt(jnp.mean(values * values, -1, keepdims=True) + 1e-06) * gain


def kernel(
    tok_h, wq_h, wkv_h, qg_h, kvg_h, wu_h, wa_h, wv_h, slot_ref, tab_h,
    out_h, cache_ref,
    tok, wq, wkv, qg, kvg, wu, wa, wv, tabk, tabq,
    psk, pok, prk, psq, poq, prq, rks, rkr, rqs, rqr, cs, cq, kb, qb, first, acc, mx, tot, ob,
    load_sem, send_sem, sib_sem, rk_sem, rq_sem, cq_sem, ky_sem, kp_sem, ks_sem, out_sem, outs_sem, own_sem,
):
    chain = lax.axis_index("chain")
    tp = lax.axis_index("tp")
    z, x = chain // 4, chain % 4
    y, core = tp // 2, tp % 2
    other = 1 - core
    mirror = 15 - chain
    half = chain // 8
    piece = core * 4 + y
    yp, ym, yf = (y + 1) % 4, (y + 3) % 4, (y + 2) % 4
    sibling = {"chain": chain, "tp": 2 * y + other}
    up = {"chain": chain, "tp": 2 * yp + core}
    down = {"chain": chain, "tp": 2 * ym + core}
    pair = {"chain": mirror, "tp": tp}
    a = x + core * (z - x)
    b = z + core * (x - z)
    stride_a, stride_b = 1 + 3 * core, 4 - 3 * core

    def at(da, db):
        return ((a + da) % 4) * stride_a + ((b + db) % 4) * stride_b

    ap = {"chain": at(1, 0), "tp": tp}
    am = {"chain": at(3, 0), "tp": tp}
    bp = {"chain": at(0, 1), "tp": tp}
    bm = {"chain": at(0, 3), "tp": tp}

    loads = {}
    for k, (name, src, dst) in enumerate(
        [
            ("tok", tok_h, tok), ("wkv", wkv_h, wkv), ("wq", wq_h, wq), ("kvg", kvg_h, kvg),
            ("qg", qg_h, qg), ("tabk", tab_h.at[chain, piece], tabk), ("wa", wa_h, wa),
            ("wu", wu_h, wu), ("wv", wv_h, wv), ("tab0", tab_h.at[chain, :, half], tabq.at[0]),
            ("tab1", tab_h.at[mirror, :, half], tabq.at[1]),
        ]
    ):
        loads[name] = pltpu.make_async_copy(src, dst, load_sem.at[k])
        if name in ("tok", "wkv", "kvg", "tabk"):
            loads[name].start()

    def loaded(*names):
        for name in names:
            loads[name].wait()

    barrier = pltpu.get_barrier_semaphore()
    partners = (sibling, up, down, pair, ap, am, bp, bm)
    for device in partners:
        pl.semaphore_signal(barrier, inc=1, device_id=device, device_id_type=MESH)
    for name in ("wq", "qg"):
        loads[name].start()

    sent = []

    def send(src, dst, recv, device):
        copy = pltpu.make_async_remote_copy(
            src_ref=src, dst_ref=dst, send_sem=send_sem.at[len(sent)], recv_sem=recv,
            device_id=device, device_id_type=MESH,
        )
        copy.start()
        sent.append(copy)

    def arrived(dst, recv):
        pltpu.make_async_remote_copy(
            src_ref=dst, dst_ref=dst, send_sem=send_sem.at[0], recv_sem=recv,
            device_id=sibling, device_id_type=MESH,
        ).wait_recv()

    def rows_of(c):
        return tok[pl.ds(pl.multiple_of(c * 128, 128), 128), :]

    def project_keys(c, dst):
        dst[...] = lax.dot_general(rows_of(c), wkv[...], NT, preferred_element_type=jnp.float32)

    def project_queries(c, dst):
        left = rows_of(c)

        def tile(i, _):
            cols = pl.ds(pl.multiple_of(i * 512, 512), 512)
            dst[:, cols] = jnp.dot(left, wq[:, cols], preferred_element_type=jnp.float32)
            return 0

        lax.fori_loop(0, 3, tile, 0)

    def ring_of(own, got, out, came, sems):
        def part(yy, h):
            rows = pl.ds(pl.multiple_of(yy * 32 + h * 16, 16), 16)
            return own[rows, :] + got[rows, :]

        def push(k, value, device):
            out[k] = value.astype(out.dtype)
            send(out.at[k], came.at[k], sems.at[k], device)

        def start():
            push(0, part(yf, 0), up)
            push(1, part(yf, 1), down)
            push(2, part(yp, 1), up)
            push(3, part(ym, 0), down)

        def middle():
            arrived(came.at[0], sems.at[0])
            push(4, part(yp, 0) + came[0].astype(jnp.float32), up)
            arrived(came.at[1], sems.at[1])
            push(5, part(ym, 1) + came[1].astype(jnp.float32), down)

        def end():
            for k in (2, 3, 4, 5):
                arrived(came.at[k], sems.at[k])
            totals = []
            for h, first, second in ((0, 4, 3), (1, 2, 5)):
                total = part(y, h) + came[first].astype(jnp.float32)
                totals.append(total + came[second].astype(jnp.float32))
            return totals

        return start, middle, end

    keys_start, keys_middle, keys_end = ring_of(pok, prk, rks, rkr, rk_sem)
    queries_start, queries_middle, queries_end = ring_of(poq, prq, rqs, rqr, rq_sem)

    loaded("tok", "wkv")
    project_keys(other, psk)
    pl.semaphore_wait(barrier, len(partners))
    send(psk, prk, sib_sem.at[0], sibling)
    project_keys(core, pok)
    arrived(prk, sib_sem.at[0])
    keys_start()
    loaded("wq")
    for name in ("wa", "wu", "wv", "tab0", "tab1"):
        loads[name].start()
    project_queries(other, psq)
    send(psq, prq, sib_sem.at[1], sibling)
    keys_middle()
    project_queries(core, poq)
    arrived(prq, sib_sem.at[1])
    queries_start()

    slot_own = 2 * chain + core

    def keys_y(yy, h, n):
        return kb.at[slot_own, pl.ds(pl.multiple_of(yy * 32 + h * 16, 16), n)]

    loaded("kvg", "tabk")
    gain_kv = jnp.concatenate([kvg[k : k + 1, :] for k in range(LAT // 128)], 1)
    for h, total in enumerate(keys_end()):
        latent = normalize(total[:, :LAT], gain_kv)
        turned = rotate(total[:, LAT:], tabk[h])
        rows = pl.ds(pl.multiple_of(y * 32 + h * 16, 16), 16)
        kb[slot_own, rows, :LAT] = latent.astype(jnp.bfloat16)
        kb[slot_own, rows, LAT:] = jnp.concatenate(
            [turned, jnp.zeros_like(turned)], 1
        ).astype(jnp.bfloat16)
    for k, device in enumerate((up, down)):
        send(keys_y(y, 0, 32), keys_y(y, 0, 32), ky_sem.at[k], device)
    arrived(keys_y(ym, 0, 32), ky_sem.at[0])
    send(keys_y(ym, 0, 16), keys_y(ym, 0, 16), ky_sem.at[2], up)
    arrived(keys_y(yp, 0, 32), ky_sem.at[1])
    send(keys_y(yp, 1, 16), keys_y(yp, 1, 16), ky_sem.at[3], down)

    def block(n, p=None):
        if p is None:
            return kb.at[2 * n + core]
        return kb.at[2 * n + core, pl.ds(64 * p, 64)]

    def pass_on(n, *devices):
        for device in devices:
            send(block(n), block(n), kp_sem.at[n, 0], device)
        send(block(n), block(n), ks_sem.at[n], sibling)

    def pass_part(n, p, device):
        send(block(n, p), block(n, p), kp_sem.at[n, p], device)

    def whole(n):
        arrived(block(n), kp_sem.at[n, 0])

    def halves(n):
        for p in range(2):
            arrived(block(n, p), kp_sem.at[n, p])

    def relay(u, v):
        n = at(u, v)
        if v == 2 or (u, v) == (2, 0):
            halves(n)
        else:
            whole(n)
        if v == 0:
            if u != 2:
                pass_part(n, 0 if u == 3 else 1, ap if u == 3 else am)
            pass_on(n, bp, bm)
        else:
            if v != 2:
                pass_part(n, 0 if v == 3 else 1, bp if v == 3 else bm)
            pass_on(n)

    arrived(keys_y(yf, 0, 16), ky_sem.at[2])
    arrived(keys_y(yf, 1, 16), ky_sem.at[3])
    pass_on(at(0, 0), ap, am, bp, bm)
    acc[...] = jnp.zeros_like(acc)
    tot[...] = jnp.zeros_like(tot)
    mx[...] = jnp.full_like(mx, FLOOR_SCORE)
    queries_middle()

    loaded("qg")
    gain_q = jnp.concatenate([qg[k : k + 1, :] for k in range(QL // 128)], 1)
    for h, total in enumerate(queries_end()):
        cs[h] = normalize(total, gain_q).astype(jnp.bfloat16)

    def give(s, p, *devices):
        for device in devices:
            send(cq.at[s, p], cq.at[s, p], cq_sem.at[s, p], device)

    def take(s, p):
        arrived(cq.at[s, p], cq_sem.at[s, p])

    send(cs.at[1 - half], cq.at[1, piece], cq_sem.at[1, piece], pair)
    cq[0, piece] = cs[half]
    give(0, piece, up, down, sibling)
    pm, pp, pf = core * 4 + ym, core * 4 + yp, core * 4 + yf
    for u, v in RINGS[1:5]:
        relay(u, v)
    take(1, piece)
    give(1, piece, up, down, sibling)
    take(0, pm)
    give(0, pm, up, sibling)
    take(0, pp)
    give(0, pp, sibling)
    for u, v in RINGS[5:7]:
        relay(u, v)
    take(1, pp)
    give(1, pp, down, sibling)
    take(1, pm)
    give(1, pm, sibling)
    for u, v in RINGS[7:11]:
        relay(u, v)
    take(0, pf)
    give(0, pf, sibling)
    take(1, pf)
    give(1, pf, sibling)
    for u, v in RINGS[11:15]:
        relay(u, v)
    for s in range(2):
        for yy in range(4):
            take(s, other * 4 + yy)

    loaded("wa", "wu", "tab0", "tab1")

    def expand(i, _):
        cols = pl.ds(pl.multiple_of(i * 384, 384), 384)
        rows = cq[...].reshape(256, QL)
        projected = jnp.dot(rows, wu[:, cols], preferred_element_type=jnp.float32)
        table = tabq[...].reshape(256, 2 * ROPE)
        for j in range(2):
            head = 2 * i + j
            base = j * (NOPE + ROPE)
            nope = projected[:, base : base + NOPE].astype(jnp.bfloat16)
            turned = rotate(projected[:, base + NOPE : base + NOPE + ROPE], table)
            turned = jnp.concatenate([turned, jnp.zeros_like(turned)], 1).astype(jnp.bfloat16)
            absorbed = jnp.dot(nope, wa[head], preferred_element_type=jnp.float32)
            absorbed = absorbed.astype(jnp.bfloat16)
            places = pl.ds(pl.multiple_of(head * 128, 128), 128)
            for s in range(2):
                qb[s, places, :LAT] = absorbed[s * 128 : s * 128 + 128]
                qb[s, places, LAT:] = turned[s * 128 : s * 128 + 128]
        return 0

    lax.fori_loop(0, HEADS // 2, expand, 0)
    relay(2, 2)

    def meet(c):
        for k in range(4):
            n = 4 * c + k
            arrived(kb.at[2 * n + other], ks_sem.at[n])

    meet(0)

    token = lax.broadcasted_iota(jnp.int32, (512, 1), 0) & 127
    place = ((token >> 4) << 5) + (token & 15) + half * 16
    key_iota = lax.broadcasted_iota(jnp.int32, (1, 1024), 1)

    def score(s, c, r):
        keys = kb[pl.ds(8 * c, 8)].reshape(1024, KEYW)
        queries = qb[s, pl.ds(pl.multiple_of(r * 512, 512), 512), :]
        return lax.dot_general(queries, keys, NT, preferred_element_type=jnp.float32)

    def tile(s, r, c, blk, size, last, following):
        rows = pl.ds(pl.multiple_of(r * 512, 512), 512)
        scores = first[:, :size] * SCALE2
        if following is not None:
            first[...] = score(*following)
        if last:
            visible = key_iota[:, :size] + 1024 * c <= place + 256 * blk
            scores = jnp.where(visible, scores, FLOOR_SCORE)
        parts = [scores[:, k : k + 128] for k in range(0, size, 128)]
        before = mx[s, rows, :]
        top = jnp.max(functools.reduce(jnp.maximum, parts), 1, keepdims=True)
        peak = jnp.maximum(before, top)
        shrink = jnp.exp2(before - peak)
        weights = [jnp.exp2(p - peak) for p in parts]
        mx[s, rows, :] = peak
        tot[s, rows, :] = tot[s, rows, :] * shrink + sum(weights[1:], weights[0])
        weights = jnp.concatenate([w.astype(jnp.bfloat16) for w in weights], 1)
        latent = kb[pl.ds(8 * c, size // 128), :, :LAT].reshape(size, LAT)
        mixed = jnp.dot(weights, latent, preferred_element_type=jnp.float32)
        shrink = jnp.concatenate([shrink] * (LAT // 128), 1)
        acc[s, rows, :] = acc[s, rows, :] * shrink + mixed

    def attend(s, r, blk, met, after):
        def step(c, _):
            @pl.when(c + 1 > met)
            def _():
                meet(c + 1)

            tile(s, r, c, blk, 1024, False, (s, c + 1, r))
            return 0

        lax.fori_loop(0, blk // 4, step, 0)
        for k in range(4):
            @pl.when(blk % 4 == k)
            def _():
                tile(s, r, blk // 4, blk, 256 * k + 256, True, after)

        finish(s, r)

    def out_cols(r):
        return pl.ds(pl.multiple_of(r * 512, 512), 512)

    def out_copy(r):
        return pltpu.make_async_remote_copy(
            src_ref=ob.at[1, :, :, out_cols(r)], dst_ref=out_h.at[:, half, :, out_cols(r)],
            send_sem=outs_sem.at[r], recv_sem=out_sem.at[r], device_id=pair, device_id_type=MESH,
        )

    def own_copy(r):
        return pltpu.make_async_copy(
            ob.at[0, :, :, out_cols(r)], out_h.at[:, half, :, out_cols(r)], own_sem.at[r]
        )

    def finish(s, r):
        for k in range(4):
            part = pl.ds(pl.multiple_of(r * 512 + k * 128, 128), 128)
            total = jnp.sum(tot[s, part, :], 1, keepdims=True)
            mixed = (acc[s, part, :] * (1.0 / total)).astype(jnp.bfloat16)
            value = jnp.dot(mixed, wv[4 * r + k], preferred_element_type=jnp.float32)
            ob[s, :, :, part] = value.astype(jnp.bfloat16).reshape(8, 16, VH)
        (own_copy, out_copy)[s](r).start()

    loaded("wv")
    first[...] = score(1, 0, 0)

    def far_pass(r, _):
        attend(1, r, mirror, r * (3 - z), (1 - r, 0, 1 - r))
        return 0

    lax.fori_loop(0, 2, far_pass, 0)
    attend(0, 0, chain, 3 - z, (0, 0, 1))
    attend(0, 1, chain, 3, None)

    def rest(c, _):
        meet(c)
        return 0

    lax.fori_loop(jnp.maximum(3 - z, z) + 1, 4, rest, 0)
    for j in range(2):
        rows = pl.ds(pl.multiple_of(tp * 16, 16), 16)
        cache_ref[j] = kb[slot_ref[j], rows, :][:, :KV]
    for r in range(2):
        own_copy(r).wait()
        out_copy(r).wait_send()
        arrived(out_h.at[:, 1 - half, :, out_cols(r)], out_sem.at[r])
    for copy in sent:
        copy.wait_send()


def hand_over(att_h, cache_h, att_out, cache_out, att, cache, sem):
    pieces = [(cache_h, cache, cache_out)]
    for k in range(4):
        rows = pl.ds(64 * k, 64)
        pieces.append((att_h.at[rows], att.at[rows], att_out.at[rows]))
    into = [pltpu.make_async_copy(p[0], p[1], sem.at[0, k]) for k, p in enumerate(pieces)]
    out = [pltpu.make_async_copy(p[1], p[2], sem.at[1, k]) for k, p in enumerate(pieces)]
    for copy in into:
        copy.start()
    for first, second in zip(into, out):
        first.wait()
        second.start()
    for copy in out:
        copy.wait()


def per_device(tokens, w_down_q, w_down_kv, q_gain, kv_gain, w_up_q, w_absorb, w_value, slot_block):
    bf16, f32 = jnp.bfloat16, jnp.float32
    table = jnp.asarray(rotary_tables())
    hbm = pl.BlockSpec(memory_space=pl.ANY)
    dma = pltpu.SemaphoreType.DMA
    attended, cache = pl.pallas_call(
        kernel,
        out_shape=(
            jax.ShapeDtypeStruct((8, 2, 16, HEADS * VH), bf16),
            jax.ShapeDtypeStruct((2, 16, KV), bf16),
        ),
        in_specs=[hbm] * 8 + [pl.BlockSpec(memory_space=pltpu.SMEM), hbm],
        out_specs=(hbm, pl.BlockSpec(memory_space=pltpu.VMEM)),
        scratch_shapes=[
            pltpu.VMEM((256, 896), bf16),
            pltpu.VMEM((896, QL), bf16),
            pltpu.VMEM((KV, 896), bf16),
            pltpu.VMEM((QL // 128, 128), f32),
            pltpu.VMEM((LAT // 128, 128), f32),
            pltpu.VMEM((QL, HEADS * (NOPE + ROPE)), bf16),
            pltpu.VMEM((HEADS, NOPE, LAT), bf16),
            pltpu.VMEM((HEADS, LAT, VH), bf16),
            pltpu.VMEM((2, 16, 2 * ROPE), f32),
            pltpu.VMEM((2, 8, 16, 2 * ROPE), f32),
            pltpu.VMEM((128, KV), f32),
            pltpu.VMEM((128, KV), f32),
            pltpu.VMEM((128, KV), f32),
            pltpu.VMEM((128, QL), f32),
            pltpu.VMEM((128, QL), f32),
            pltpu.VMEM((128, QL), f32),
            pltpu.VMEM((6, 16, KV), bf16),
            pltpu.VMEM((6, 16, KV), bf16),
            pltpu.VMEM((6, 16, QL), f32),
            pltpu.VMEM((6, 16, QL), f32),
            pltpu.VMEM((2, 16, QL), bf16),
            pltpu.VMEM((2, 8, 16, QL), bf16),
            pltpu.VMEM((32, 128, KEYW), bf16),
            pltpu.VMEM((2, HEADS * 128, KEYW), bf16),
            pltpu.VMEM((512, 1024), f32),
            pltpu.VMEM((2, HEADS * 128, LAT), f32),
            pltpu.VMEM((2, HEADS * 128, 128), f32),
            pltpu.VMEM((2, HEADS * 128, 128), f32),
            pltpu.VMEM((2, 8, 16, HEADS * VH), bf16),
            dma((11,)),
            dma((N_SEND,)),
            dma((2,)),
            dma((6,)),
            dma((6,)),
            dma((2, 8)),
            dma((4,)),
            dma((16, 2)),
            dma((16,)),
            dma((2,)),
            dma((2,)),
            dma((2,)),
        ],
        compiler_params=pltpu.CompilerParams(
            collective_id=0, has_side_effects=True, vmem_limit_bytes=56 * 2**20
        ),
    )(
        tokens, w_down_q, w_down_kv.T, q_gain.reshape(-1, 128), kv_gain.reshape(-1, 128),
        w_up_q, w_absorb, w_value, slot_block, table,
    )
    attended = attended.reshape(256, HEADS * VH)
    return pl.pallas_call(
        hand_over,
        out_shape=(
            jax.ShapeDtypeStruct(attended.shape, bf16),
            jax.ShapeDtypeStruct(cache.shape, bf16),
        ),
        in_specs=[hbm, hbm],
        out_specs=(hbm, hbm),
        scratch_shapes=[
            pltpu.VMEM(attended.shape, bf16),
            pltpu.VMEM(cache.shape, bf16),
            dma((2, 5)),
        ],
        compiler_params=pltpu.CompilerParams(vmem_limit_bytes=60 * 2**20),
    )(attended, cache)


def solution(mesh):
    placed = (
        P("chain", "tp"),
        P("tp", None),
        P("tp", None),
        P(),
        P(),
        P(None, "tp"),
        P("tp", None, None),
        P("tp", None, None),
        P("chain"),
    )
    return jax.shard_map(
        per_device,
        mesh=mesh,
        in_specs=placed,
        out_specs=(P("chain", "tp"), P("chain", "tp", None)),
        check_vma=False,
    )
```

```python
import functools
import math

import jax
import jax.numpy as jnp
import numpy as np
from jax import lax
from jax.experimental import pallas as pl
from jax.experimental.pallas import tpu as pltpu
from jax.sharding import PartitionSpec as P

MESH = pl.DeviceIdType.MESH
ROPE_BASE = 50000.0
FLOOR_SCORE = -1e30
QL, LAT, ROPE, NOPE, VH, HEADS = 1536, 512, 64, 128, 128, 8
KEYW = 640
KV = LAT + ROPE
SCALE2 = (NOPE + ROPE) ** -0.5 * math.log2(math.e)
NT = (((1,), (1,)), ((), ()))
N_SEND = 80
RINGS = (
    (0, 0), (3, 0), (1, 0), (0, 3), (0, 1), (2, 0), (0, 2), (3, 3), (3, 1), (1, 3), (1, 1),
    (2, 3), (2, 1), (3, 2), (1, 2), (2, 2),
)


def rotary_tables():
    inverse = ROPE_BASE ** (-2.0 * np.arange(ROPE // 2) / ROPE)
    angles = np.arange(4096)[:, None] * inverse[None, :]
    cosine = np.concatenate([np.cos(angles), np.cos(angles)], 1)
    sine = np.concatenate([-np.sin(angles), np.sin(angles)], 1)
    both = np.concatenate([cosine, sine], 1).astype(np.float32)
    return both.reshape(16, 8, 2, 16, 2 * ROPE)


def rotate(values, table):
    half = ROPE // 2
    swapped = jnp.concatenate([values[:, half:], values[:, :half]], 1)
    return values * table[:, :ROPE] + swapped * table[:, ROPE:]


def normalize(values, gain):
    return values * lax.rsqrt(jnp.mean(values * values, -1, keepdims=True) + 1e-06) * gain


def kernel(
    tok_h, wq_h, wkv_h, qg_h, kvg_h, wu_h, wa_h, wv_h, slot_ref, tab_h,
    out_h, cache_ref,
    tok, wq, wkv, qg, kvg, wu, wa, wv, tabk, tabq,
    psk, pok, prk, psq, poq, prq, rks, rkr, rqs, rqr, cs, cq, kb, qb, first, acc, mx, tot, ob,
    load_sem, send_sem, sib_sem, rk_sem, rq_sem, cq_sem, ky_sem, kp_sem, ks_sem, out_sem, outs_sem, own_sem,
):
    chain = lax.axis_index("chain")
    tp = lax.axis_index("tp")
    z, x = chain // 4, chain % 4
    y, core = tp // 2, tp % 2
    other = 1 - core
    mirror = 15 - chain
    half = chain // 8
    piece = core * 4 + y
    yp, ym, yf = (y + 1) % 4, (y + 3) % 4, (y + 2) % 4
    sibling = {"chain": chain, "tp": 2 * y + other}
    up = {"chain": chain, "tp": 2 * yp + core}
    down = {"chain": chain, "tp": 2 * ym + core}
    pair = {"chain": mirror, "tp": tp}
    a = x + core * (z - x)
    b = z + core * (x - z)
    stride_a, stride_b = 1 + 3 * core, 4 - 3 * core

    def at(da, db):
        return ((a + da) % 4) * stride_a + ((b + db) % 4) * stride_b

    ap = {"chain": at(1, 0), "tp": tp}
    am = {"chain": at(3, 0), "tp": tp}
    bp = {"chain": at(0, 1), "tp": tp}
    bm = {"chain": at(0, 3), "tp": tp}

    loads = {}
    for k, (name, src, dst) in enumerate(
        [
            ("tok", tok_h, tok), ("wkv", wkv_h, wkv), ("wq", wq_h, wq), ("kvg", kvg_h, kvg),
            ("qg", qg_h, qg), ("tabk", tab_h.at[chain, piece], tabk), ("wa", wa_h, wa),
            ("wu", wu_h, wu), ("wv", wv_h, wv), ("tab0", tab_h.at[chain, :, half], tabq.at[0]),
            ("tab1", tab_h.at[mirror, :, half], tabq.at[1]),
        ]
    ):
        loads[name] = pltpu.make_async_copy(src, dst, load_sem.at[k])
        if name in ("tok", "wkv", "kvg", "tabk"):
            loads[name].start()

    def loaded(*names):
        for name in names:
            loads[name].wait()

    barrier = pltpu.get_barrier_semaphore()
    partners = (sibling, up, down, pair, ap, am, bp, bm)
    for device in partners:
        pl.semaphore_signal(barrier, inc=1, device_id=device, device_id_type=MESH)
    for name in ("wq", "qg"):
        loads[name].start()

    sent = []

    def send(src, dst, recv, device):
        copy = pltpu.make_async_remote_copy(
            src_ref=src, dst_ref=dst, send_sem=send_sem.at[len(sent)], recv_sem=recv,
            device_id=device, device_id_type=MESH,
        )
        copy.start()
        sent.append(copy)

    def arrived(dst, recv):
        pltpu.make_async_remote_copy(
            src_ref=dst, dst_ref=dst, send_sem=send_sem.at[0], recv_sem=recv,
            device_id=sibling, device_id_type=MESH,
        ).wait_recv()

    def rows_of(c):
        return tok[pl.ds(pl.multiple_of(c * 128, 128), 128), :]

    def project_keys(c, dst):
        dst[...] = lax.dot_general(rows_of(c), wkv[...], NT, preferred_element_type=jnp.float32)

    def project_queries(c, dst):
        left = rows_of(c)

        def tile(i, _):
            cols = pl.ds(pl.multiple_of(i * 512, 512), 512)
            dst[:, cols] = jnp.dot(left, wq[:, cols], preferred_element_type=jnp.float32)
            return 0

        lax.fori_loop(0, 3, tile, 0)

    def ring_of(own, got, out, came, sems):
        def part(yy, h):
            rows = pl.ds(pl.multiple_of(yy * 32 + h * 16, 16), 16)
            return own[rows, :] + got[rows, :]

        def push(k, value, device):
            out[k] = value.astype(out.dtype)
            send(out.at[k], came.at[k], sems.at[k], device)

        def start():
            push(0, part(yf, 0), up)
            push(1, part(yf, 1), down)
            push(2, part(yp, 1), up)
            push(3, part(ym, 0), down)

        def middle():
            arrived(came.at[0], sems.at[0])
            push(4, part(yp, 0) + came[0].astype(jnp.float32), up)
            arrived(came.at[1], sems.at[1])
            push(5, part(ym, 1) + came[1].astype(jnp.float32), down)

        def end():
            for k in (2, 3, 4, 5):
                arrived(came.at[k], sems.at[k])
            totals = []
            for h, first, second in ((0, 4, 3), (1, 2, 5)):
                total = part(y, h) + came[first].astype(jnp.float32)
                totals.append(total + came[second].astype(jnp.float32))
            return totals

        return start, middle, end

    keys_start, keys_middle, keys_end = ring_of(pok, prk, rks, rkr, rk_sem)
    queries_start, queries_middle, queries_end = ring_of(poq, prq, rqs, rqr, rq_sem)

    loaded("tok", "wkv")
    project_keys(other, psk)
    pl.semaphore_wait(barrier, len(partners))
    send(psk, prk, sib_sem.at[0], sibling)
    project_keys(core, pok)
    arrived(prk, sib_sem.at[0])
    keys_start()
    loaded("wq")
    for name in ("wa", "wu", "wv", "tab0", "tab1"):
        loads[name].start()
    project_queries(other, psq)
    send(psq, prq, sib_sem.at[1], sibling)
    keys_middle()
    project_queries(core, poq)
    arrived(prq, sib_sem.at[1])
    queries_start()

    slot_own = 2 * chain + core

    def keys_y(yy, h, n):
        return kb.at[slot_own, pl.ds(pl.multiple_of(yy * 32 + h * 16, 16), n)]

    loaded("kvg", "tabk")
    gain_kv = jnp.concatenate([kvg[k : k + 1, :] for k in range(LAT // 128)], 1)
    for h, total in enumerate(keys_end()):
        latent = normalize(total[:, :LAT], gain_kv)
        turned = rotate(total[:, LAT:], tabk[h])
        rows = pl.ds(pl.multiple_of(y * 32 + h * 16, 16), 16)
        kb[slot_own, rows, :LAT] = latent.astype(jnp.bfloat16)
        kb[slot_own, rows, LAT:] = jnp.concatenate(
            [turned, jnp.zeros_like(turned)], 1
        ).astype(jnp.bfloat16)
    for k, device in enumerate((up, down)):
        send(keys_y(y, 0, 32), keys_y(y, 0, 32), ky_sem.at[k], device)
    arrived(keys_y(ym, 0, 32), ky_sem.at[0])
    send(keys_y(ym, 0, 16), keys_y(ym, 0, 16), ky_sem.at[2], up)
    arrived(keys_y(yp, 0, 32), ky_sem.at[1])
    send(keys_y(yp, 1, 16), keys_y(yp, 1, 16), ky_sem.at[3], down)

    def block(n, p=None):
        if p is None:
            return kb.at[2 * n + core]
        return kb.at[2 * n + core, pl.ds(64 * p, 64)]

    def pass_on(n, *devices):
        for device in devices:
            send(block(n), block(n), kp_sem.at[n, 0], device)
        send(block(n), block(n), ks_sem.at[n], sibling)

    def pass_part(n, p, device):
        send(block(n, p), block(n, p), kp_sem.at[n, p], device)

    def whole(n):
        arrived(block(n), kp_sem.at[n, 0])

    def halves(n):
        for p in range(2):
            arrived(block(n, p), kp_sem.at[n, p])

    def relay(u, v):
        n = at(u, v)
        if v == 2 or (u, v) == (2, 0):
            halves(n)
        else:
            whole(n)
        if v == 0:
            if u != 2:
                pass_part(n, 0 if u == 3 else 1, ap if u == 3 else am)
            pass_on(n, bp, bm)
        else:
            if v != 2:
                pass_part(n, 0 if v == 3 else 1, bp if v == 3 else bm)
            pass_on(n)

    arrived(keys_y(yf, 0, 16), ky_sem.at[2])
    arrived(keys_y(yf, 1, 16), ky_sem.at[3])
    pass_on(at(0, 0), ap, am, bp, bm)
    acc[...] = jnp.zeros_like(acc)
    tot[...] = jnp.zeros_like(tot)
    mx[...] = jnp.full_like(mx, FLOOR_SCORE)
    queries_middle()

    loaded("qg")
    gain_q = jnp.concatenate([qg[k : k + 1, :] for k in range(QL // 128)], 1)
    for h, total in enumerate(queries_end()):
        cs[h] = normalize(total, gain_q).astype(jnp.bfloat16)

    def give(s, p, *devices):
        for device in devices:
            send(cq.at[s, p], cq.at[s, p], cq_sem.at[s, p], device)

    def take(s, p):
        arrived(cq.at[s, p], cq_sem.at[s, p])

    send(cs.at[1 - half], cq.at[1, piece], cq_sem.at[1, piece], pair)
    cq[0, piece] = cs[half]
    give(0, piece, up, down, sibling)
    pm, pp, pf = core * 4 + ym, core * 4 + yp, core * 4 + yf
    for u, v in RINGS[1:5]:
        relay(u, v)
    take(1, piece)
    give(1, piece, up, down, sibling)
    take(0, pm)
    give(0, pm, up, sibling)
    take(0, pp)
    give(0, pp, sibling)
    take(1, pp)
    give(1, pp, down, sibling)
    for u, v in RINGS[5:7]:
        relay(u, v)
    take(1, pm)
    give(1, pm, sibling)
    for u, v in RINGS[7:11]:
        relay(u, v)
    take(0, pf)
    give(0, pf, sibling)
    take(1, pf)
    give(1, pf, sibling)
    for u, v in RINGS[11:15]:
        relay(u, v)
    for s in range(2):
        for yy in range(4):
            take(s, other * 4 + yy)

    loaded("wa", "wu", "tab0", "tab1")

    def expand(i, _):
        cols = pl.ds(pl.multiple_of(i * 384, 384), 384)
        rows = cq[...].reshape(256, QL)
        projected = jnp.dot(rows, wu[:, cols], preferred_element_type=jnp.float32)
        table = tabq[...].reshape(256, 2 * ROPE)
        for j in range(2):
            head = 2 * i + j
            base = j * (NOPE + ROPE)
            nope = projected[:, base : base + NOPE].astype(jnp.bfloat16)
            turned = rotate(projected[:, base + NOPE : base + NOPE + ROPE], table)
            turned = jnp.concatenate([turned, jnp.zeros_like(turned)], 1).astype(jnp.bfloat16)
            absorbed = jnp.dot(nope, wa[head], preferred_element_type=jnp.float32)
            absorbed = absorbed.astype(jnp.bfloat16)
            places = pl.ds(pl.multiple_of(head * 128, 128), 128)
            for s in range(2):
                qb[s, places, :LAT] = absorbed[s * 128 : s * 128 + 128]
                qb[s, places, LAT:] = turned[s * 128 : s * 128 + 128]
        return 0

    lax.fori_loop(0, HEADS // 2, expand, 0)
    relay(2, 2)

    def meet(c):
        for k in range(4):
            n = 4 * c + k
            arrived(kb.at[2 * n + other], ks_sem.at[n])

    meet(0)

    token = lax.broadcasted_iota(jnp.int32, (512, 1), 0) & 127
    place = ((token >> 4) << 5) + (token & 15) + half * 16
    key_iota = lax.broadcasted_iota(jnp.int32, (1, 1024), 1)

    def score(s, c, r):
        keys = kb[pl.ds(8 * c, 8)].reshape(1024, KEYW)
        queries = qb[s, pl.ds(pl.multiple_of(r * 512, 512), 512), :]
        return lax.dot_general(queries, keys, NT, preferred_element_type=jnp.float32)

    def tile(s, r, c, blk, size, last, following):
        rows = pl.ds(pl.multiple_of(r * 512, 512), 512)
        scores = first[:, :size] * SCALE2
        if following is not None:
            first[...] = score(*following)
        if last:
            visible = key_iota[:, :size] + 1024 * c <= place + 256 * blk
            scores = jnp.where(visible, scores, FLOOR_SCORE)
        parts = [scores[:, k : k + 128] for k in range(0, size, 128)]
        before = mx[s, rows, :]
        top = jnp.max(functools.reduce(jnp.maximum, parts), 1, keepdims=True)
        peak = jnp.maximum(before, top)
        shrink = jnp.exp2(before - peak)
        weights = [jnp.exp2(p - peak) for p in parts]
        mx[s, rows, :] = peak
        tot[s, rows, :] = tot[s, rows, :] * shrink + sum(weights[1:], weights[0])
        weights = jnp.concatenate([w.astype(jnp.bfloat16) for w in weights], 1)
        latent = kb[pl.ds(8 * c, size // 128), :, :LAT].reshape(size, LAT)
        mixed = jnp.dot(weights, latent, preferred_element_type=jnp.float32)
        shrink = jnp.concatenate([shrink] * (LAT // 128), 1)
        acc[s, rows, :] = acc[s, rows, :] * shrink + mixed

    def attend(s, r, blk, met, after):
        def step(c, _):
            @pl.when(c + 1 > met)
            def _():
                meet(c + 1)

            tile(s, r, c, blk, 1024, False, (s, c + 1, r))
            return 0

        lax.fori_loop(0, blk // 4, step, 0)
        for k in range(4):
            @pl.when(blk % 4 == k)
            def _():
                tile(s, r, blk // 4, blk, 256 * k + 256, True, after)

        finish(s, r)

    def out_cols(r):
        return pl.ds(pl.multiple_of(r * 512, 512), 512)

    def out_copy(r):
        return pltpu.make_async_remote_copy(
            src_ref=ob.at[1, :, :, out_cols(r)], dst_ref=out_h.at[:, half, :, out_cols(r)],
            send_sem=outs_sem.at[r], recv_sem=out_sem.at[r], device_id=pair, device_id_type=MESH,
        )

    def own_copy(r):
        return pltpu.make_async_copy(
            ob.at[0, :, :, out_cols(r)], out_h.at[:, half, :, out_cols(r)], own_sem.at[r]
        )

    def finish(s, r):
        for k in range(4):
            part = pl.ds(pl.multiple_of(r * 512 + k * 128, 128), 128)
            total = jnp.sum(tot[s, part, :], 1, keepdims=True)
            mixed = (acc[s, part, :] * (1.0 / total)).astype(jnp.bfloat16)
            value = jnp.dot(mixed, wv[4 * r + k], preferred_element_type=jnp.float32)
            ob[s, :, :, part] = value.astype(jnp.bfloat16).reshape(8, 16, VH)
        (own_copy, out_copy)[s](r).start()

    loaded("wv")
    first[...] = score(1, 0, 0)

    def far_pass(r, _):
        attend(1, r, mirror, r * (3 - z), (1 - r, 0, 1 - r))
        return 0

    lax.fori_loop(0, 2, far_pass, 0)
    attend(0, 0, chain, 3 - z, (0, 0, 1))
    attend(0, 1, chain, 3, None)

    def rest(c, _):
        meet(c)
        return 0

    lax.fori_loop(jnp.maximum(3 - z, z) + 1, 4, rest, 0)
    for j in range(2):
        rows = pl.ds(pl.multiple_of(tp * 16, 16), 16)
        cache_ref[j] = kb[slot_ref[j], rows, :][:, :KV]
    for r in range(2):
        own_copy(r).wait()
        out_copy(r).wait_send()
        arrived(out_h.at[:, 1 - half, :, out_cols(r)], out_sem.at[r])
    for copy in sent:
        copy.wait_send()


def hand_over(att_h, cache_h, att_out, cache_out, att, cache, sem):
    pieces = [(cache_h, cache, cache_out)]
    for k in range(4):
        rows = pl.ds(64 * k, 64)
        pieces.append((att_h.at[rows], att.at[rows], att_out.at[rows]))
    into = [pltpu.make_async_copy(p[0], p[1], sem.at[0, k]) for k, p in enumerate(pieces)]
    out = [pltpu.make_async_copy(p[1], p[2], sem.at[1, k]) for k, p in enumerate(pieces)]
    for copy in into:
        copy.start()
    for first, second in zip(into, out):
        first.wait()
        second.start()
    for copy in out:
        copy.wait()


def per_device(tokens, w_down_q, w_down_kv, q_gain, kv_gain, w_up_q, w_absorb, w_value, slot_block):
    bf16, f32 = jnp.bfloat16, jnp.float32
    table = jnp.asarray(rotary_tables())
    hbm = pl.BlockSpec(memory_space=pl.ANY)
    dma = pltpu.SemaphoreType.DMA
    attended, cache = pl.pallas_call(
        kernel,
        out_shape=(
            jax.ShapeDtypeStruct((8, 2, 16, HEADS * VH), bf16),
            jax.ShapeDtypeStruct((2, 16, KV), bf16),
        ),
        in_specs=[hbm] * 8 + [pl.BlockSpec(memory_space=pltpu.SMEM), hbm],
        out_specs=(hbm, pl.BlockSpec(memory_space=pltpu.VMEM)),
        scratch_shapes=[
            pltpu.VMEM((256, 896), bf16),
            pltpu.VMEM((896, QL), bf16),
            pltpu.VMEM((KV, 896), bf16),
            pltpu.VMEM((QL // 128, 128), f32),
            pltpu.VMEM((LAT // 128, 128), f32),
            pltpu.VMEM((QL, HEADS * (NOPE + ROPE)), bf16),
            pltpu.VMEM((HEADS, NOPE, LAT), bf16),
            pltpu.VMEM((HEADS, LAT, VH), bf16),
            pltpu.VMEM((2, 16, 2 * ROPE), f32),
            pltpu.VMEM((2, 8, 16, 2 * ROPE), f32),
            pltpu.VMEM((128, KV), f32),
            pltpu.VMEM((128, KV), f32),
            pltpu.VMEM((128, KV), f32),
            pltpu.VMEM((128, QL), f32),
            pltpu.VMEM((128, QL), f32),
            pltpu.VMEM((128, QL), f32),
            pltpu.VMEM((6, 16, KV), bf16),
            pltpu.VMEM((6, 16, KV), bf16),
            pltpu.VMEM((6, 16, QL), f32),
            pltpu.VMEM((6, 16, QL), f32),
            pltpu.VMEM((2, 16, QL), bf16),
            pltpu.VMEM((2, 8, 16, QL), bf16),
            pltpu.VMEM((32, 128, KEYW), bf16),
            pltpu.VMEM((2, HEADS * 128, KEYW), bf16),
            pltpu.VMEM((512, 1024), f32),
            pltpu.VMEM((2, HEADS * 128, LAT), f32),
            pltpu.VMEM((2, HEADS * 128, 128), f32),
            pltpu.VMEM((2, HEADS * 128, 128), f32),
            pltpu.VMEM((2, 8, 16, HEADS * VH), bf16),
            dma((11,)),
            dma((N_SEND,)),
            dma((2,)),
            dma((6,)),
            dma((6,)),
            dma((2, 8)),
            dma((4,)),
            dma((16, 2)),
            dma((16,)),
            dma((2,)),
            dma((2,)),
            dma((2,)),
        ],
        compiler_params=pltpu.CompilerParams(
            collective_id=0, has_side_effects=True, vmem_limit_bytes=56 * 2**20
        ),
    )(
        tokens, w_down_q, w_down_kv.T, q_gain.reshape(-1, 128), kv_gain.reshape(-1, 128),
        w_up_q, w_absorb, w_value, slot_block, table,
    )
    attended = attended.reshape(256, HEADS * VH)
    return pl.pallas_call(
        hand_over,
        out_shape=(
            jax.ShapeDtypeStruct(attended.shape, bf16),
            jax.ShapeDtypeStruct(cache.shape, bf16),
        ),
        in_specs=[hbm, hbm],
        out_specs=(hbm, hbm),
        scratch_shapes=[
            pltpu.VMEM(attended.shape, bf16),
            pltpu.VMEM(cache.shape, bf16),
            dma((2, 5)),
        ],
        compiler_params=pltpu.CompilerParams(vmem_limit_bytes=60 * 2**20),
    )(attended, cache)


def solution(mesh):
    placed = (
        P("chain", "tp"),
        P("tp", None),
        P("tp", None),
        P(),
        P(),
        P(None, "tp"),
        P("tp", None, None),
        P("tp", None, None),
        P("chain"),
    )
    return jax.shard_map(
        per_device,
        mesh=mesh,
        in_specs=placed,
        out_specs=(P("chain", "tp"), P("chain", "tp", None)),
        check_vma=False,
    )
```
